32 devices in a mesh: section: 2 (over core), dp: 4 (over z), expert: 4 (over y, x).
Axes of the slice: x: 2, y: 2, z: 4, core: 2. Of those that a mesh axis runs over, the one named last changes fastest.
Arguments:
- layer_input: bfloat16 [2, 2048, 1536], P(None, ('dp', 'expert')), may hold values from -6 to 6
- output_cotangent: bfloat16 [2, 2048, 1536], P(None, ('dp', 'expert')), may hold values from -6 to 6
- documents: int32 [2, 2048], P(None, 'dp'), may hold values from 0 to 2, as said below
- expert_routes: int32 [2, 2, 2048, 8], P('section', None, ('dp', 'expert')), may hold values from 0 to 11, as said below
- attention_gain: float32 [2, 1536], P('section'), may hold values from 0.5 to 1.5
- query_weight: bfloat16 [2, 1536, 1536], P('section', 'dp'), may hold values from -0.15625 to 0.15625
- key_weight: bfloat16 [2, 1536, 512], P('section', 'dp'), may hold values from -0.15625 to 0.15625
- value_weight: bfloat16 [2, 1536, 512], P('section', 'dp'), may hold values from -0.15625 to 0.15625
- output_weight: bfloat16 [2, 1536, 1536], P('section', 'dp'), may hold values from -1.25 to 1.25
- router_weight: bfloat16 [2, 1536, 12], P('section', 'dp'), may hold values from -0.078125 to 0.078125
- mixture_gain: float32 [2, 1536], P('section'), may hold values from 0.5 to 1.5
- expert_gate: bfloat16 [2, 12, 1536, 512], P('section', 'expert'), may hold values from -0.15625 to 0.15625
- expert_up: bfloat16 [2, 12, 1536, 512], P('section', 'expert'), may hold values from -0.15625 to 0.15625
- expert_down: bfloat16 [2, 12, 512, 1536], P('section', 'expert'), may hold values from -1 to 1
Outputs:
- layer_outputs: bfloat16 [2, 2, 2048, 1536], P('section', None, ('dp', 'expert'))
- input_grads: float32 [2, 2, 2048, 1536], P('section', None, ('dp', 'expert'))
- attention_gain_gradient: float32 [2, 1536], P('section')
- query_weight_gradient: float32 [2, 1536, 1536], P('section', 'dp')
- key_weight_gradient: float32 [2, 1536, 512], P('section', 'dp')
- value_weight_gradient: float32 [2, 1536, 512], P('section', 'dp')
- output_weight_gradient: float32 [2, 1536, 1536], P('section', 'dp')
- router_weight_gradient: float32 [2, 1536, 12], P('section', 'dp')
- mixture_gain_gradient: float32 [2, 1536], P('section')
- expert_gate_gradient: float32 [2, 12, 1536, 512], P('section', 'expert')
- expert_up_gradient: float32 [2, 12, 1536, 512], P('section', 'expert')
- expert_down_gradient: float32 [2, 12, 512, 1536], P('section', 'expert')
The draws below stay inside these ranges and needn't reach their ends.
Inputs may be any that keep to these rules, and one draw needn't show every extreme that they name: `documents`: along each sequence of 512 tokens the numbers never fall, and every sequence holds 0, 1 and 2. `expert_routes`: each token names 8 different experts. In every micro-batch and layer some expert is named by all tokens of a sequence, so one device's 128 rows may all go to one expert.
All inputs are finite; a program needn't handle non-finite values.
Results may differ from the reference program's by a relative error of at most 0.03.
Values may be sent and summed in bfloat16 or wider, within the bound.
A program may use at most 320 MiB of HBM per device.

```python
import jax
import jax.numpy as jnp
from jax import lax

D = 1536
H = 24
KVH = 8
HD = 64
FF = 512
TOPK = 8
MB = 2
TOK_MB = 128
SEQ = 512
TOKENS = 2048
EXPERTS = 12


def draw_documents(key, part):
    key = jax.random.fold_in(key, 11)
    start_key, end_key = jax.random.split(key)
    count_seq = MB * (TOKENS // SEQ)
    starts = jax.random.randint(start_key, (count_seq, 1), 1, TOK_MB // 2 + 1)
    ends = jax.random.randint(end_key, (count_seq, 1), SEQ - TOK_MB // 2, SEQ)
    places = jnp.arange(SEQ, dtype=jnp.int32)[None, :]
    labels = (places >= starts).astype(jnp.int32) + (places >= ends).astype(jnp.int32)
    return labels.reshape(MB, TOKENS)


def draw_expert_routes(key, part):
    key = jax.random.fold_in(key, 23)
    base_key, lean_key, busy_key = jax.random.split(key, 3)
    blocks = SEQ // TOK_MB
    sequences = TOKENS // SEQ
    base = jax.random.randint(base_key, (2, MB, sequences, blocks, TOK_MB, EXPERTS), 0, 64)
    leaning = jax.random.randint(lean_key, (2, MB, sequences, blocks, 1, EXPERTS), 0, 48)
    busiest = jax.random.randint(busy_key, (2, MB, sequences, 1, 1, 1), 0, EXPERTS)
    numbers = jnp.arange(EXPERTS, dtype=jnp.int32)
    scores = base + leaning + 10000 * (numbers == busiest).astype(jnp.int32)
    distinct = scores * EXPERTS + numbers
    ranked = lax.top_k(distinct, TOPK)[1]
    return ranked.astype(jnp.int32).reshape(2, MB, TOKENS, TOPK)


def block_scale(key, extent, cuts, low, largest):
    level = 1.0
    for axis_at, shards_of in cuts:
        draws = jax.random.uniform(jax.random.fold_in(jax.random.fold_in(key, 6), axis_at), (shards_of,), jnp.float32, low / len(cuts), largest / len(cuts))
        level = level * jnp.repeat(jnp.exp(draws), extent[axis_at] // shards_of).reshape((-1,) + (1,) * (len(extent) - 1 - axis_at))
    return level


def centred(own_key, dims, spread, reach, shards=(), held_as=jnp.bfloat16):
    values = spread * jax.random.normal(own_key, dims, jnp.float32)
    if shards:
        values = values * block_scale(own_key, dims, shards, -0.22, 0.18)
    return jnp.clip(values, -reach, reach).astype(held_as)


def setup_inputs(seed: int = 0) -> dict:
    key_list = jax.random.split(jax.random.key(seed), 15)
    layer_input = centred(key_list[0], (MB, TOKENS, D), 1.0, 6.0, ((1, 16),))
    output_cotangent = centred(key_list[1], (MB, TOKENS, D), 1.0, 6.0, ((1, 16),))
    documents = draw_documents(jax.random.fold_in(key_list[14], 71), 0)
    expert_routes = draw_expert_routes(jax.random.fold_in(key_list[14], 71), 0)
    attention_gain = jnp.clip(1.0 + 0.1 * jax.random.normal(key_list[4], (2, D), jnp.float32), 0.5, 1.5)
    query_weight = centred(key_list[5], (2, D, H * HD), D ** -0.5, 0.15625, ((0, 2), (1, 4)))
    key_weight = centred(key_list[6], (2, D, KVH * HD), D ** -0.5, 0.15625, ((0, 2), (1, 4)))
    value_weight = centred(key_list[7], (2, D, KVH * HD), D ** -0.5, 0.15625, ((0, 2), (1, 4)))
    output_weight = centred(key_list[8], (2, H * HD, D), (H * HD // 64) ** -0.5, 1.25, ((0, 2), (1, 4)))
    router_weight = centred(key_list[9], (2, D, EXPERTS), (4 * D) ** -0.5, 0.078125, ((0, 2), (1, 4)))
    mixture_gain = jnp.clip(1.0 + 0.1 * jax.random.normal(key_list[10], (2, D), jnp.float32), 0.5, 1.5)
    expert_gate = centred(key_list[11], (2, EXPERTS, D, FF), D ** -0.5, 0.15625, ((0, 2), (1, 4)))
    expert_up = centred(key_list[12], (2, EXPERTS, D, FF), D ** -0.5, 0.15625, ((0, 2), (1, 4)))
    expert_down = centred(key_list[13], (2, EXPERTS, FF, D), (FF // 16) ** -0.5, 1.0, ((0, 2), (1, 4)))
    return {"layer_input": layer_input, "output_cotangent": output_cotangent, "documents": documents, "expert_routes": expert_routes, "attention_gain": attention_gain, "query_weight": query_weight, "key_weight": key_weight, "value_weight": value_weight, "output_weight": output_weight, "router_weight": router_weight, "mixture_gain": mixture_gain, "expert_gate": expert_gate, "expert_up": expert_up, "expert_down": expert_down}


EPS = 1e-06
THETA = 10000.0
BIG = 1e+30
HIGH = lax.Precision.HIGHEST

@jax.custom_vjp
def low(v):
    return lax.optimization_barrier(v.astype(jnp.bfloat16)).astype(jnp.float32)

@jax.custom_vjp
def low_back(v):
    return v

def low_keep(v):
    return (low(v), None)

def low_pass(kept, grad):
    return (grad,)

def back_keep(v):
    return (v, None)

def back_low(kept, grad):
    return (low(grad),)
low.defvjp(low_keep, low_pass)
low_back.defvjp(back_keep, back_low)

def matmul(left, right):
    return jnp.dot(left, right, precision=HIGH, preferred_element_type=jnp.float32)

def norm_rows(values, gain):
    scale = lax.rsqrt(lax.optimization_barrier(jnp.mean(values * values, axis=-1, keepdims=True)) + EPS)
    return values * scale * gain

def rotate_rows(values, heads):
    half_dim = HD // 2
    places = jnp.arange(SEQ, dtype=jnp.int32).astype(jnp.float32)
    inverse = THETA ** (-jnp.arange(half_dim, dtype=jnp.float32) * 2.0 / HD)
    angles = places[:, None] * inverse[None, :]
    cosine = jnp.cos(angles)[:, None, :]
    sine_table = jnp.sin(angles)[:, None, :]
    shaped = values.reshape(values.shape[0], SEQ, heads, HD)
    leading = shaped[..., :half_dim]
    trailing = shaped[..., half_dim:]
    turned = jnp.concatenate([leading * cosine - trailing * sine_table, trailing * cosine + leading * sine_table], axis=-1)
    return turned.reshape(values.shape[0], SEQ, heads * HD)

def attend(sequence_item):
    queries, keys, values, labels = sequence_item
    grouped = queries.reshape(SEQ, KVH, H // KVH, HD)
    scores = jnp.einsum('tkgd,skd->kgts', grouped, keys.reshape(SEQ, KVH, HD), precision=HIGH) * HD ** (-0.5)
    scores = low_back(scores)
    places = jnp.arange(SEQ, dtype=jnp.int32)
    allowed = (labels[:, None] == labels[None, :]) & (places[None, :] <= places[:, None])
    scores = jnp.where(allowed[None, None], scores, -BIG)
    probabilities = low(jax.nn.softmax(scores, axis=-1))
    mixed = jnp.einsum('kgts,skd->tkgd', probabilities, values.reshape(SEQ, KVH, HD), precision=HIGH)
    return mixed.reshape(SEQ, H * HD)

def one_layer(weights, layer_rows, labels, route):
    gain_one, query_w, key_w, value_w, out_w, router_w, gain_two, gate_stack, up_stack, down_stack = weights
    sequences = TOKENS // SEQ
    normed = low(norm_rows(layer_rows, gain_one))
    queries = low(rotate_rows(low_back(matmul(normed, query_w)).reshape(sequences, SEQ, H * HD), H))
    keys = low(rotate_rows(low_back(matmul(normed, key_w)).reshape(sequences, SEQ, KVH * HD), KVH))
    values = low(low_back(matmul(normed, value_w))).reshape(sequences, SEQ, KVH * HD)
    mixed = lax.map(jax.checkpoint(attend), (queries, keys, values, labels.reshape(sequences, SEQ)))
    mixed = low(low_back(mixed.reshape(TOKENS, H * HD)))
    middle = layer_rows + low_back(matmul(mixed, out_w))
    normed_two = low(norm_rows(middle, gain_two))
    logits = low_back(matmul(normed_two, router_w))
    choose = (route[:, :, None] == jnp.arange(EXPERTS, dtype=jnp.int32)[None, None, :]).astype(jnp.float32)
    chosen = jnp.einsum('tke,te->tk', choose, logits, precision=HIGH)
    gate_values = jax.nn.softmax(chosen, axis=-1)
    columns = jnp.einsum('tk,tke->et', gate_values, choose, precision=HIGH)

    def one_expert(running, expert_item):
        gate_w, up_w, down_w, column = expert_item
        entry = low_back(normed_two)
        gate_val = low_back(matmul(entry, gate_w))
        up_val = low_back(matmul(entry, up_w))
        hidden = low(jax.nn.silu(gate_val) * up_val)
        result = low(low_back(matmul(hidden, down_w)))
        return (running + column[:, None] * result, None)
    mixture, _ = lax.scan(jax.checkpoint(one_expert), jnp.zeros((TOKENS, D), jnp.float32), (gate_stack, up_stack, down_stack, columns))
    return middle + mixture

def forward(layers, inputs, probes, documents, expert_routes):
    firsts = []
    seconds = []
    for moment in range(MB):
        upper = one_layer(layers[0], inputs[moment], documents[moment], expert_routes[0, moment])
        passed = low(low_back(upper)) + probes[moment]
        lower = one_layer(layers[1], passed, documents[moment], expert_routes[1, moment])
        firsts.append(upper)
        seconds.append(lower)
    return (jnp.stack(firsts), jnp.stack(seconds))

def reference(layer_input, output_cotangent, documents, expert_routes, attention_gain, query_weight, key_weight, value_weight, output_weight, router_weight, mixture_gain, expert_gate, expert_up, expert_down):
    weight_list = [attention_gain, query_weight, key_weight, value_weight, output_weight, router_weight, mixture_gain, expert_gate, expert_up, expert_down]
    layers = tuple((tuple((weight.astype(jnp.float32)[index] for weight in weight_list)) for index in range(2)))
    inputs = layer_input.astype(jnp.float32)
    probes = jnp.zeros((MB, TOKENS, D), jnp.float32)

    def whole_run(layers_arg, inputs_arg, probes_arg):
        return forward(layers_arg, inputs_arg, probes_arg, documents, expert_routes)
    (firsts, seconds), pullback = jax.vjp(whole_run, layers, inputs, probes)
    layer_grads, input_grad, probe_grad = pullback((jnp.zeros_like(firsts), output_cotangent.astype(jnp.float32)))
    stacked = [jnp.stack([layer_grads[0][index], layer_grads[1][index]]) for index in range(10)]
    layer_outputs = jnp.stack([firsts, seconds]).astype(jnp.bfloat16)
    input_grads = jnp.stack([input_grad, probe_grad])
    return (layer_outputs, input_grads, stacked[0], stacked[1], stacked[2], stacked[3], stacked[4], stacked[5], stacked[6], stacked[7], stacked[8], stacked[9])
```

```python
import functools

import jax
import jax.numpy as jnp
from jax import lax
from jax.experimental import pallas as pl
from jax.experimental.pallas import tpu as pltpu
from jax.sharding import PartitionSpec as P

H = 24
KVH = 8
HD = 64
GROUP = H // KVH
HALF = HD // 2

EPS = 1e-06
THETA = 10000.0
BIG = 1e30
LANES = 128
LOW = 64
SCALE = HD ** (-0.5)
VMEM = 60 * 1024 * 1024

F32 = jnp.float32
BF16 = jnp.bfloat16


def params(*semantics):
    return pltpu.CompilerParams(vmem_limit_bytes=VMEM, dimension_semantics=semantics or None)


def cost(flops, nbytes):
    return pl.CostEstimate(flops=int(flops), bytes_accessed=int(nbytes), transcendentals=0)


def dot(left, right, contract):
    return lax.dot_general(left, right, (contract, ((), ())), preferred_element_type=F32)


def shape(dims, dtype):
    return jax.ShapeDtypeStruct(dims, dtype)


def whole():
    return pl.BlockSpec(memory_space=pltpu.VMEM)


def shift(block, axis, distance, sections=None):
    count = lax.axis_size(axis)
    if sections is None:
        return lax.ppermute(block, axis, [(i, (i + distance) % count) for i in range(count)])
    route = [
        (section * count + i, section * count + (i + distance) % count)
        for section in sections
        for i in range(count)
    ]
    return lax.ppermute(block, ("section", axis), route)


def from_behind(block, distance):
    devices = range(lax.axis_size("section"))
    route = [(i - distance, i) for i in devices if i - distance in devices]
    return lax.ppermute(block, "section", route)


def spread(block, sections=None, axis="expert"):
    return [block] + [
        shift(block, axis, distance, sections) for distance in range(1, lax.axis_size(axis))
    ]


def partner(me, distance):
    other = me
    bit = 1
    while bit <= distance:
        if distance & bit:
            other = other + bit - 2 * bit * (me // bit % 2)
        bit *= 2
    return other


def plane_peers(blocks):
    me = lax.axis_index("expert")
    here = (lax.axis_index("section"), lax.axis_index("dp"))
    return [here + (partner(me, d),) for d in range(1, blocks)]


def line_peers(members):
    place = lax.axis_index("dp")
    return [
        (lax.axis_index("section"), lax.rem(place + k, members), lax.axis_index("expert"))
        for k in range(1, members)
    ]


def greet(peers):
    barrier = pltpu.get_barrier_semaphore()
    for peer in peers:
        pl.semaphore_signal(barrier, inc=1, device_id=peer, device_id_type=pl.DeviceIdType.MESH)
    pl.semaphore_wait(barrier, len(peers))


def send(source, target, send_sem, recv_sem, peer):
    return pltpu.make_async_remote_copy(
        src_ref=source,
        dst_ref=target,
        send_sem=send_sem,
        recv_sem=recv_sem,
        device_id=peer,
        device_id_type=pl.DeviceIdType.MESH,
    )


def in_section(section):
    return pl.when(lax.axis_index("section") == section)


def in_sections(sections):
    if len(sections) == 1:
        return in_section(sections[0])
    return lambda run: run()


def relay_sems(blocks, members):
    line = (2, members - 1)
    plane = (members - 1, blocks - 2)
    return [pltpu.SemaphoreType.DMA(dims) for dims in (line, line, plane, plane, (1,))]


class Relay:
    def __init__(self, near, dest, sems):
        self.near, self.dest = near, dest
        self.members, self.blocks = dest.shape[:2]
        self.line_send, self.line_recv, self.plane_send, self.plane_recv, self.near_sem = sems

    def line(self, which, k):
        slot = which * (self.blocks - 1)
        return send(
            self.near.at[slot],
            self.dest.at[k, slot],
            self.line_send.at[which, k - 1],
            self.line_recv.at[which, k - 1],
            line_peers(self.members)[k - 1],
        )

    def plane(self, k, d):
        return send(
            self.dest.at[k, 0],
            self.dest.at[k, d],
            self.plane_send.at[k - 1, d - 1],
            self.plane_recv.at[k - 1, d - 1],
            plane_peers(self.blocks)[d - 1],
        )

    def start(self, which):
        for k in range(1, self.members):
            self.line(which, k).start()

    def keep(self):
        return pltpu.make_async_copy(self.near, self.dest.at[0], self.near_sem.at[0])

    def forward(self):
        for k in range(1, self.members):
            self.line(0, k).wait_recv()
            for d in range(1, self.blocks - 1):
                self.plane(k, d).start()

    def finish(self):
        for k in range(1, self.members):
            self.line(1, k).wait_recv()
            for which in range(2):
                self.line(which, k).wait_send()
            for d in range(1, self.blocks - 1):
                self.plane(k, d).wait()
        self.keep().wait()


def gather_kernel(section, chained, *refs):
    q_ref, k_ref, v_ref, o_ref, router_ref = refs[:5]
    refs = refs[9:] if chained else refs[5:]
    inner, out, router, local_sem, line_sem, plane_sem, router_sem, own_sem = refs
    blocks = inner.shape[0]
    depth = q_ref.shape[0]
    members = inner.shape[1] // depth
    me = lax.axis_index("expert")
    place = lax.axis_index("dp")

    def rows(member):
        return pl.ds(pl.multiple_of(member * depth, depth), depth)

    def local(e):
        copies = []
        at = 0
        for source, target, start in (
            (q_ref, inner, 0),
            (k_ref, inner, q_ref.shape[1] // blocks),
            (v_ref, inner, (q_ref.shape[1] + k_ref.shape[1]) // blocks),
            (o_ref, out, 0),
        ):
            part = source.shape[1] // blocks
            copies.append(
                pltpu.make_async_copy(
                    source.at[:, pl.ds(pl.multiple_of(e * part, LANES), part)],
                    target.at[e, rows(place), pl.ds(start, part)],
                    local_sem.at[at],
                )
            )
            at += 1
        return copies

    @in_section(section)
    def _():
        diagonal = partner(me, blocks - 1)
        for copy in local(me):
            copy.start()
        mine = pltpu.make_async_copy(router_ref, router.at[rows(place)], own_sem.at[0])
        mine.start()
        greet(plane_peers(blocks) + line_peers(members))
        for copy in local(me):
            copy.wait()

        def line(which, k):
            target, column = ((inner, me), (out, me), (out, diagonal))[which]
            piece = target.at[column, rows(place)]
            return send(
                piece,
                piece,
                line_sem.at[0, which, k - 1],
                line_sem.at[1, which, k - 1],
                line_peers(members)[k - 1],
            )

        def plane(which, k, d):
            target = (inner, out)[which]
            piece = target.at[me, rows(lax.rem(place + members - k, members))]
            return send(
                piece,
                piece,
                plane_sem.at[0, which, k - 1, d - 1],
                plane_sem.at[1, which, k - 1, d - 1],
                plane_peers(blocks)[d - 1],
            )

        def narrow(k):
            piece = router.at[rows(place)]
            return send(
                piece, piece, router_sem.at[0, k - 1], router_sem.at[1, k - 1], line_peers(members)[k - 1]
            )

        for which in range(2):
            for k in range(1, members):
                line(which, k).start()
        for d in range(1, blocks):
            for copy in local(partner(me, d)):
                copy.start()
            for copy in local(partner(me, d)):
                copy.wait()
        mine.wait()
        for k in range(1, members):
            line(2, k).start()
        for k in range(1, members):
            narrow(k).start()
        reach = (blocks, blocks - 1)
        for which in range(2):
            for k in range(1, members):
                line(which, k).wait_recv()
                for d in range(1, reach[which]):
                    plane(which, k, d).start()
        for k in range(1, members):
            line(2, k).wait_recv()
            narrow(k).wait()
            for which in range(3):
                line(which, k).wait_send()
            for which in range(2):
                for d in range(1, reach[which]):
                    plane(which, k, d).wait()


def gather_weights(section, number, sources, before=None, after=None):
    q, k, v, o, router = sources
    blocks = lax.axis_size("expert")
    members = lax.axis_size("dp")
    depth = q.shape[0] * members
    wide = (q.shape[1] + k.shape[1] + v.shape[1]) // blocks
    shapes = [
        shape((blocks, depth, wide), BF16),
        shape((blocks, depth, o.shape[1] // blocks), BF16),
        shape((depth, LANES), BF16),
    ]
    chained = before is not None
    return pl.pallas_call(
        functools.partial(gather_kernel, section, chained),
        in_specs=[pl.BlockSpec(memory_space=pl.ANY)] * (9 if chained else 5),
        out_specs=[pl.BlockSpec(memory_space=pl.ANY)] * 3,
        out_shape=shapes,
        scratch_shapes=[
            pltpu.SemaphoreType.DMA((4,)),
            pltpu.SemaphoreType.DMA((2, 3, members - 1)),
            pltpu.SemaphoreType.DMA((2, 2, members - 1, blocks - 1)),
            pltpu.SemaphoreType.DMA((2, members - 1)),
            pltpu.SemaphoreType.DMA((1,)),
        ],
        input_output_aliases={5: 0, 6: 1, 7: 2} if chained else {},
        compiler_params=pltpu.CompilerParams(collective_id=number, has_side_effects=True),
        name="gather_weights",
    )(*sources, *((*before, after) if chained else ()))


def group_of(ref, group):
    base = pl.multiple_of(group * GROUP * HD, HD)
    return jnp.concatenate(
        [ref[pl.ds(base + head * HD, HD), :] for head in range(GROUP)], axis=1
    )


def keys_of(ref, which, group):
    base = pl.multiple_of(group * HD, HD)
    return jnp.concatenate(
        [ref[block, which, pl.ds(base, HD), :] for block in range(ref.shape[0])], axis=1
    )


def turn_heads(turned, cosine, sine, target, at, count, sign):
    for head in range(0, count, HD):
        leading = turned[head : head + HALF]
        trailing = turned[head + HALF : head + HD]
        target[at + head : at + head + HALF] = (leading * cosine - trailing * sine * sign).astype(
            BF16
        )
        target[at + head + HALF : at + head + HD] = (
            trailing * cosine + leading * sine * sign
        ).astype(BF16)


def enter(sections, relays, blocks):
    for section in range(lax.axis_size("section")):
        peers = []
        own = [relay for at, relay in relays if at == section]
        if section in sections or own:
            peers = plane_peers(blocks)
        if own:
            peers = peers + line_peers(own[0].members)
        if peers:
            in_section(section)(lambda peers=peers: greet(peers))


def open_relay(relay):
    relay.keep().start()
    relay.start(0)
    relay.start(1)


def forward_kernel(sections, tasks, fresh, reused, groups_of_blocks, *refs):
    sources = [refs[14 + i] for i in range(len(tasks))]
    inputs = refs[:14]
    at = 14 + len(tasks) + reused
    outputs = refs[at : at + 8]
    dests = refs[at + 8 : at + 8 + fresh + reused]
    at = at + 8 + fresh + reused
    scratch = refs[at : at + 23]
    relay_refs = refs[at + 23 :]
    relays = [
        (section, Relay(sources[i], dests[dest], relay_refs[5 * i : 5 * i + 5]))
        for i, (section, dest) in enumerate(tasks)
    ]
    (
    entry_ref,
    gain_one_ref,
    cos_ref,
    sin_ref,
    bias_ref,
    gain_two_ref,
    router_ref,
    chosen_ref,
    pick_ref,
    inner_hbm,
    out_hbm,
    gate_hbm,
    up_hbm,
    down_hbm,
    ) = inputs
    (
    normed_out,
    q_out,
    kv_out,
    att_out,
    lse_out,
    middle_out,
    payload_out,
    output_out,
    ) = outputs
    (
    inner,
    out,
    gates_w,
    ups_w,
    downs_w,
    normed,
    query,
    kv,
    att,
    lse,
    middle,
    payload,
    sent,
    back,
    own,
    result,
    inner_sem,
    out_sem,
    expert_sem,
    kv_sem,
    payload_sem,
    back_sem,
    save_sem,
    ) = scratch
    blocks = kv.shape[0]
    rows, width = entry_ref.shape
    local, _, hidden_width = gates_w.shape
    queries = query.shape[0] // blocks
    keys = kv.shape[2] // blocks
    part = width // blocks

    enter(sections, relays, blocks)
    for section, relay in relays:
        in_section(section)(lambda relay=relay: open_relay(relay))

    @in_sections(sections)
    def _():
        peers = plane_peers(blocks)
        inner_copies = [
            pltpu.make_async_copy(inner_hbm.at[e], inner.at[e], inner_sem.at[e])
            for e in range(blocks)
        ]
        out_copy = pltpu.make_async_copy(out_hbm, out, out_sem)
        expert_copies = []
        for e in range(local):
            band = pl.ds(e * hidden_width, hidden_width)
            expert_copies.append(
                (
                    pltpu.make_async_copy(gate_hbm.at[e], gates_w.at[e], expert_sem.at[e, 0]),
                    pltpu.make_async_copy(up_hbm.at[e], ups_w.at[e], expert_sem.at[e, 1]),
                    pltpu.make_async_copy(down_hbm.at[e], downs_w.at[band], expert_sem.at[e, 2]),
                )
            )
        for copy in inner_copies:
            copy.start()
        out_copy.start()
        for copies in expert_copies:
            for copy in copies:
                copy.start()

        saves = []

        def save(source, target):
            copy = pltpu.make_async_copy(source, target, save_sem.at[len(saves)])
            copy.start()
            saves.append(copy)

        values = entry_ref[...].astype(F32)
        scale = lax.rsqrt(jnp.mean(values * values, axis=-1, keepdims=True) + EPS)
        normed[...] = (values * scale * gain_one_ref[...]).astype(BF16)
        save(normed, normed_out)
        cosine = cos_ref[...]
        sine = sin_ref[...]
        for e in range(blocks):
            inner_copies[e].wait()
            turned = dot(normed[...], inner[e, :, queries:], ((1,), (0,))).T
            turn_heads(turned[:keys], cosine, sine, kv.at[0, 0], e * keys, keys, 1.0)
            kv[0, 1, e * keys : (e + 1) * keys] = turned[keys:].astype(BF16)
        kv_copies = [
            send(kv.at[0], kv.at[d], kv_sem.at[0, d - 1], kv_sem.at[1, d - 1], peers[d - 1])
            for d in range(1, blocks)
        ]
        for copy in kv_copies:
            copy.start()
        for e in range(blocks):
            turned = dot(normed[...], inner[e, :, :queries], ((1,), (0,))).T
            turn_heads(turned, cosine, sine, query, e * queries, queries, 1.0)
        save(query, q_out)
        bias = jnp.concatenate([bias_ref[...]] * GROUP, axis=1)
        for copy in kv_copies:
            copy.wait()
        save(kv, kv_out)

        def one(group, carry):
            query_group = group_of(query, group)
            scores = dot(keys_of(kv, 0, group), query_group, ((0,), (0,))) * SCALE + bias
            highest = jnp.max(scores, axis=0, keepdims=True)
            powers = jnp.exp(scores - highest)
            totals = jnp.sum(powers, axis=0, keepdims=True)
            lse[group] = highest + jnp.log(totals)
            probabilities = (powers * (1.0 / totals)).astype(BF16)
            mixed = dot(keys_of(kv, 1, group), probabilities, ((1,), (0,))).astype(BF16)
            for head in range(GROUP):
                base = pl.multiple_of(group * GROUP * HD + head * HD, HD)
                att[pl.ds(base, HD), :] = mixed[:, head * rows : (head + 1) * rows]
            return carry

        lax.fori_loop(0, kv.shape[2] // HD, one, 0)
        for section, relay in relays:
            if section in sections:
                in_section(section)(relay.forward)
        save(att, att_out)
        save(lse, lse_out)
        attended = att[...].T
        out_copy.wait()
        for e in range(blocks):
            columns = slice(e * part, (e + 1) * part)
            middle[:, columns] = entry_ref[:, columns].astype(F32) + dot(
                attended, out[e], ((1,), (0,))
            )
        save(middle, middle_out)
        held = middle[...]
        scale = lax.rsqrt(jnp.mean(held * held, axis=-1, keepdims=True) + EPS)
        normed_two = (held * scale * gain_two_ref[...]).astype(BF16)
        payload[0, :, :width] = normed_two
        logits = dot(normed_two, router_ref[...], ((1,), (0,))) + chosen_ref[...]
        highest = jnp.max(logits, axis=-1, keepdims=True)
        powers = jnp.exp(logits - highest)
        shares = powers / jnp.sum(powers, axis=-1, keepdims=True)
        high = shares.astype(BF16).astype(F32)
        payload[0, :, width:] = (high + pltpu.roll(shares - high, LOW, 1)).astype(BF16)
        payload_copies = [
            send(
                payload.at[0],
                payload.at[d],
                payload_sem.at[0, d - 1],
                payload_sem.at[1, d - 1],
                peers[d - 1],
            )
            for d in range(1, blocks)
        ]
        for copy in payload_copies:
            copy.start()
        back_copies = [
            send(sent.at[d - 1], back.at[d - 1], back_sem.at[0, d - 1], back_sem.at[1, d - 1], peers[d - 1])
            for d in range(1, blocks)
        ]
        for at, members in enumerate(groups_of_blocks):
            for d in members:
                if d:
                    payload_copies[d - 1].wait_recv()
            stacked = jnp.concatenate([payload[d] for d in members], axis=0)
            lanes = stacked[:, width:].astype(F32)
            pieces = []
            for e in range(local):
                if at == 0:
                    for copy in expert_copies[e]:
                        copy.wait()
                gate = dot(stacked[:, :width], gates_w[e], ((1,), (0,)))
                up = dot(stacked[:, :width], ups_w[e], ((1,), (0,)))
                share = jnp.sum(lanes * pick_ref[e], axis=-1, keepdims=True)
                pieces.append((gate / (1.0 + jnp.exp(-gate)) * up * share).astype(BF16))
            total = dot(jnp.concatenate(pieces, axis=1), downs_w[...], ((1,), (0,)))
            for place, d in enumerate(members):
                piece = total[place * rows : (place + 1) * rows]
                if d:
                    sent[d - 1] = piece.astype(BF16)
                    back_copies[d - 1].start()
                else:
                    own[...] = middle[...] + piece
        save(payload, payload_out)
        total = own[...]
        for d in range(1, blocks):
            back_copies[d - 1].wait_recv()
            total = total + back[d - 1].astype(F32)
        result[...] = total.astype(BF16)
        save(result, output_out)
        for d in range(1, blocks):
            payload_copies[d - 1].wait_send()
            back_copies[d - 1].wait_send()
        for copy in saves:
            copy.wait()

    for section, relay in relays:
        if section not in sections:
            in_section(section)(relay.forward)
        in_section(section)(relay.finish)


def forward_layer(
    sections,
    number,
    entry,
    gain_one,
    cosine,
    sine,
    bias,
    gain_two,
    router,
    chosen,
    pick,
    weights,
    tasks=(),
    fresh=0,
    reused=(),
):
    inner, out, gate_all, up_all, down_all = weights
    rows, width = entry.shape
    blocks = inner.shape[0]
    members = lax.axis_size("dp")
    local, _, hidden = gate_all.shape
    keys = KVH * HD
    flops = 2 * rows * width * (H + 2 * KVH) * HD + 4 * rows * rows * blocks * H * HD
    flops += 2 * rows * H * HD * width + 6 * rows * blocks * local * width * hidden
    groups_of_blocks = [[0], list(range(1, blocks - 1)), [blocks - 1]]
    pair = (2, blocks - 1)
    anywhere = pl.BlockSpec(memory_space=pl.ANY)
    first_reused = 14 + len(tasks)
    results = pl.pallas_call(
        functools.partial(
            forward_kernel,
            sections,
            [(section, dest) for section, _, dest in tasks],
            fresh,
            len(reused),
            groups_of_blocks,
        ),
        in_specs=[whole()] * 9 + [anywhere] * (5 + len(tasks) + len(reused)),
        out_specs=[anywhere] * (8 + len(reused) + fresh),
        out_shape=[
            shape((rows, width), BF16),
            shape((H * HD, rows), BF16),
            shape((blocks, 2, keys, rows), BF16),
            shape((H * HD, rows), BF16),
            shape((KVH, 1, GROUP * rows), F32),
            shape((rows, width), F32),
            shape((blocks, rows, width + LANES), BF16),
            shape((rows, width), BF16),
        ]
        + [shape((members, blocks, rows, width + LANES), BF16)] * (len(reused) + fresh),
        scratch_shapes=[
            pltpu.VMEM(inner.shape, BF16),
            pltpu.VMEM(out.shape, BF16),
            pltpu.VMEM(gate_all.shape, BF16),
            pltpu.VMEM(up_all.shape, BF16),
            pltpu.VMEM((local * hidden, width), BF16),
            pltpu.VMEM((rows, width), BF16),
            pltpu.VMEM((H * HD, rows), BF16),
            pltpu.VMEM((blocks, 2, keys, rows), BF16),
            pltpu.VMEM((H * HD, rows), BF16),
            pltpu.VMEM((KVH, 1, GROUP * rows), F32),
            pltpu.VMEM((rows, width), F32),
            pltpu.VMEM((blocks, rows, width + LANES), BF16),
            pltpu.VMEM((blocks - 1, rows, width), BF16),
            pltpu.VMEM((blocks - 1, rows, width), BF16),
            pltpu.VMEM((rows, width), F32),
            pltpu.VMEM((rows, width), BF16),
            pltpu.SemaphoreType.DMA((blocks,)),
            pltpu.SemaphoreType.DMA(()),
            pltpu.SemaphoreType.DMA((local, 3)),
            pltpu.SemaphoreType.DMA(pair),
            pltpu.SemaphoreType.DMA(pair),
            pltpu.SemaphoreType.DMA(pair),
            pltpu.SemaphoreType.DMA((8,)),
        ]
        + relay_sems(blocks, members) * len(tasks),
        input_output_aliases={first_reused + i: 8 + i for i in range(len(reused))},
        compiler_params=pltpu.CompilerParams(
            vmem_limit_bytes=VMEM, collective_id=number, has_side_effects=True
        ),
        cost_estimate=cost(flops, 3e7),
        name="forward_layer",
    )(
        entry,
        gain_one,
        cosine,
        sine,
        bias,
        gain_two,
        router,
        chosen,
        pick,
        inner,
        out,
        gate_all,
        up_all,
        down_all,
        *[payloads for _, payloads, _ in tasks],
        *reused,
    )
    return results[:8], results[8:]


def activation(gate, up, hidden_grad):
    sigmoid = 1.0 / (1.0 + jnp.exp(-gate))
    silu = gate * sigmoid
    slope = sigmoid * (1.0 + gate * (1.0 - sigmoid))
    return silu * up, hidden_grad * up * slope, hidden_grad * silu


def norm_back(values, gain, grad):
    width = values.shape[1]
    scale = lax.rsqrt(jnp.mean(values * values, axis=-1, keepdims=True) + EPS)
    scaled = grad * gain
    inner = jnp.sum(values * scaled, axis=-1, keepdims=True) * (1.0 / width)
    part = scale * scaled - values * (scale * scale * scale * inner)
    return part, jnp.sum(grad * values * scale, axis=0, keepdims=True)


HELD = 7


def backward_kernel(sections, holders, tasks, grad_dests, fresh, reused, groups_of_blocks, *refs):
    refs = list(refs)

    def take(count):
        taken = refs[:count]
        del refs[:count]
        return taken

    g_ref, gain_one_ref, gain_two_ref, router_ref, cos_ref, sin_ref, pick_ref, mark_ref = take(8)
    inner_hbm, out_hbm, gate_hbm, up_hbm, down_hbm = take(5)
    sets = [take(HELD) for _ in holders]
    sources = take(len(tasks))
    take(reused)
    outputs = take(7)
    dests = take(fresh + reused)
    gates_w, ups_w, downs_w, out, inner = take(5)
    held = take(HELD)
    entry, bias_v, query, kv, lse, middle, payload = held
    grads, gate_v, up_v, own, sent, back = take(6)
    branch, logit, middle_grad, datt = take(4)
    own_kv, sent_kv, back_kv, turned, entry_grad, entry_low, gain_one_v, gain_two_v = take(8)
    expert_sem, out_sem, inner_sem, held_sem, grads_sem, back_sem, kv_sem, save_sem = take(8)
    relays = [
        (section, Relay(sources[i], dests[dest], take(5))) for i, (section, dest) in enumerate(tasks)
    ]
    grad_relays = [(section, Relay(grads, dests[dest], take(5))) for section, dest in grad_dests]

    blocks, rows, width = grads.shape
    local, _, hidden_width = gates_w.shape
    keys = kv.shape[2]
    part = width // blocks
    queries = H * HD // blocks
    own_keys = keys // blocks

    enter(sections, relays + grad_relays, blocks)
    for section, relay in relays:
        in_section(section)(lambda relay=relay: open_relay(relay))

    @in_sections(sections)
    def _():
        peers = plane_peers(blocks)
        expert_copies = []
        for e in range(local):
            band = pl.ds(e * hidden_width, hidden_width)
            expert_copies.append(
                (
                    pltpu.make_async_copy(gate_hbm.at[e], gates_w.at[e], expert_sem.at[e, 0]),
                    pltpu.make_async_copy(up_hbm.at[e], ups_w.at[e], expert_sem.at[e, 1]),
                    pltpu.make_async_copy(down_hbm.at[e], downs_w.at[band], expert_sem.at[e, 2]),
                )
            )
        out_copy = pltpu.make_async_copy(out_hbm, out, out_sem)
        inner_copy = pltpu.make_async_copy(inner_hbm, inner, inner_sem)
        grads[0] = g_ref[...]
        grads_copies = [
            send(
                grads.at[0],
                grads.at[d],
                grads_sem.at[0, d - 1],
                grads_sem.at[1, d - 1],
                peers[d - 1],
            )
            for d in range(1, blocks)
        ]
        for copy in grads_copies:
            copy.start()

        def fetch(at, index):
            return pltpu.make_async_copy(sets[at][index], held[index], held_sem.at[index])

        order = (HELD - 1,) + tuple(range(HELD - 1))
        for at, section in enumerate(holders):

            @in_section(section)
            def _(at=at):
                fetch(at, HELD - 1).start()

        for copy in expert_copies[0]:
            copy.start()
        for at, section in enumerate(holders):

            @in_section(section)
            def _(at=at):
                for index in order[1:]:
                    fetch(at, index).start()

        for copies in expert_copies[1:]:
            for copy in copies:
                copy.start()
        out_copy.start()
        inner_copy.start()
        for section, relay in grad_relays:
            in_section(section)(lambda relay=relay: relay.start(0))

        saves = []

        def save(source, target):
            copy = pltpu.make_async_copy(source, target, save_sem.at[len(saves)])
            copy.start()
            saves.append(copy)

        fetch(0, HELD - 1).wait()
        stacked = payload[...].reshape(blocks * rows, width + LANES)
        for e in range(local):
            for copy in expert_copies[e]:
                copy.wait()
            gate_v[e] = dot(stacked[:, :width], gates_w[e], ((1,), (0,)))
            up_v[e] = dot(stacked[:, :width], ups_w[e], ((1,), (0,)))
        back_copies = [
            send(
                sent.at[d - 1],
                back.at[d - 1],
                back_sem.at[0, d - 1],
                back_sem.at[1, d - 1],
                peers[d - 1],
            )
            for d in range(1, blocks)
        ]
        for members in groups_of_blocks:
            for d in members:
                if d:
                    grads_copies[d - 1].wait_recv()
            if blocks - 1 in members:
                for section, relay in grad_relays:

                    @in_section(section)
                    def _(relay=relay):
                        relay.start(1)
                        relay.keep().start()

            held_rows = slice(members[0] * rows, (members[-1] + 1) * rows)
            grad = jnp.concatenate([grads[d] for d in members], axis=0)
            lanes = jnp.concatenate([payload[d, :, width:] for d in members], axis=0).astype(F32)
            hidden_grad = dot(grad, downs_w[...], ((1,), (1,)))
            total = jnp.zeros((rows * len(members), width), F32)
            share = jnp.zeros((rows * len(members), LANES), F32)
            for e in range(local):
                columns = slice(e * hidden_width, (e + 1) * hidden_width)
                raw = hidden_grad[:, columns]
                hidden, gate_part, up_part = activation(gate_v[e, held_rows], up_v[e, held_rows], raw)
                hidden = hidden.astype(BF16).astype(F32)
                share = share + jnp.sum(hidden * raw, axis=-1, keepdims=True) * mark_ref[e]
                weight = jnp.sum(lanes * pick_ref[e], axis=-1, keepdims=True)
                total = total + dot((gate_part * weight).astype(BF16), gates_w[e], ((1,), (1,)))
                total = total + dot((up_part * weight).astype(BF16), ups_w[e], ((1,), (1,)))
            high = share.astype(BF16).astype(F32)
            both = high + pltpu.roll(share - high, LOW, 1)
            for place, d in enumerate(members):
                band = slice(place * rows, (place + 1) * rows)
                if d:
                    sent[d - 1, :, :width] = total[band].astype(BF16)
                    sent[d - 1, :, width:] = both[band].astype(BF16)
                    back_copies[d - 1].start()
                else:
                    own[:, :width] = total[band]
                    own[:, width:] = share[band]
        for at, section in enumerate(holders):
            if at == 0:
                for index in order[1:]:
                    fetch(0, index).wait()
        for section, relay in grad_relays + [item for item in relays if item[0] in sections]:
            in_section(section)(relay.forward)

        total = own[:, :width]
        share = own[:, width:]
        for d in range(1, blocks):
            back_copies[d - 1].wait_recv()
            total = total + back[d - 1, :, :width].astype(F32)
            share = share + back[d - 1, :, width:].astype(F32)
        first = lax.broadcasted_iota(jnp.int32, (1, LANES), 1) < LOW
        shares = payload[0, :, width:].astype(F32)
        shares = jnp.where(first, shares + pltpu.roll(shares, LOW, 1), 0.0)
        share = jnp.where(first, share + pltpu.roll(share, LOW, 1), 0.0)
        weighted = shares * share
        logit_grad = (weighted - shares * jnp.sum(weighted, axis=-1, keepdims=True)).astype(BF16)
        logit[...] = logit_grad
        total = total + dot(logit_grad, router_ref[...], ((1,), (1,)))
        piece, gain_two_v[...] = norm_back(middle[...], gain_two_ref[...], total)
        middle_grad[...] = g_ref[...].astype(F32) + piece
        branch[...] = middle_grad[...].astype(BF16)
        save(logit, outputs[4])
        save(branch, outputs[3])
        save(gain_two_v, outputs[6])
        out_copy.wait()
        total = jnp.zeros(datt.shape, F32)
        for e in range(blocks):
            total = total + dot(out[e], branch[:, e * part : (e + 1) * part], ((1,), (1,)))
        datt[...] = total.astype(BF16)

        bias = jnp.concatenate([bias_v[...]] * GROUP, axis=1)
        cosine = cos_ref[...]
        sine = sin_ref[...]
        per_block = queries // (GROUP * HD)

        def one(group, carry):
            query_group = group_of(query, group)
            key_group = keys_of(kv, 0, group)
            grad_group = group_of(datt, group)
            scores = dot(key_group, query_group, ((0,), (0,))) * SCALE + bias
            probabilities = jnp.exp(scores - lse[group])
            probability_grad = dot(keys_of(kv, 1, group), grad_group, ((0,), (0,)))
            centre = jnp.sum(probabilities * probability_grad, axis=0, keepdims=True)
            score_grad = (probabilities * (probability_grad - centre)).astype(BF16)
            query_part = dot(key_group, score_grad, ((1,), (0,))) * SCALE
            e = lax.div(group, per_block)
            base = lax.rem(group, per_block) * (GROUP * HD)
            for head in range(GROUP):
                start = pl.multiple_of(base + head * HD, HALF)
                leading = query_part[:HALF, head * rows : (head + 1) * rows]
                trailing = query_part[HALF:, head * rows : (head + 1) * rows]
                turned[e, pl.ds(start, HALF), :] = (leading * cosine + trailing * sine).astype(BF16)
                turned[e, pl.ds(start + HALF, HALF), :] = (
                    trailing * cosine - leading * sine
                ).astype(BF16)
            key_part = dot(query_group, score_grad, ((1,), (1,))) * SCALE
            value_part = dot(grad_group, probabilities.astype(BF16), ((1,), (1,)))
            base = pl.multiple_of(group * HD, HD)
            for which, piece in ((0, key_part), (1, value_part)):
                own_kv[which, pl.ds(base, HD), :] = piece[:, :rows]
                for d in range(1, blocks):
                    sent_kv[d - 1, which, pl.ds(base, HD), :] = piece[
                        :, d * rows : (d + 1) * rows
                    ].astype(BF16)
            return carry

        heads = keys // HD
        kv_copies = []
        for half in range(2):
            lax.fori_loop(half * heads // 2, (half + 1) * heads // 2, one, 0)
            band = pl.ds(half * keys // 2, keys // 2)
            for d in range(1, blocks):
                copy = send(
                    sent_kv.at[d - 1, :, band],
                    back_kv.at[d - 1, :, band],
                    kv_sem.at[0, half, d - 1],
                    kv_sem.at[1, half, d - 1],
                    peers[d - 1],
                )
                copy.start()
                kv_copies.append(copy)

        inner_copy.wait()
        total = jnp.zeros((rows, width), F32)
        for e in range(blocks):
            total = total + dot(turned[e, :queries], inner[e, :, :queries], ((0,), (1,)))
        for copy in kv_copies:
            copy.wait_recv()
        pair = own_kv[...]
        for d in range(1, blocks):
            pair = pair + back_kv[d - 1].astype(F32)
        for e in range(blocks):
            band = slice(e * own_keys, (e + 1) * own_keys)
            turn_heads(pair[0, band], cosine, sine, turned.at[e], queries, own_keys, -1.0)
            turned[e, queries + own_keys :] = pair[1, band].astype(BF16)
        save(turned, outputs[2])
        for e in range(blocks):
            total = total + dot(turned[e, queries:], inner[e, :, queries:], ((0,), (1,)))
        piece, gain_one_v[...] = norm_back(entry[...].astype(F32), gain_one_ref[...], total)
        result = middle_grad[...] + piece
        entry_grad[...] = result
        entry_low[...] = result.astype(BF16)
        save(entry_low, outputs[1])
        save(entry_grad, outputs[0])
        save(gain_one_v, outputs[5])
        for d in range(1, blocks):
            grads_copies[d - 1].wait_send()
            back_copies[d - 1].wait_send()
        for copy in kv_copies:
            copy.wait_send()
        for copy in saves:
            copy.wait()

    for section, relay in relays:
        if section not in sections:
            in_section(section)(relay.forward)
    for section, relay in relays + grad_relays:
        in_section(section)(relay.finish)


def backward_layer(
    sections,
    number,
    grad,
    sets,
    gain_one,
    gain_two,
    router,
    cosine,
    sine,
    pick,
    mark,
    weights,
    tasks=(),
    grad_dests=(),
    fresh=(),
    reused=(),
):
    inner, out, gate_all, up_all, down_all = weights
    rows, width = grad.shape
    blocks = inner.shape[0]
    members = lax.axis_size("dp")
    local, _, hidden = gate_all.shape
    keys = KVH * HD
    length = rows * blocks
    flops = 4 * rows * width * (H + 2 * KVH) * HD + 10 * rows * length * H * HD
    flops += 2 * rows * H * HD * width + 10 * length * local * width * hidden
    groups_of_blocks = [[0], list(range(1, blocks - 1)), [blocks - 1]]
    pair = (2, blocks - 1)
    anywhere = pl.BlockSpec(memory_space=pl.ANY)
    first_reused = 13 + HELD * len(sets) + len(tasks)
    held = sets[0][1]
    results = pl.pallas_call(
        functools.partial(
            backward_kernel,
            sections,
            [section for section, _ in sets],
            [(section, dest) for section, _, dest in tasks],
            grad_dests,
            len(fresh),
            len(reused),
            groups_of_blocks,
        ),
        in_specs=[whole()] * 8
        + [anywhere] * (5 + HELD * len(sets) + len(tasks) + len(reused)),
        out_specs=[anywhere] * (7 + len(reused) + len(fresh)),
        out_shape=[
            shape((rows, width), F32),
            shape((rows, width), BF16),
            shape((blocks, inner.shape[2], rows), BF16),
            shape((rows, width), BF16),
            shape((rows, LANES), BF16),
            shape((1, width), F32),
            shape((1, width), F32),
        ]
        + [shape(dest.shape, BF16) for dest in reused]
        + [shape((members, blocks, rows, columns), BF16) for columns in fresh],
        scratch_shapes=[
            pltpu.VMEM(gate_all.shape, BF16),
            pltpu.VMEM(up_all.shape, BF16),
            pltpu.VMEM((local * hidden, width), BF16),
            pltpu.VMEM(out.shape, BF16),
            pltpu.VMEM(inner.shape, BF16),
        ]
        + [pltpu.VMEM(array.shape, array.dtype) for array in held]
        + [
            pltpu.VMEM((blocks, rows, width), BF16),
            pltpu.VMEM((local, length, hidden), F32),
            pltpu.VMEM((local, length, hidden), F32),
            pltpu.VMEM((rows, width + LANES), F32),
            pltpu.VMEM((blocks - 1, rows, width + LANES), BF16),
            pltpu.VMEM((blocks - 1, rows, width + LANES), BF16),
            pltpu.VMEM((rows, width), BF16),
            pltpu.VMEM((rows, LANES), BF16),
            pltpu.VMEM((rows, width), F32),
            pltpu.VMEM((H * HD, rows), BF16),
            pltpu.VMEM((2, keys, rows), F32),
            pltpu.VMEM((blocks - 1, 2, keys, rows), BF16),
            pltpu.VMEM((blocks - 1, 2, keys, rows), BF16),
            pltpu.VMEM((blocks, inner.shape[2], rows), BF16),
            pltpu.VMEM((rows, width), F32),
            pltpu.VMEM((rows, width), BF16),
            pltpu.VMEM((1, width), F32),
            pltpu.VMEM((1, width), F32),
            pltpu.SemaphoreType.DMA((local, 3)),
            pltpu.SemaphoreType.DMA(()),
            pltpu.SemaphoreType.DMA(()),
            pltpu.SemaphoreType.DMA((HELD,)),
            pltpu.SemaphoreType.DMA(pair),
            pltpu.SemaphoreType.DMA(pair),
            pltpu.SemaphoreType.DMA((2, 2, blocks - 1)),
            pltpu.SemaphoreType.DMA((7,)),
        ]
        + relay_sems(blocks, members) * (len(tasks) + len(grad_dests)),
        input_output_aliases={first_reused + i: 7 + i for i in range(len(reused))},
        compiler_params=pltpu.CompilerParams(
            vmem_limit_bytes=VMEM, collective_id=number, has_side_effects=True
        ),
        cost_estimate=cost(flops, 4e7),
        name="backward_layer",
    )(
        grad,
        gain_one,
        gain_two,
        router,
        cosine,
        sine,
        pick,
        mark,
        inner,
        out,
        gate_all,
        up_all,
        down_all,
        *[array for _, arrays in sets for array in arrays],
        *[payloads for _, payloads, _ in tasks],
        *reused,
    )
    return results[:7], results[7:]


def expert_weights_kernel(batches, *refs):
    token_refs = refs[:batches]
    grad_refs = refs[batches : 2 * batches]
    pick_ref, gate_ref, up_ref, down_ref, dgate_ref, dup_ref, ddown_ref = refs[2 * batches :]
    tile = pl.program_id(1)
    tiles = pl.num_programs(1) // batches
    width = grad_refs[0].shape[1]

    @pl.when(tile == 0)
    def _():
        for out in (dgate_ref, dup_ref, ddown_ref):
            out[...] = jnp.zeros_like(out)

    for batch in range(batches):

        @pl.when(tile // tiles == batch)
        def _(x_ref=token_refs[batch], g_ref=grad_refs[batch]):
            entry = x_ref[:, :width]
            grad = g_ref[...]
            weight = jnp.sum(x_ref[:, width:].astype(F32) * pick_ref[0], axis=-1, keepdims=True)
            gate = dot(entry, gate_ref[0], ((1,), (0,)))
            up = dot(entry, up_ref[0], ((1,), (0,)))
            hidden_grad = dot(grad, down_ref[0], ((1,), (1,)))
            hidden, gate_part, up_part = activation(gate, up, hidden_grad * weight)
            dgate_ref[0] += dot(entry, gate_part.astype(BF16), ((0,), (0,)))
            dup_ref[0] += dot(entry, up_part.astype(BF16), ((0,), (0,)))
            ddown_ref[0] += dot((hidden * weight).astype(BF16), grad, ((0,), (0,)))


def expert_weights(tokens, grads, pick, gate_all, up_all, down_all, tile=512):
    local, width, hidden = gate_all.shape
    batches = len(tokens)
    total = tokens[0].shape[0]
    tile = min(tile, total)
    tiles = total // tile
    columns = pl.BlockSpec((1, width, hidden), lambda e, t: (e, 0, 0))
    bands = pl.BlockSpec((1, hidden, width), lambda e, t: (e, 0, 0))

    def rows(batch, lanes):
        return pl.BlockSpec(
            (tile, lanes), lambda e, t: (jnp.clip(t - batch * tiles, 0, tiles - 1), 0)
        )

    return pl.pallas_call(
        functools.partial(expert_weights_kernel, batches),
        grid=(local, batches * tiles),
        in_specs=[rows(batch, width + LANES) for batch in range(batches)]
        + [rows(batch, width) for batch in range(batches)]
        + [pl.BlockSpec((1, 1, LANES), lambda e, t: (e, 0, 0)), columns, columns, bands],
        out_specs=[columns, columns, bands],
        out_shape=[
            shape((local, width, hidden), F32),
            shape((local, width, hidden), F32),
            shape((local, hidden, width), F32),
        ],
        compiler_params=params("arbitrary", "arbitrary"),
        cost_estimate=cost(
            2 * total * batches * local * 6 * width * hidden,
            local * 3 * width * hidden * 6 + total * batches * local * width * 4,
        ),
        name="expert_weights",
    )(*tokens, *grads, pick, gate_all, up_all, down_all)


def pad_lanes(block):
    return jnp.pad(block, ((0, 0), (0, LANES - block.shape[1])))


def scatter_sum(blocks_of, axis):
    count = lax.axis_size(axis)
    me = lax.axis_index(axis)
    total = blocks_of(me).astype(F32)
    for distance in range(1, count):
        total = total + shift(blocks_of((me + distance) % count), axis, distance).astype(F32)
    return total


def body(
    layer_input,
    output_cotangent,
    documents,
    expert_routes,
    attention_gain,
    query_weight,
    key_weight,
    value_weight,
    output_weight,
    router_weight,
    mixture_gain,
    expert_gate,
    expert_up,
    expert_down,
):
    batches, rows, width = layer_input.shape
    groups = lax.axis_size("expert")
    members = lax.axis_size("dp")
    local = expert_gate.shape[1]
    experts_all = local * groups
    me = lax.axis_index("expert")
    first = lax.axis_index("section") == 0

    def choose(upper, lower):
        return jax.tree.map(lambda a, b: jnp.where(first, a, b), upper, lower)

    places = (me * rows + jnp.arange(rows, dtype=jnp.int32)).astype(F32)
    inverse = THETA ** (-jnp.arange(HALF, dtype=F32) * 2.0 / HD)
    angles = inverse[:, None] * places[None, :]
    cosine = jnp.cos(angles)
    sine = jnp.sin(angles)
    number = me * local + jnp.arange(local, dtype=jnp.int32)
    lanes = jnp.arange(LANES, dtype=jnp.int32)
    mark = (lanes[None, :] == number[:, None]).astype(F32)[:, None, :]
    pick = mark + (lanes[None, :] == number[:, None] + LOW).astype(F32)[:, None, :]

    def bias_of(batch):
        labels = documents[batch]
        own = lax.dynamic_slice_in_dim(labels, me * rows, rows)
        pieces = []
        for distance in range(groups):
            source = me ^ distance
            theirs = lax.dynamic_slice_in_dim(labels, source * rows, rows)
            order = source * rows + jnp.arange(rows, dtype=jnp.int32)
            allowed = (theirs[:, None] == own[None, :]) & (
                order[:, None] <= (me * rows + jnp.arange(rows, dtype=jnp.int32))[None, :]
            )
            pieces.append(jnp.where(allowed, 0.0, -BIG))
        return jnp.concatenate(pieces, axis=0)

    def chosen_of(batch):
        named = (expert_routes[0, batch][:, :, None] == lanes[None, None, :]).any(axis=1)
        return jnp.where(named, 0.0, -BIG)

    biases = [bias_of(batch) for batch in range(batches)]
    chosens = [chosen_of(batch) for batch in range(batches)]

    sources = (
        query_weight[0],
        key_weight[0],
        value_weight[0],
        output_weight[0],
        pad_lanes(router_weight[0]),
    )
    gathered = gather_weights(0, 0, sources)
    done = from_behind(gathered[2][:8], 1)
    inner, out, router = gather_weights(1, 1, sources, gathered, done)
    gain_one = attention_gain
    gain_two = mixture_gain
    gate_all, up_all, down_all = (expert_gate[0], expert_up[0], expert_down[0])
    weights = (inner, out, gate_all, up_all, down_all)

    def active(moment):
        return [s for s in range(2) if 0 <= moment - s < batches]

    payload_all = [None] * batches
    grads_all = [None] * batches
    stored = []
    produced = []
    inbound = jnp.zeros((rows, width), BF16)

    def plan_tasks(moment):
        tasks, reused, fresh = [], [], []
        for section in active(moment - 1):
            batch = moment - 1 - section
            (fresh if payload_all[batch] is None else reused).append((section, batch))
        for at, (section, batch) in enumerate(reused + fresh):
            tasks.append((section, stored[moment - 1]["payloads"], at))
        return tasks, [batch for _, batch in reused], [batch for _, batch in fresh]

    for moment in range(batches + 1):
        sections = active(moment)
        early = min(moment, batches - 1)
        late = max(moment - 1, 0)
        if sections == [0]:
            entry, bias, chosen = layer_input[early], biases[early], chosens[early]
        elif sections == [1]:
            entry, bias, chosen = inbound, biases[late], chosens[late]
        else:
            entry, bias, chosen = choose(
                (layer_input[early], biases[early], chosens[early]),
                (inbound, biases[late], chosens[late]),
            )
        tasks, reused, fresh = plan_tasks(moment)
        results, dests = forward_layer(
            sections,
            2 + moment,
            entry,
            gain_one,
            cosine,
            sine,
            bias,
            gain_two,
            router,
            chosen,
            pick,
            weights,
            tasks,
            len(fresh),
            [payload_all[batch] for batch in reused],
        )
        for batch, dest in zip(reused + fresh, dests):
            payload_all[batch] = dest
        normed, queries, kv, attended, lse, middle, payloads, output = results
        produced.append(output)
        if moment < batches:
            inbound = from_behind(output, 1)
        stored.append(
            dict(
                held=(entry, bias, queries, kv, lse, middle, payloads),
                normed=normed,
                attended=attended,
                payloads=payloads,
            )
        )

    received = None
    moments = []
    for moment in range(batches + 1):
        sections = [s for s in range(2) if 0 <= moment - (1 - s) < batches]
        if received is None:
            grad = output_cotangent[moment]
        else:
            grad = received if moment == batches else choose(received, output_cotangent[moment])
        sets = [
            (s, stored[moment - 1 if s == 0 else moment + 1]["held"]) for s in sections
        ]
        tasks, reused, fresh = plan_tasks(batches + 1) if moment == 0 else ([], [], [])
        wanted = [(s, moment - (1 - s)) for s in sections]
        old = [(s, batch) for s, batch in wanted if grads_all[batch] is not None]
        new = [(s, batch) for s, batch in wanted if grads_all[batch] is None]
        grad_dests = []
        for at, (s, batch) in enumerate(old):
            grad_dests.append((s, len(reused) + at))
        for at, (s, batch) in enumerate(new):
            grad_dests.append((s, len(reused) + len(old) + len(fresh) + at))
        results, dests = backward_layer(
            sections,
            3 + batches + moment,
            grad,
            sets,
            gain_one,
            gain_two,
            router,
            cosine,
            sine,
            pick,
            mark,
            weights,
            tasks,
            grad_dests,
            [width + LANES] * len(fresh) + [width] * len(new),
            [payload_all[batch] for batch in reused] + [grads_all[batch] for _, batch in old],
        )
        dests = list(dests)
        for batch in reused:
            payload_all[batch] = dests.pop(0)
        for _, batch in old:
            grads_all[batch] = dests.pop(0)
        for batch in fresh:
            payload_all[batch] = dests.pop(0)
        for _, batch in new:
            grads_all[batch] = dests.pop(0)
        entry_grad, sent, turned, branch, logit_grad, gain_one_part, gain_two_part = results
        moments.append((entry_grad, turned, branch, logit_grad, gain_one_part, gain_two_part))
        if moment < batches:
            received = from_behind(sent, -1)

    gate_grad, up_grad, down_grad = expert_weights(
        [block.reshape(-1, width + LANES) for block in payload_all],
        [block.reshape(-1, width) for block in grads_all],
        pick,
        gate_all,
        up_all,
        down_all,
    )

    kept = [
        choose(
            (stored[batch]["payloads"][0], stored[batch]["normed"], stored[batch]["attended"]),
            (
                stored[batch + 1]["payloads"][0],
                stored[batch + 1]["normed"],
                stored[batch + 1]["attended"],
            ),
        )
        for batch in range(batches)
    ]
    final = [choose(moments[batch + 1], moments[batch]) for batch in range(batches)]
    layer_outputs = jnp.stack(
        [choose(produced[batch], produced[batch + 1]) for batch in range(batches)]
    )
    input_grads = jnp.stack([part[0] for part in final])

    def stack(parts, axis):
        return jnp.concatenate(parts, axis=axis)

    normed_all = stack([kept[batch][1] for batch in range(batches)], 0)
    attended_all = stack([kept[batch][2] for batch in range(batches)], 1)
    turned_all = stack([part[1] for part in final], 2)
    branch_all = stack([part[2] for part in final], 0)
    part_width = width // groups
    inner_grad = jnp.einsum(
        "td,ect->edc", normed_all, turned_all, preferred_element_type=F32
    ).astype(BF16)
    out_grad = jnp.einsum(
        "ct,ted->ecd",
        attended_all,
        branch_all.reshape(-1, groups, part_width),
        preferred_element_type=F32,
    ).astype(BF16)

    def settle(blocks):
        mine = scatter_sum(
            lambda i: lax.dynamic_index_in_dim(blocks, i, 0, keepdims=False), "expert"
        ).astype(BF16)
        depth = mine.shape[0] // members
        shard = scatter_sum(
            lambda i: lax.dynamic_slice_in_dim(mine, i * depth, depth, 0), "dp"
        ).astype(BF16)
        everyone = jnp.zeros((groups,) + shard.shape, BF16)
        for distance, piece in enumerate(spread(shard)):
            everyone = lax.dynamic_update_index_in_dim(
                everyone, piece, (me - distance) % groups, 0
            )
        return everyone

    def join(block):
        return jnp.moveaxis(block, 0, 1).reshape(block.shape[1], -1).astype(F32)

    inner_grad = settle(inner_grad)
    out_grad = settle(out_grad)
    q_cols = H * HD // groups
    kv_cols = KVH * HD // groups
    query_grad = join(inner_grad[:, :, :q_cols])
    key_grad = join(inner_grad[:, :, q_cols : q_cols + kv_cols])
    value_grad = join(inner_grad[:, :, q_cols + kv_cols :])
    out_grad = join(out_grad)

    small = 0.0
    for batch in range(batches):
        router_part = jnp.einsum(
            "te,td->ed",
            final[batch][3][:, :experts_all],
            kept[batch][0][:, :width],
            preferred_element_type=F32,
        )
        small = small + jnp.concatenate([router_part, final[batch][4], final[batch][5]], axis=0)
    small = lax.psum(small, ("dp", "expert"))
    depth = width // members
    router_grad = lax.dynamic_slice_in_dim(
        small[:experts_all], lax.axis_index("dp") * depth, depth, 1
    ).T
    return (
        layer_outputs[None],
        input_grads[None],
        small[experts_all][None],
        query_grad[None],
        key_grad[None],
        value_grad[None],
        out_grad[None],
        router_grad[None],
        small[experts_all + 1][None],
        gate_grad[None],
        up_grad[None],
        down_grad[None],
    )


def solution(mesh):
    placed = (
        P(None, ("dp", "expert"), None),
        P(None, ("dp", "expert"), None),
        P(None, "dp"),
        P("section", None, ("dp", "expert"), None),
        P("section", None),
        P("section", "dp", None),
        P("section", "dp", None),
        P("section", "dp", None),
        P("section", "dp", None),
        P("section", "dp", None),
        P("section", None),
        P("section", "expert", None, None),
        P("section", "expert", None, None),
        P("section", "expert", None, None),
    )
    return jax.shard_map(
        body,
        mesh=mesh,
        in_specs=placed,
        out_specs=(
            P("section", None, ("dp", "expert"), None),
            P("section", None, ("dp", "expert"), None),
            P("section", None),
            P("section", "dp", None),
            P("section", "dp", None),
            P("section", "dp", None),
            P("section", "dp", None),
            P("section", "dp", None),
            P("section", None),
            P("section", "expert", None, None),
            P("section", "expert", None, None),
            P("section", "expert", None, None),
        ),
        check_vma=False,
    )
```

```python
import functools

import jax
import jax.numpy as jnp
from jax import lax
from jax.experimental import pallas as pl
from jax.experimental.pallas import tpu as pltpu
from jax.sharding import PartitionSpec as P

H = 24
KVH = 8
HD = 64
GROUP = H // KVH
HALF = HD // 2

EPS = 1e-06
THETA = 10000.0
BIG = 1e30
LANES = 128
LOW = 64
SCALE = HD ** (-0.5)
VMEM = 60 * 1024 * 1024
PREPARED = 8192
SMALL = 24
LARGE = 63 * 1024 * 1024

F32 = jnp.float32
BF16 = jnp.bfloat16


def params(*semantics):
    return pltpu.CompilerParams(vmem_limit_bytes=VMEM, dimension_semantics=semantics or None)


def cost(flops, nbytes):
    return pl.CostEstimate(flops=int(flops), bytes_accessed=int(nbytes), transcendentals=0)


def dot(left, right, contract):
    return lax.dot_general(left, right, (contract, ((), ())), preferred_element_type=F32)


def shape(dims, dtype):
    return jax.ShapeDtypeStruct(dims, dtype)


def whole():
    return pl.BlockSpec(memory_space=pltpu.VMEM)


def shift(block, axis, distance, sections=None):
    count = lax.axis_size(axis)
    if sections is None:
        return lax.ppermute(block, axis, [(i, (i + distance) % count) for i in range(count)])
    route = [
        (section * count + i, section * count + (i + distance) % count)
        for section in sections
        for i in range(count)
    ]
    return lax.ppermute(block, ("section", axis), route)


def from_behind(block, distance):
    devices = range(lax.axis_size("section"))
    route = [(i - distance, i) for i in devices if i - distance in devices]
    return lax.ppermute(block, "section", route)


def spread(block, sections=None, axis="expert"):
    return [block] + [
        shift(block, axis, distance, sections) for distance in range(1, lax.axis_size(axis))
    ]


def partner(me, distance):
    other = me
    bit = 1
    while bit <= distance:
        if distance & bit:
            other = other + bit - 2 * bit * (me // bit % 2)
        bit *= 2
    return other


def plane_peers(blocks):
    me = lax.axis_index("expert")
    here = (lax.axis_index("section"), lax.axis_index("dp"))
    return [here + (partner(me, d),) for d in range(1, blocks)]


def line_peers(members):
    place = lax.axis_index("dp")
    return [
        (lax.axis_index("section"), lax.rem(place + k, members), lax.axis_index("expert"))
        for k in range(1, members)
    ]


def greet(peers):
    barrier = pltpu.get_barrier_semaphore()
    for peer in peers:
        pl.semaphore_signal(barrier, inc=1, device_id=peer, device_id_type=pl.DeviceIdType.MESH)
    pl.semaphore_wait(barrier, len(peers))


def send(source, target, send_sem, recv_sem, peer):
    return pltpu.make_async_remote_copy(
        src_ref=source,
        dst_ref=target,
        send_sem=send_sem,
        recv_sem=recv_sem,
        device_id=peer,
        device_id_type=pl.DeviceIdType.MESH,
    )


def in_section(section):
    return pl.when(lax.axis_index("section") == section)


def in_sections(sections):
    if len(sections) == 1:
        return in_section(sections[0])
    return lambda run: run()


def relay_sems(blocks, members):
    line = (2, members - 1)
    plane = (members - 1, blocks - 1)
    return [pltpu.SemaphoreType.DMA(dims) for dims in (line, line, plane, plane, (blocks,))]


class Relay:
    def __init__(self, section, stages, near, dest, pair, sems):
        self.section, self.near, self.dest = section, near, dest
        self.keeps, self.lines, self.planes = ("keep" in stages, "line" in stages, "plane" in stages)
        self.members, self.blocks = dest.shape[:2]
        self.me, self.place = lax.axis_index("expert"), lax.axis_index("dp")
        self.reach = self.blocks - 1 if pair else self.blocks
        self.sent = range(2 if pair else 1)
        self.line_send, self.line_recv, self.plane_send, self.plane_recv, self.near_sem = sems

    def line(self, which, k):
        slot = which * (self.blocks - 1)
        target = self.dest.at[self.place, partner(self.me, slot)]
        return send(
            self.near.at[slot] if self.keeps else target,
            target,
            self.line_send.at[which, k - 1],
            self.line_recv.at[which, k - 1],
            line_peers(self.members)[k - 1],
        )

    def plane(self, k, d):
        block = self.dest.at[lax.rem(self.place + self.members - k, self.members), self.me]
        return send(
            block,
            block,
            self.plane_send.at[k - 1, d - 1],
            self.plane_recv.at[k - 1, d - 1],
            plane_peers(self.blocks)[d - 1],
        )

    def start(self, which):
        if self.lines and which in self.sent:
            for k in range(1, self.members):
                self.line(which, k).start()

    def copies(self):
        return [
            pltpu.make_async_copy(
                self.near.at[d],
                self.dest.at[self.place, partner(self.me, d)],
                self.near_sem.at[d],
            )
            for d in range(self.blocks)
        ]

    def keep(self):
        if self.keeps:
            for copy in self.copies():
                copy.start()

    def open(self):
        if not self.keeps:
            self.start(0)
            self.start(1)

    def forward(self):
        if self.planes:
            for k in range(1, self.members):
                if self.lines:
                    self.line(0, k).wait_recv()
                for d in range(1, self.reach):
                    self.plane(k, d).start()

    def finish(self):
        for k in range(1, self.members):
            if self.lines:
                for which in self.sent:
                    if which or not self.planes:
                        self.line(which, k).wait_recv()
                    self.line(which, k).wait_send()
            if self.planes:
                for d in range(1, self.reach):
                    self.plane(k, d).wait()
        if self.keeps:
            for copy in self.copies():
                copy.wait()


def make_relays(tasks, near, names, dests, take):
    return [
        Relay(
            section,
            stages,
            near if "keep" in stages else None,
            dests[names.index(name)].at[batch],
            pair,
            take(5),
        )
        for section, stages, name, batch, pair in tasks
    ]


def run_relays(relays, step, sections=None, outside=False):
    for relay in relays:
        if sections is None or (relay.section in sections) != outside:
            in_section(relay.section)(lambda relay=relay: step(relay))


def relay_arrays(tasks, arrays):
    names = sorted({task[2] for task in tasks}, key=lambda name: arrays[name][0] is None)
    held = [arrays[name][0] for name in names if arrays[name][0] is not None]
    return names, held, [arrays[name][1] for name in names]


def enter(sections, relays, blocks):
    for section in range(lax.axis_size("section")):
        peers = []
        own = [relay for relay in relays if relay.section == section]
        if section in sections or any(relay.planes for relay in own):
            peers = plane_peers(blocks)
        if any(relay.lines for relay in own):
            peers = peers + line_peers(own[0].members)
        if peers:
            in_section(section)(lambda peers=peers: greet(peers))


def gather_kernel(q_ref, k_ref, v_ref, o_ref, router_ref, inner, out, router, *sems):
    local_sem, line_sem, plane_sem, router_sem, turn_sem = sems
    blocks = inner.shape[0]
    depth = q_ref.shape[0]
    members = inner.shape[1] // depth
    me = lax.axis_index("expert")
    place = lax.axis_index("dp")
    section = lax.axis_index("section")
    diagonal = partner(me, blocks - 1)
    gathered = (inner, out)
    pieces = []
    at = 0
    for source in (q_ref, k_ref, v_ref):
        pieces.append((source, inner, at, source.shape[1] // blocks))
        at += source.shape[1] // blocks
    pieces.append((o_ref, out, 0, o_ref.shape[1] // blocks))
    sent = [(i, me) for i in range(4)] + [(3, diagonal)] + [(i, diagonal) for i in range(3)]

    def rows(member):
        return pl.ds(pl.multiple_of(member * depth, depth), depth)

    def ends(i, e):
        source, target, start, part = pieces[i]
        return (
            source.at[:, pl.ds(pl.multiple_of(e * part, LANES), part)],
            target.at[e, rows(place), pl.ds(start, part)],
        )

    def line(which, k):
        source, target = ends(*sent[which])
        return send(
            source,
            target,
            line_sem.at[0, which, k - 1],
            line_sem.at[1, which, k - 1],
            line_peers(members)[k - 1],
        )

    def plane(which, k, d):
        piece = gathered[which].at[me, rows(lax.rem(place + members - k, members))]
        return send(
            piece,
            piece,
            plane_sem.at[0, which, k - 1, d - 1],
            plane_sem.at[1, which, k - 1, d - 1],
            plane_peers(blocks)[d - 1],
        )

    def narrow(k):
        return send(
            router_ref,
            router.at[rows(place)],
            router_sem.at[0, k - 1],
            router_sem.at[1, k - 1],
            line_peers(members)[k - 1],
        )

    other = (1 - section, place, me)
    greet(plane_peers(blocks) + line_peers(members) + [other])

    @in_section(1)
    def _():
        pl.semaphore_wait(turn_sem, 1)

    for which in range(5):
        for k in range(1, members):
            line(which, k).start()
    for k in range(1, members):
        narrow(k).start()

    @in_section(1)
    def _():
        for which in range(5, 8):
            for k in range(1, members):
                line(which, k).start()

    copies = [pltpu.make_async_copy(router_ref, router.at[rows(place)], local_sem.at[4 * blocks])]
    for e in range(blocks):
        for i in range(4):
            copies.append(pltpu.make_async_copy(*ends(i, e), local_sem.at[4 * e + i]))
    for copy in copies:
        copy.start()
    for k in range(1, members):
        for which in range(3):
            line(which, k).wait_recv()
        for d in range(1, blocks - 1):
            plane(0, k, d).start()

        @in_section(0)
        def _(k=k):
            plane(0, k, blocks - 1).start()

    for k in range(1, members):
        line(3, k).wait_recv()
        for d in range(1, blocks - 1):
            plane(1, k, d).start()
    for k in range(1, members):
        line(4, k).wait_recv()
        narrow(k).wait()

    @in_section(0)
    def _():
        pl.semaphore_signal(
            turn_sem, inc=1, device_id=other, device_id_type=pl.DeviceIdType.MESH
        )

    for k in range(1, members):
        for which in range(5):
            line(which, k).wait_send()
        for which in range(2):
            for d in range(1, blocks - 1):
                plane(which, k, d).wait()

        @in_section(0)
        def _(k=k):
            plane(0, k, blocks - 1).wait()

        @in_section(1)
        def _(k=k):
            for which in range(5, 8):
                line(which, k).wait()

    for copy in copies:
        copy.wait()


def gather_weights(number, q, k, v, o, router):
    blocks = lax.axis_size("expert")
    members = lax.axis_size("dp")
    depth = q.shape[0]
    wide = (q.shape[1] + k.shape[1] + v.shape[1]) // blocks
    anywhere = pl.BlockSpec(memory_space=pl.ANY)
    return pl.pallas_call(
        gather_kernel,
        in_specs=[whole()] * 5,
        out_specs=[anywhere] * 3,
        out_shape=[
            shape((blocks, depth * members, wide), BF16),
            shape((blocks, depth * members, o.shape[1] // blocks), BF16),
            shape((depth * members, LANES), BF16),
        ],
        scratch_shapes=[
            pltpu.SemaphoreType.DMA((1 + 4 * blocks,)),
            pltpu.SemaphoreType.DMA((2, 8, members - 1)),
            pltpu.SemaphoreType.DMA((2, 2, members - 1, blocks - 1)),
            pltpu.SemaphoreType.DMA((2, members - 1)),
            pltpu.SemaphoreType.REGULAR,
        ],
        compiler_params=pltpu.CompilerParams(
            vmem_limit_bytes=VMEM, collective_id=number, has_side_effects=True
        ),
        name="gather_weights",
    )(q, k, v, o, router)


def group_of(ref, group):
    base = pl.multiple_of(group * GROUP * HD, HD)
    return jnp.concatenate(
        [ref[pl.ds(base + head * HD, HD), :] for head in range(GROUP)], axis=1
    )


def keys_of(ref, which, group):
    base = pl.multiple_of(group * HD, HD)
    return jnp.concatenate(
        [ref[block, which, pl.ds(base, HD), :] for block in range(ref.shape[0])], axis=1
    )


def turn_heads(turned, cosine, sine, target, at, count, sign):
    for head in range(0, count, HD):
        leading = turned[head : head + HALF]
        trailing = turned[head + HALF : head + HD]
        target[at + head : at + head + HALF] = (leading * cosine - trailing * sine * sign).astype(
            BF16
        )
        target[at + head + HALF : at + head + HD] = (
            trailing * cosine + leading * sine * sign
        ).astype(BF16)


def forward_kernel(sections, tasks, names, held, groups_of_blocks, *refs):
    refs = list(refs)

    def take(count):
        taken = refs[:count]
        del refs[:count]
        return taken

    inputs = take(14)
    take(held)
    outputs = take(8)
    dests = take(len(names))
    scratch = take(23)
    relays = make_relays(tasks, scratch[11], names, dests, take)
    (
    entry_ref,
    gain_one_ref,
    cos_ref,
    sin_ref,
    bias_ref,
    gain_two_ref,
    router_ref,
    chosen_ref,
    pick_ref,
    inner_hbm,
    out_hbm,
    gate_hbm,
    up_hbm,
    down_hbm,
    ) = inputs
    (
    normed_out,
    q_out,
    kv_out,
    att_out,
    lse_out,
    middle_out,
    payload_out,
    output_out,
    ) = outputs
    (
    inner,
    out,
    gates_w,
    ups_w,
    downs_w,
    normed,
    query,
    kv,
    att,
    lse,
    middle,
    payload,
    sent,
    back,
    own,
    result,
    inner_sem,
    out_sem,
    expert_sem,
    kv_sem,
    payload_sem,
    back_sem,
    save_sem,
    ) = scratch
    blocks = kv.shape[0]
    rows, width = entry_ref.shape
    local, _, hidden_width = gates_w.shape
    queries = query.shape[0] // blocks
    keys = kv.shape[2] // blocks
    part = width // blocks

    enter(sections, relays, blocks)
    run_relays(relays, Relay.open)

    @in_sections(sections)
    def _():
        peers = plane_peers(blocks)
        inner_copies = [
            pltpu.make_async_copy(inner_hbm.at[e], inner.at[e], inner_sem.at[e])
            for e in range(blocks)
        ]
        out_copy = pltpu.make_async_copy(out_hbm, out, out_sem)
        expert_copies = []
        for e in range(local):
            band = pl.ds(e * hidden_width, hidden_width)
            expert_copies.append(
                (
                    pltpu.make_async_copy(gate_hbm.at[e], gates_w.at[e], expert_sem.at[e, 0]),
                    pltpu.make_async_copy(up_hbm.at[e], ups_w.at[e], expert_sem.at[e, 1]),
                    pltpu.make_async_copy(down_hbm.at[e], downs_w.at[band], expert_sem.at[e, 2]),
                )
            )
        for copy in inner_copies:
            copy.start()
        out_copy.start()
        for copies in expert_copies:
            for copy in copies:
                copy.start()

        saves = []

        def save(source, target):
            copy = pltpu.make_async_copy(source, target, save_sem.at[len(saves)])
            copy.start()
            saves.append(copy)

        values = entry_ref[...].astype(F32)
        scale = lax.rsqrt(jnp.mean(values * values, axis=-1, keepdims=True) + EPS)
        normed[...] = (values * scale * gain_one_ref[...]).astype(BF16)
        save(normed, normed_out)
        cosine = cos_ref[...]
        sine = sin_ref[...]
        for e in range(blocks):
            inner_copies[e].wait()
            turned = dot(normed[...], inner[e, :, queries:], ((1,), (0,))).T
            turn_heads(turned[:keys], cosine, sine, kv.at[0, 0], e * keys, keys, 1.0)
            kv[0, 1, e * keys : (e + 1) * keys] = turned[keys:].astype(BF16)
        kv_copies = [
            send(kv.at[0], kv.at[d], kv_sem.at[0, d - 1], kv_sem.at[1, d - 1], peers[d - 1])
            for d in range(1, blocks)
        ]
        for copy in kv_copies:
            copy.start()
        for e in range(blocks):
            turned = dot(normed[...], inner[e, :, :queries], ((1,), (0,))).T
            turn_heads(turned, cosine, sine, query, e * queries, queries, 1.0)
        save(query, q_out)
        bias = jnp.concatenate([bias_ref[...]] * GROUP, axis=1)
        for copy in kv_copies:
            copy.wait()
        save(kv, kv_out)
        run_relays(relays, Relay.forward, sections)

        def one(group, carry):
            query_group = group_of(query, group)
            scores = dot(keys_of(kv, 0, group), query_group, ((0,), (0,))) * SCALE + bias
            highest = jnp.max(scores, axis=0, keepdims=True)
            powers = jnp.exp(scores - highest)
            totals = jnp.sum(powers, axis=0, keepdims=True)
            lse[group] = highest + jnp.log(totals)
            probabilities = (powers * (1.0 / totals)).astype(BF16)
            mixed = dot(keys_of(kv, 1, group), probabilities, ((1,), (0,))).astype(BF16)
            for head in range(GROUP):
                base = pl.multiple_of(group * GROUP * HD + head * HD, HD)
                att[pl.ds(base, HD), :] = mixed[:, head * rows : (head + 1) * rows]
            return carry

        lax.fori_loop(0, kv.shape[2] // HD, one, 0)
        save(att, att_out)
        save(lse, lse_out)
        attended = att[...].T
        out_copy.wait()
        for e in range(blocks):
            columns = slice(e * part, (e + 1) * part)
            middle[:, columns] = entry_ref[:, columns].astype(F32) + dot(
                attended, out[e], ((1,), (0,))
            )
        save(middle, middle_out)
        held = middle[...]
        scale = lax.rsqrt(jnp.mean(held * held, axis=-1, keepdims=True) + EPS)
        normed_two = (held * scale * gain_two_ref[...]).astype(BF16)
        payload[0, :, :width] = normed_two
        logits = dot(normed_two, router_ref[...], ((1,), (0,))) + chosen_ref[...]
        highest = jnp.max(logits, axis=-1, keepdims=True)
        powers = jnp.exp(logits - highest)
        shares = powers / jnp.sum(powers, axis=-1, keepdims=True)
        high = shares.astype(BF16).astype(F32)
        payload[0, :, width:] = (high + pltpu.roll(shares - high, LOW, 1)).astype(BF16)
        payload_copies = [
            send(
                payload.at[0],
                payload.at[d],
                payload_sem.at[0, d - 1],
                payload_sem.at[1, d - 1],
                peers[d - 1],
            )
            for d in range(1, blocks)
        ]
        for copy in payload_copies:
            copy.start()
        back_copies = [
            send(sent.at[d - 1], back.at[d - 1], back_sem.at[0, d - 1], back_sem.at[1, d - 1], peers[d - 1])
            for d in range(1, blocks)
        ]
        for at, members in enumerate(groups_of_blocks):
            for d in members:
                if d:
                    payload_copies[d - 1].wait_recv()
            stacked = jnp.concatenate([payload[d] for d in members], axis=0)
            lanes = stacked[:, width:].astype(F32)
            pieces = []
            for e in range(local):
                if at == 0:
                    for copy in expert_copies[e]:
                        copy.wait()
                gate = dot(stacked[:, :width], gates_w[e], ((1,), (0,)))
                up = dot(stacked[:, :width], ups_w[e], ((1,), (0,)))
                share = jnp.sum(lanes * pick_ref[e], axis=-1, keepdims=True)
                pieces.append((gate / (1.0 + jnp.exp(-gate)) * up * share).astype(BF16))
            total = dot(jnp.concatenate(pieces, axis=1), downs_w[...], ((1,), (0,)))
            for place, d in enumerate(members):
                piece = total[place * rows : (place + 1) * rows]
                if d:
                    sent[d - 1] = piece.astype(BF16)
                    back_copies[d - 1].start()
                else:
                    own[...] = middle[...] + piece
        save(payload, payload_out)
        run_relays(relays, Relay.keep, sections)
        total = own[...]
        for d in range(1, blocks):
            back_copies[d - 1].wait_recv()
            total = total + back[d - 1].astype(F32)
        result[...] = total.astype(BF16)
        save(result, output_out)
        for d in range(1, blocks):
            payload_copies[d - 1].wait_send()
            back_copies[d - 1].wait_send()
        for copy in saves:
            copy.wait()

    run_relays(relays, Relay.forward, sections, outside=True)
    run_relays(relays, Relay.finish)


def forward_layer(
    sections,
    number,
    entry,
    gain_one,
    cosine,
    sine,
    bias,
    gain_two,
    router,
    chosen,
    pick,
    weights,
    tasks,
    arrays,
):
    inner, out, gate_all, up_all, down_all = weights
    rows, width = entry.shape
    blocks = inner.shape[0]
    members = lax.axis_size("dp")
    names, before, dests = relay_arrays(tasks, arrays)
    local, _, hidden = gate_all.shape
    keys = KVH * HD
    flops = 2 * rows * width * (H + 2 * KVH) * HD + 4 * rows * rows * blocks * H * HD
    flops += 2 * rows * H * HD * width + 6 * rows * blocks * local * width * hidden
    groups_of_blocks = [[0], list(range(1, blocks - 1)), [blocks - 1]]
    pair = (2, blocks - 1)
    anywhere = pl.BlockSpec(memory_space=pl.ANY)
    results = pl.pallas_call(
        functools.partial(
            forward_kernel, sections, tasks, names, len(before), groups_of_blocks
        ),
        in_specs=[whole()] * 9 + [anywhere] * (5 + len(before)),
        out_specs=[anywhere] * (8 + len(names)),
        out_shape=[
            shape((rows, width), BF16),
            shape((H * HD, rows), BF16),
            shape((blocks, 2, keys, rows), BF16),
            shape((H * HD, rows), BF16),
            shape((KVH, 1, GROUP * rows), F32),
            shape((rows, width), F32),
            shape((blocks, rows, width + LANES), BF16),
            shape((rows, width), BF16),
            *dests,
        ],
        scratch_shapes=[
            pltpu.VMEM(inner.shape, BF16),
            pltpu.VMEM(out.shape, BF16),
            pltpu.VMEM(gate_all.shape, BF16),
            pltpu.VMEM(up_all.shape, BF16),
            pltpu.VMEM((local * hidden, width), BF16),
            pltpu.VMEM((rows, width), BF16),
            pltpu.VMEM((H * HD, rows), BF16),
            pltpu.VMEM((blocks, 2, keys, rows), BF16),
            pltpu.VMEM((H * HD, rows), BF16),
            pltpu.VMEM((KVH, 1, GROUP * rows), F32),
            pltpu.VMEM((rows, width), F32),
            pltpu.VMEM((blocks, rows, width + LANES), BF16),
            pltpu.VMEM((blocks - 1, rows, width), BF16),
            pltpu.VMEM((blocks - 1, rows, width), BF16),
            pltpu.VMEM((rows, width), F32),
            pltpu.VMEM((rows, width), BF16),
            pltpu.SemaphoreType.DMA((blocks,)),
            pltpu.SemaphoreType.DMA(()),
            pltpu.SemaphoreType.DMA((local, 3)),
            pltpu.SemaphoreType.DMA(pair),
            pltpu.SemaphoreType.DMA(pair),
            pltpu.SemaphoreType.DMA(pair),
            pltpu.SemaphoreType.DMA((8,)),
        ]
        + relay_sems(blocks, members) * len(tasks),
        input_output_aliases={14 + i: 8 + i for i in range(len(before))},
        compiler_params=pltpu.CompilerParams(
            vmem_limit_bytes=VMEM, collective_id=number, has_side_effects=True
        ),
        cost_estimate=cost(flops, 3e7),
        name="forward_layer",
    )(
        entry,
        gain_one,
        cosine,
        sine,
        bias,
        gain_two,
        router,
        chosen,
        pick,
        inner,
        out,
        gate_all,
        up_all,
        down_all,
        *before,
    )
    return results[:8], dict(zip(names, results[8:]))


def activation(gate, up, hidden_grad):
    sigmoid = 1.0 / (1.0 + jnp.exp(-gate))
    silu = gate * sigmoid
    slope = sigmoid * (1.0 + gate * (1.0 - sigmoid))
    return silu * up, hidden_grad * up * slope, hidden_grad * silu


def norm_back(values, gain, grad):
    width = values.shape[1]
    scale = lax.rsqrt(jnp.mean(values * values, axis=-1, keepdims=True) + EPS)
    scaled = grad * gain
    inner = jnp.sum(values * scaled, axis=-1, keepdims=True) * (1.0 / width)
    part = scale * scaled - values * (scale * scale * scale * inner)
    return part, jnp.sum(grad * values * scale, axis=0, keepdims=True)


HELD = 7


def backward_kernel(sections, holders, tasks, names, before, groups_of_blocks, *refs):
    refs = list(refs)

    def take(count):
        taken = refs[:count]
        del refs[:count]
        return taken

    g_ref, gain_one_ref, gain_two_ref, router_ref, cos_ref, sin_ref, pick_ref, mark_ref = take(8)
    inner_hbm, out_hbm, gate_hbm, up_hbm, down_hbm = take(5)
    sets = [take(HELD) for _ in holders]
    take(before)
    outputs = take(7)
    dests = take(len(names))
    gates_w, ups_w, downs_w, out, inner = take(5)
    held = take(HELD)
    entry, bias_v, query, kv, lse, middle, payload = held
    grads, gate_v, up_v, own, sent, back = take(6)
    branch, logit, middle_grad, datt = take(4)
    own_kv, sent_kv, back_kv, turned, entry_grad, entry_low, gain_one_v, gain_two_v = take(8)
    expert_sem, out_sem, inner_sem, held_sem, grads_sem, back_sem, kv_sem, save_sem = take(8)
    relays = make_relays(tasks, grads, names, dests, take)
    grad_relays = [relay for relay in relays if relay.keeps]

    blocks, rows, width = grads.shape
    local, _, hidden_width = gates_w.shape
    keys = kv.shape[2]
    part = width // blocks
    queries = H * HD // blocks
    own_keys = keys // blocks

    enter(sections, relays, blocks)
    run_relays(relays, Relay.open)

    @in_sections(sections)
    def _():
        peers = plane_peers(blocks)
        expert_copies = []
        for e in range(local):
            band = pl.ds(e * hidden_width, hidden_width)
            expert_copies.append(
                (
                    pltpu.make_async_copy(gate_hbm.at[e], gates_w.at[e], expert_sem.at[e, 0]),
                    pltpu.make_async_copy(up_hbm.at[e], ups_w.at[e], expert_sem.at[e, 1]),
                    pltpu.make_async_copy(down_hbm.at[e], downs_w.at[band], expert_sem.at[e, 2]),
                )
            )
        out_copy = pltpu.make_async_copy(out_hbm, out, out_sem)
        inner_copy = pltpu.make_async_copy(inner_hbm, inner, inner_sem)
        grads[0] = g_ref[...]
        grads_copies = [
            send(
                grads.at[0],
                grads.at[d],
                grads_sem.at[0, d - 1],
                grads_sem.at[1, d - 1],
                peers[d - 1],
            )
            for d in range(1, blocks)
        ]
        for copy in grads_copies:
            copy.start()

        def fetch(at, index):
            return pltpu.make_async_copy(sets[at][index], held[index], held_sem.at[index])

        order = (HELD - 1,) + tuple(range(HELD - 1))
        for at, section in enumerate(holders):

            @in_section(section)
            def _(at=at):
                fetch(at, HELD - 1).start()

        for copy in expert_copies[0]:
            copy.start()
        for at, section in enumerate(holders):

            @in_section(section)
            def _(at=at):
                for index in order[1:]:
                    fetch(at, index).start()

        for copies in expert_copies[1:]:
            for copy in copies:
                copy.start()
        out_copy.start()
        inner_copy.start()
        run_relays(grad_relays, lambda relay: relay.start(0))

        saves = []

        def save(source, target):
            copy = pltpu.make_async_copy(source, target, save_sem.at[len(saves)])
            copy.start()
            saves.append(copy)

        fetch(0, HELD - 1).wait()
        stacked = payload[...].reshape(blocks * rows, width + LANES)
        for e in range(local):
            for copy in expert_copies[e]:
                copy.wait()
            gate_v[e] = dot(stacked[:, :width], gates_w[e], ((1,), (0,)))
            up_v[e] = dot(stacked[:, :width], ups_w[e], ((1,), (0,)))
        back_copies = [
            send(
                sent.at[d - 1],
                back.at[d - 1],
                back_sem.at[0, d - 1],
                back_sem.at[1, d - 1],
                peers[d - 1],
            )
            for d in range(1, blocks)
        ]
        for members in groups_of_blocks:
            for d in members:
                if d:
                    grads_copies[d - 1].wait_recv()
            if blocks - 1 in members:
                run_relays(grad_relays, lambda relay: relay.start(1))
                run_relays(grad_relays, Relay.keep)

            held_rows = slice(members[0] * rows, (members[-1] + 1) * rows)
            grad = jnp.concatenate([grads[d] for d in members], axis=0)
            lanes = jnp.concatenate([payload[d, :, width:] for d in members], axis=0).astype(F32)
            hidden_grad = dot(grad, downs_w[...], ((1,), (1,)))
            total = jnp.zeros((rows * len(members), width), F32)
            share = jnp.zeros((rows * len(members), LANES), F32)
            for e in range(local):
                columns = slice(e * hidden_width, (e + 1) * hidden_width)
                raw = hidden_grad[:, columns]
                hidden, gate_part, up_part = activation(gate_v[e, held_rows], up_v[e, held_rows], raw)
                hidden = hidden.astype(BF16).astype(F32)
                share = share + jnp.sum(hidden * raw, axis=-1, keepdims=True) * mark_ref[e]
                weight = jnp.sum(lanes * pick_ref[e], axis=-1, keepdims=True)
                total = total + dot((gate_part * weight).astype(BF16), gates_w[e], ((1,), (1,)))
                total = total + dot((up_part * weight).astype(BF16), ups_w[e], ((1,), (1,)))
            high = share.astype(BF16).astype(F32)
            both = high + pltpu.roll(share - high, LOW, 1)
            for place, d in enumerate(members):
                band = slice(place * rows, (place + 1) * rows)
                if d:
                    sent[d - 1, :, :width] = total[band].astype(BF16)
                    sent[d - 1, :, width:] = both[band].astype(BF16)
                    back_copies[d - 1].start()
                else:
                    own[:, :width] = total[band]
                    own[:, width:] = share[band]
        for at, section in enumerate(holders):
            if at == 0:
                for index in order[1:]:
                    fetch(0, index).wait()

        total = own[:, :width]
        share = own[:, width:]
        for d in range(1, blocks):
            back_copies[d - 1].wait_recv()
            total = total + back[d - 1, :, :width].astype(F32)
            share = share + back[d - 1, :, width:].astype(F32)
        run_relays(relays, Relay.forward, sections)
        first = lax.broadcasted_iota(jnp.int32, (1, LANES), 1) < LOW
        shares = payload[0, :, width:].astype(F32)
        shares = jnp.where(first, shares + pltpu.roll(shares, LOW, 1), 0.0)
        share = jnp.where(first, share + pltpu.roll(share, LOW, 1), 0.0)
        weighted = shares * share
        logit_grad = (weighted - shares * jnp.sum(weighted, axis=-1, keepdims=True)).astype(BF16)
        logit[...] = logit_grad
        total = total + dot(logit_grad, router_ref[...], ((1,), (1,)))
        piece, gain_two_v[...] = norm_back(middle[...], gain_two_ref[...], total)
        middle_grad[...] = g_ref[...].astype(F32) + piece
        branch[...] = middle_grad[...].astype(BF16)
        save(logit, outputs[4])
        save(branch, outputs[3])
        save(gain_two_v, outputs[6])
        out_copy.wait()
        total = jnp.zeros(datt.shape, F32)
        for e in range(blocks):
            total = total + dot(out[e], branch[:, e * part : (e + 1) * part], ((1,), (1,)))
        datt[...] = total.astype(BF16)

        bias = jnp.concatenate([bias_v[...]] * GROUP, axis=1)
        cosine = cos_ref[...]
        sine = sin_ref[...]
        per_block = queries // (GROUP * HD)

        def one(group, carry):
            query_group = group_of(query, group)
            key_group = keys_of(kv, 0, group)
            grad_group = group_of(datt, group)
            scores = dot(key_group, query_group, ((0,), (0,))) * SCALE + bias
            probabilities = jnp.exp(scores - lse[group])
            probability_grad = dot(keys_of(kv, 1, group), grad_group, ((0,), (0,)))
            centre = jnp.sum(probabilities * probability_grad, axis=0, keepdims=True)
            score_grad = (probabilities * (probability_grad - centre)).astype(BF16)
            query_part = dot(key_group, score_grad, ((1,), (0,))) * SCALE
            e = lax.div(group, per_block)
            base = lax.rem(group, per_block) * (GROUP * HD)
            for head in range(GROUP):
                start = pl.multiple_of(base + head * HD, HALF)
                leading = query_part[:HALF, head * rows : (head + 1) * rows]
                trailing = query_part[HALF:, head * rows : (head + 1) * rows]
                turned[e, pl.ds(start, HALF), :] = (leading * cosine + trailing * sine).astype(BF16)
                turned[e, pl.ds(start + HALF, HALF), :] = (
                    trailing * cosine - leading * sine
                ).astype(BF16)
            key_part = dot(query_group, score_grad, ((1,), (1,))) * SCALE
            value_part = dot(grad_group, probabilities.astype(BF16), ((1,), (1,)))
            base = pl.multiple_of(group * HD, HD)
            for which, piece in ((0, key_part), (1, value_part)):
                own_kv[which, pl.ds(base, HD), :] = piece[:, :rows]
                for d in range(1, blocks):
                    sent_kv[d - 1, which, pl.ds(base, HD), :] = piece[
                        :, d * rows : (d + 1) * rows
                    ].astype(BF16)
            return carry

        heads = keys // HD
        kv_copies = []
        for half in range(2):
            lax.fori_loop(half * heads // 2, (half + 1) * heads // 2, one, 0)
            band = pl.ds(half * keys // 2, keys // 2)
            for d in range(1, blocks):
                copy = send(
                    sent_kv.at[d - 1, :, band],
                    back_kv.at[d - 1, :, band],
                    kv_sem.at[0, half, d - 1],
                    kv_sem.at[1, half, d - 1],
                    peers[d - 1],
                )
                copy.start()
                kv_copies.append(copy)

        inner_copy.wait()
        total = jnp.zeros((rows, width), F32)
        for e in range(blocks):
            total = total + dot(turned[e, :queries], inner[e, :, :queries], ((0,), (1,)))
        for copy in kv_copies:
            copy.wait_recv()
        pair = own_kv[...]
        for d in range(1, blocks):
            pair = pair + back_kv[d - 1].astype(F32)
        for e in range(blocks):
            band = slice(e * own_keys, (e + 1) * own_keys)
            turn_heads(pair[0, band], cosine, sine, turned.at[e], queries, own_keys, -1.0)
            turned[e, queries + own_keys :] = pair[1, band].astype(BF16)
        save(turned, outputs[2])
        for e in range(blocks):
            total = total + dot(turned[e, queries:], inner[e, :, queries:], ((0,), (1,)))
        piece, gain_one_v[...] = norm_back(entry[...].astype(F32), gain_one_ref[...], total)
        result = middle_grad[...] + piece
        entry_grad[...] = result
        entry_low[...] = result.astype(BF16)
        save(entry_low, outputs[1])
        save(entry_grad, outputs[0])
        save(gain_one_v, outputs[5])
        for d in range(1, blocks):
            grads_copies[d - 1].wait_send()
            back_copies[d - 1].wait_send()
        for copy in kv_copies:
            copy.wait_send()
        for copy in saves:
            copy.wait()

    run_relays(relays, Relay.forward, sections, outside=True)
    run_relays(relays, Relay.finish)


def backward_layer(
    sections,
    number,
    grad,
    sets,
    gain_one,
    gain_two,
    router,
    cosine,
    sine,
    pick,
    mark,
    weights,
    tasks,
    arrays,
):
    names, before, dests = relay_arrays(tasks, arrays)
    inner, out, gate_all, up_all, down_all = weights
    rows, width = grad.shape
    blocks = inner.shape[0]
    members = lax.axis_size("dp")
    local, _, hidden = gate_all.shape
    keys = KVH * HD
    length = rows * blocks
    flops = 4 * rows * width * (H + 2 * KVH) * HD + 10 * rows * length * H * HD
    flops += 2 * rows * H * HD * width + 10 * length * local * width * hidden
    groups_of_blocks = [[0], list(range(1, blocks - 1)), [blocks - 1]]
    pair = (2, blocks - 1)
    anywhere = pl.BlockSpec(memory_space=pl.ANY)
    first_before = 13 + HELD * len(sets)
    held = sets[0][1]
    results = pl.pallas_call(
        functools.partial(
            backward_kernel,
            sections,
            [section for section, _ in sets],
            tasks,
            names,
            len(before),
            groups_of_blocks,
        ),
        in_specs=[whole()] * 8
        + [anywhere] * (5 + HELD * len(sets) + len(before)),
        out_specs=[anywhere] * (7 + len(names)),
        out_shape=[
            shape((rows, width), F32),
            shape((rows, width), BF16),
            shape((blocks, inner.shape[2], rows), BF16),
            shape((rows, width), BF16),
            shape((rows, LANES), BF16),
            shape((1, width), F32),
            shape((1, width), F32),
            *dests,
        ],
        scratch_shapes=[
            pltpu.VMEM(gate_all.shape, BF16),
            pltpu.VMEM(up_all.shape, BF16),
            pltpu.VMEM((local * hidden, width), BF16),
            pltpu.VMEM(out.shape, BF16),
            pltpu.VMEM(inner.shape, BF16),
        ]
        + [pltpu.VMEM(array.shape, array.dtype) for array in held]
        + [
            pltpu.VMEM((blocks, rows, width), BF16),
            pltpu.VMEM((local, length, hidden), F32),
            pltpu.VMEM((local, length, hidden), F32),
            pltpu.VMEM((rows, width + LANES), F32),
            pltpu.VMEM((blocks - 1, rows, width + LANES), BF16),
            pltpu.VMEM((blocks - 1, rows, width + LANES), BF16),
            pltpu.VMEM((rows, width), BF16),
            pltpu.VMEM((rows, LANES), BF16),
            pltpu.VMEM((rows, width), F32),
            pltpu.VMEM((H * HD, rows), BF16),
            pltpu.VMEM((2, keys, rows), F32),
            pltpu.VMEM((blocks - 1, 2, keys, rows), BF16),
            pltpu.VMEM((blocks - 1, 2, keys, rows), BF16),
            pltpu.VMEM((blocks, inner.shape[2], rows), BF16),
            pltpu.VMEM((rows, width), F32),
            pltpu.VMEM((rows, width), BF16),
            pltpu.VMEM((1, width), F32),
            pltpu.VMEM((1, width), F32),
            pltpu.SemaphoreType.DMA((local, 3)),
            pltpu.SemaphoreType.DMA(()),
            pltpu.SemaphoreType.DMA(()),
            pltpu.SemaphoreType.DMA((HELD,)),
            pltpu.SemaphoreType.DMA(pair),
            pltpu.SemaphoreType.DMA(pair),
            pltpu.SemaphoreType.DMA((2, 2, blocks - 1)),
            pltpu.SemaphoreType.DMA((7,)),
        ]
        + relay_sems(blocks, members) * len(tasks),
        input_output_aliases={first_before + i: 7 + i for i in range(len(before))},
        compiler_params=pltpu.CompilerParams(
            vmem_limit_bytes=VMEM, collective_id=number, has_side_effects=True
        ),
        cost_estimate=cost(flops, 4e7),
        name="backward_layer",
    )(
        grad,
        gain_one,
        gain_two,
        router,
        cosine,
        sine,
        pick,
        mark,
        inner,
        out,
        gate_all,
        up_all,
        down_all,
        *[array for _, held_arrays in sets for array in held_arrays],
        *before,
    )
    return results[:7], dict(zip(names, results[7:]))


def prepare_kernel(tile, batches, *refs):
    tokens, (pick, gate_w, up_w, *outputs) = refs[:batches], refs[batches:]
    local, width, hidden_width = gate_w.shape
    count = tokens[0].shape[0] // tile

    def body(x_ref, pick_ref, gate_ref, up_ref, hidden_ref, gate_factor_ref, up_factor_ref):
        entry = x_ref[:, :width]
        weight = jnp.sum(x_ref[:, width:].astype(F32) * pick_ref[0], axis=-1, keepdims=True)
        gate = dot(entry, gate_ref[0], ((1,), (0,)))
        up = dot(entry, up_ref[0], ((1,), (0,)))
        held, gate_part, up_part = activation(gate, up, weight)
        hidden_ref[...] = (held * weight).astype(BF16)
        gate_factor_ref[...] = gate_part.astype(BF16)
        up_factor_ref[...] = up_part.astype(BF16)

    @in_section(0)
    def _():
        weight = pl.BlockSpec((1, width, hidden_width), lambda t, e: (e, 0, 0))
        for batch, x_hbm in enumerate(tokens):
            piece = pl.BlockSpec((tile, hidden_width), lambda t, e: (batch * count + t, e))
            pltpu.emit_pipeline(
                body,
                grid=(count, local),
                in_specs=[
                    pl.BlockSpec((tile, width + LANES), lambda t, e: (t, 0)),
                    pl.BlockSpec((1, 1, LANES), lambda t, e: (e, 0, 0)),
                    weight,
                    weight,
                ],
                out_specs=[piece] * 3,
            )(x_hbm, pick, gate_w, up_w, *outputs)


def prepare(tokens, pick, gate_all, up_all, tile=512):
    local, width, hidden = gate_all.shape
    rows = sum(block.shape[0] for block in tokens)
    anywhere = pl.BlockSpec(memory_space=pl.ANY)
    return pl.pallas_call(
        functools.partial(prepare_kernel, min(tile, tokens[0].shape[0]), len(tokens)),
        in_specs=[anywhere] * (3 + len(tokens)),
        out_specs=[anywhere] * 3,
        out_shape=[shape((rows, local * hidden), BF16)] * 3,
        compiler_params=params(),
        cost_estimate=cost(4 * rows * local * width * hidden, rows * width * 8),
        name="prepare",
    )(*tokens, pick, gate_all, up_all)


def weights_step(ready, x_ref, g_ref, down_ref, held, outs):
    width = g_ref.shape[1]
    entry = x_ref[:, :width]
    grad = g_ref[...]
    hidden_grad = dot(grad, down_ref[0], ((1,), (1,)))
    if ready:
        hidden = held[0][...]
        gate_part = hidden_grad * held[1][...].astype(F32)
        up_part = hidden_grad * held[2][...].astype(F32)
    else:
        pick_ref, gate_ref, up_ref = held[-3:]
        weight = jnp.sum(x_ref[:, width:].astype(F32) * pick_ref[0], axis=-1, keepdims=True)
        gate = dot(entry, gate_ref[0], ((1,), (0,)))
        up = dot(entry, up_ref[0], ((1,), (0,)))
        hidden, gate_part, up_part = activation(gate, up, hidden_grad * weight)
        hidden = (hidden * weight).astype(BF16)
    dgate_ref, dup_ref, ddown_ref = outs
    dgate_ref[0] += dot(entry, gate_part.astype(BF16), ((0,), (0,)))
    dup_ref[0] += dot(entry, up_part.astype(BF16), ((0,), (0,)))
    ddown_ref[0] += dot(hidden, grad, ((0,), (0,)))


def weights_specs(ready, first, tile, expert, shapes):
    width, hidden = shapes
    columns = pl.BlockSpec((1, width, hidden), lambda e, t: (expert(e), 0, 0))
    bands = pl.BlockSpec((1, hidden, width), lambda e, t: (expert(e), 0, 0))
    piece = pl.BlockSpec((tile, hidden), lambda e, t: (first + t, expert(e)))
    specs = [
        pl.BlockSpec((tile, width + LANES), lambda e, t: (t, 0)),
        pl.BlockSpec((tile, width), lambda e, t: (t, 0)),
        bands,
    ]
    if ready:
        specs += [piece] * 3
    specs += [pl.BlockSpec((1, 1, LANES), lambda e, t: (expert(e), 0, 0)), columns, columns]
    return specs, [columns, columns, bands]


def weights_both(ready, x_ref, g_ref, down_ref, held, outs):
    if not ready:
        weights_step(False, x_ref, g_ref, down_ref, held, outs)
        return
    for section in range(2):

        @in_section(section)
        def _(section=section):
            weights_step(section == 0, x_ref, g_ref, down_ref, held, outs)


def first_weights_kernel(ready, tasks, names, *refs):
    refs = list(refs)

    def take(count):
        taken = refs[:count]
        del refs[:count]
        return taken

    x_ref, g_ref, down_ref, *held = take(9 if ready else 6)
    take(len(names))
    outs = take(3)
    dests = take(len(names))
    relays = make_relays(tasks, None, names, dests, take)
    step = pl.program_id(0) * pl.num_programs(1) + pl.program_id(1)

    early = [relay for relay in relays if relay.section == 0]
    late = [relay for relay in relays if relay.section != 0]

    @pl.when(step == 0)
    def _():
        enter([], early, dests[0].shape[2])
        run_relays(early, Relay.forward)

    @pl.when(pl.program_id(1) == 0)
    def _():
        for out in outs:
            out[...] = jnp.zeros_like(out)

    weights_both(ready, x_ref, g_ref, down_ref, held, outs)

    @pl.when(step == pl.num_programs(0) * pl.num_programs(1) - 1)
    def _():
        enter([], late, dests[0].shape[2])
        run_relays(late, Relay.forward)
        run_relays(relays, Relay.finish)


def first_weights(number, tasks, arrays, tokens, grads, down_all, prepared, forward, tile=512):
    local, hidden, width = down_all.shape
    names, before, dests = relay_arrays(tasks, arrays)
    _, members, blocks, _, _ = dests[0].shape
    rows = grads.shape[0]
    tile = min(tile, rows)
    ready = prepared is not None
    specs, outs = weights_specs(ready, 0, tile, lambda e: e, (width, hidden))
    anywhere = pl.BlockSpec(memory_space=pl.ANY)
    results = pl.pallas_call(
        functools.partial(first_weights_kernel, ready, tasks, names),
        grid=(1, rows // tile),
        in_specs=specs + [anywhere] * len(names),
        out_specs=outs + [anywhere] * len(names),
        out_shape=[
            shape((local, width, hidden), F32),
            shape((local, width, hidden), F32),
            shape((local, hidden, width), F32),
            *dests,
        ],
        scratch_shapes=relay_sems(blocks, members) * len(tasks),
        input_output_aliases={len(specs) + i: 3 + i for i in range(len(names))},
        compiler_params=pltpu.CompilerParams(
            vmem_limit_bytes=VMEM,
            collective_id=number,
            has_side_effects=True,
            dimension_semantics=("arbitrary", "arbitrary"),
        ),
        cost_estimate=cost(8 * rows * width * hidden, rows * (4 * width + 6 * hidden)),
        name="first_weights",
    )(tokens, grads, down_all, *(prepared if ready else ()), *forward, *before)
    return results[:3], dict(zip(names, results[3:]))


def whole_weights_kernel(ready, batches, *refs):
    x_refs, refs = refs[:batches], refs[batches:]
    g_refs, (down_ref, *rest) = refs[:batches], refs[batches:]
    held = rest[: 6 if ready else 3]
    outs = rest[-3:]
    tiles = pl.num_programs(0) // batches

    @pl.when(pl.program_id(0) == 0)
    def _():
        for out in outs:
            out[...] = jnp.zeros_like(out)

    for batch in range(batches):

        @pl.when(pl.program_id(0) // tiles == batch)
        def _(batch=batch):
            weights_both(ready, x_refs[batch], g_refs[batch], down_ref, held, outs)


def whole_weights(expert, tokens, grads, down_all, prepared, forward, chain=None, tile=512):
    local, hidden, width = down_all.shape
    batches = len(tokens)
    rows = grads[0].shape[0]
    tile = min(tile, rows)
    tiles = rows // tile
    ready = prepared is not None
    chained = chain is not None

    def band(batch, lanes):
        return pl.BlockSpec((tile, lanes), lambda t: (jnp.clip(t - batch * tiles, 0, tiles - 1), 0))

    columns = pl.BlockSpec((1, width, hidden), lambda t: (expert, 0, 0))
    bands = pl.BlockSpec((1, hidden, width), lambda t: (expert, 0, 0))
    specs = [band(batch, width + LANES) for batch in range(batches)]
    specs += [band(batch, width) for batch in range(batches)] + [bands]
    if ready:
        specs += [pl.BlockSpec((tile, hidden), lambda t: (t, expert))] * 3
    specs += [pl.BlockSpec((1, 1, LANES), lambda t: (expert, 0, 0)), columns, columns]
    return pl.pallas_call(
        functools.partial(whole_weights_kernel, ready, batches),
        grid=(batches * tiles,),
        in_specs=specs + [pl.BlockSpec(memory_space=pl.ANY)] * (3 if chained else 0),
        out_specs=[columns, columns, bands],
        out_shape=[
            shape((local, width, hidden), F32),
            shape((local, width, hidden), F32),
            shape((local, hidden, width), F32),
        ],
        input_output_aliases={len(specs) + i: i for i in range(3)} if chained else {},
        compiler_params=pltpu.CompilerParams(
            vmem_limit_bytes=LARGE, dimension_semantics=("arbitrary",)
        ),
        cost_estimate=cost(
            8 * rows * batches * width * hidden, rows * batches * (4 * width + 6 * hidden)
        ),
        name="whole_weights",
    )(
        *tokens,
        *grads,
        down_all,
        *(prepared if ready else ()),
        *forward,
        *(chain if chained else ()),
    )


def last_weights_kernel(ready, chained, *refs):
    x_ref, g_ref, down_ref, *rest = refs
    count = 6 if ready else 3
    held, before = rest[:count], rest[count : count + 3]
    outs = rest[count + 6 :] if chained else rest[count + 3 :]

    @pl.when(pl.program_id(1) == 0)
    def _():
        for out, source in zip(outs, before):
            out[...] = source[...]

    weights_both(ready, x_ref, g_ref, down_ref, held, outs)


def last_weights(experts, tokens, grads, down_all, prepared, forward, before, chain=None, tile=512):
    in_place = chain is before
    if in_place:
        chain = None
    local, hidden, width = down_all.shape
    rows = grads.shape[0]
    tile = min(tile, rows)
    chained = chain is not None
    ready = prepared is not None
    first = (prepared[0].shape[0] - rows) // tile if ready else 0
    specs, outs = weights_specs(ready, first, tile, lambda e: experts[0] + e, (width, hidden))
    held = [
        pl.BlockSpec(spec.block_shape, spec.index_map, pipeline_mode=pl.Buffered(1)) for spec in outs
    ]
    count = len(specs)
    anywhere = pl.BlockSpec(memory_space=pl.ANY)
    return pl.pallas_call(
        functools.partial(last_weights_kernel, ready, chained),
        grid=(experts[1] - experts[0], rows // tile),
        in_specs=specs + held + [anywhere] * (3 if chained else 0),
        out_specs=outs,
        out_shape=[
            shape((local, width, hidden), F32),
            shape((local, width, hidden), F32),
            shape((local, hidden, width), F32),
        ],
        input_output_aliases={count + (3 if chained else 0) + i: i for i in range(3)}
        if chained or in_place
        else {},
        compiler_params=pltpu.CompilerParams(
            vmem_limit_bytes=LARGE, dimension_semantics=("arbitrary", "arbitrary")
        ),
        cost_estimate=cost(
            8 * rows * width * hidden * (experts[1] - experts[0]), rows * (4 * width + 6 * hidden)
        ),
        name="last_weights",
    )(
        tokens,
        grads,
        down_all,
        *(prepared if ready else ()),
        *forward,
        *before,
        *(chain if chained else ()),
    )


def attention_weights_kernel(section, batches, blocks, members, by_rows, *refs):
    sets = [refs[8 * m : 8 * m + 8] for m in range(batches)]
    refs = refs[8 * batches :]
    count = members if by_rows else blocks
    outputs = refs[:count]
    small_out = refs[count]
    held = refs[count + 1 : count + 1 + blocks]
    normed, turned, attended, branch, mixed, logit, gains, small, sems, save_sems = refs[
        count + 1 + blocks :
    ]
    place = lax.axis_index("dp")
    depth = held[0].shape[0] // members
    rows = normed.shape[0] // batches
    me = lax.axis_index("expert")
    part = branch.shape[1] // blocks
    columns = turned.shape[1]

    @in_section(section)
    def _():
        copies = []
        for m in range(batches):
            band = pl.ds(m * rows, rows)
            targets = (
                normed.at[band],
                turned.at[:, :, band],
                attended.at[:, band],
                branch.at[band],
                mixed.at[band],
                logit.at[band],
                gains.at[m, 0],
                gains.at[m, 1],
            )
            for i, (source, target) in enumerate(zip(sets[m], targets)):
                copies.append(pltpu.make_async_copy(source, target, sems.at[m, i]))
        for copy in copies:
            copy.start()
        for copy in copies:
            copy.wait()
        router = dot(logit[...], mixed[:, : normed.shape[1]], ((0,), (0,)))
        small[...] = router[: small.shape[0]]
        for i in range(2):
            total = gains[0, i]
            for m in range(1, batches):
                total = total + gains[m, i]
            small[pl.ds(small.shape[0] - 2 + i, 1), :] = total
        saves = [pltpu.make_async_copy(small, small_out, save_sems.at[blocks, 0])]
        saves[0].start()
        for d in [*range(1, blocks), 0]:
            e = partner(me, d)
            at = pl.multiple_of(e * part, LANES)
            held[d][:, :columns] = dot(normed[...], turned[e], ((0,), (1,))).astype(BF16)
            held[d][:, columns:] = dot(
                attended[...], branch[:, pl.ds(at, part)], ((1,), (0,))
            ).astype(BF16)
            if not by_rows:
                saves.append(pltpu.make_async_copy(held[d], outputs[d], save_sems.at[d, 0]))
                saves[-1].start()
                continue
            for k in range(members):
                at = pl.multiple_of(lax.rem(place + k, members) * depth, depth)
                save = pltpu.make_async_copy(
                    held[d].at[pl.ds(at, depth)],
                    outputs[k].at[pl.ds(d * depth, depth)],
                    save_sems.at[d, k],
                )
                save.start()
                saves.append(save)
        for save in saves:
            save.wait()


def attention_weights(section, sets, by_rows):
    members = lax.axis_size("dp")
    batches = len(sets)
    normed, turned, attended, branch, mixed, logit, _, _ = sets[0]
    blocks, columns, rows = turned.shape
    width = branch.shape[1]
    wide = columns + width // blocks
    flat = [array for one in sets for array in one]
    anywhere = pl.BlockSpec(memory_space=pl.ANY)
    return pl.pallas_call(
        functools.partial(
            attention_weights_kernel, section, batches, blocks, members, by_rows
        ),
        in_specs=[anywhere] * len(flat),
        out_specs=[anywhere] * (1 + (members if by_rows else blocks)),
        out_shape=(
            [shape((width * blocks // members, wide), BF16)] * members
            if by_rows
            else [shape((width, wide), BF16)] * blocks
        )
        + [shape((SMALL, width), F32)],
        scratch_shapes=[pltpu.VMEM((width, wide), BF16)] * blocks
        + [
            pltpu.VMEM((batches * rows, width), BF16),
            pltpu.VMEM((blocks, columns, batches * rows), BF16),
            pltpu.VMEM((attended.shape[0], batches * rows), BF16),
            pltpu.VMEM((batches * rows, width), BF16),
            pltpu.VMEM((batches * rows, mixed.shape[1]), BF16),
            pltpu.VMEM((batches * rows, logit.shape[1]), BF16),
            pltpu.VMEM((batches, 2, 1, width), F32),
            pltpu.VMEM((SMALL, width), F32),
            pltpu.SemaphoreType.DMA((batches, 8)),
            pltpu.SemaphoreType.DMA((blocks + 1, members)),
        ],
        compiler_params=params(),
        cost_estimate=cost(2 * batches * rows * width * wide * blocks, 2e7),
        name="attention_weights",
    )(*flat)


def sum_kernel(counts, depth, *refs):
    output = refs[-1]
    wide = output.shape[1]
    tile = depth // 2
    at = 0
    for section, (terms, bands) in enumerate(counts):

        def body(*tiles, terms=terms):
            total = tiles[0][...].astype(F32)
            for piece in tiles[1:terms]:
                total = total + piece[...].astype(F32)
            tiles[terms][...] = total.astype(BF16)

        @in_section(section)
        def _(at=at, terms=terms, bands=bands, section=section, body=body):
            first = 2 * lax.axis_index("dp") if section == 0 else 0
            pltpu.emit_pipeline(
                body,
                grid=(2 * bands,),
                in_specs=[
                    pl.BlockSpec((tile, wide), lambda i: (lax.rem(first + i, 2 * bands), 0))
                ]
                * terms,
                out_specs=[pl.BlockSpec((tile, wide), lambda i: (i, 0))],
            )(*refs[at : at + terms], output)

        at += terms


def sum_blocks(upper, lower, depth):
    wide = upper[0].shape[1]
    rows = max(upper[0].shape[0], lower[0].shape[0])
    counts = [(len(terms), terms[0].shape[0] // depth) for terms in (upper, lower)]
    anywhere = pl.BlockSpec(memory_space=pl.ANY)
    total = pl.pallas_call(
        functools.partial(sum_kernel, counts, depth),
        in_specs=[anywhere] * (len(upper) + len(lower)),
        out_specs=anywhere,
        out_shape=shape((rows, wide), BF16),
        compiler_params=params(),
        cost_estimate=cost(0, rows * wide * 2 * (len(upper) + 1)),
        name="sum_blocks",
    )(*upper, *lower)
    return jnp.split(total, rows // depth, axis=0)


def small_kernel(upper, lower, total, own, plane, line, fetch_sem, plane_sem, line_sem):
    blocks = plane.shape[0] + 1
    members = line.shape[0] + 1
    for section, source in ((0, upper), (1, lower)):

        @in_section(section)
        def _(source=source):
            fetch = pltpu.make_async_copy(source, own, fetch_sem)
            fetch.start()
            fetch.wait()

    greet(plane_peers(blocks) + line_peers(members))
    for peers, room, sems in (
        (plane_peers(blocks), plane, plane_sem),
        (line_peers(members), line, line_sem),
    ):
        copies = [
            send(own, room.at[i], sems.at[0, i], sems.at[1, i], peer) for i, peer in enumerate(peers)
        ]
        for copy in copies:
            copy.start()
        for copy in copies:
            copy.wait()
        held = own[...]
        for i in range(len(peers)):
            held = held + room[i]
        own[...] = held
    total[...] = own[...]


def sum_small(number, upper, lower):
    blocks = lax.axis_size("expert")
    members = lax.axis_size("dp")
    return pl.pallas_call(
        small_kernel,
        in_specs=[pl.BlockSpec(memory_space=pl.ANY)] * 2,
        out_specs=whole(),
        out_shape=shape(upper.shape, F32),
        scratch_shapes=[
            pltpu.VMEM(upper.shape, F32),
            pltpu.VMEM((blocks - 1,) + upper.shape, F32),
            pltpu.VMEM((members - 1,) + upper.shape, F32),
            pltpu.SemaphoreType.DMA(()),
            pltpu.SemaphoreType.DMA((2, blocks - 1)),
            pltpu.SemaphoreType.DMA((2, members - 1)),
        ],
        compiler_params=pltpu.CompilerParams(
            vmem_limit_bytes=VMEM, collective_id=number, has_side_effects=True
        ),
        name="sum_small",
    )(upper, lower)


def assemble_kernel(blocks, *refs):
    outputs = refs[blocks:]
    me = lax.axis_index("expert")
    for d in range(blocks):
        e = partner(me, d)
        at = 0
        for out in outputs:
            part = out.shape[1] // blocks
            start = pl.multiple_of(e * part, LANES)
            out[:, pl.ds(start, part)] = refs[d][:, at : at + part].astype(F32)
            at += part


def assemble(shards, widths):
    rows = shards[0].shape[0]
    return pl.pallas_call(
        functools.partial(assemble_kernel, len(shards)),
        in_specs=[whole()] * len(shards),
        out_specs=[whole()] * len(widths),
        out_shape=[shape((rows, columns), F32) for columns in widths],
        compiler_params=params(),
        cost_estimate=cost(0, rows * sum(widths) * 6),
        name="assemble",
    )(*shards)


def pad_lanes(block):
    return jnp.pad(block, ((0, 0), (0, LANES - block.shape[1])))


def swap(block, distance, sections):
    count = lax.axis_size("expert")
    route = [
        (section * count + i, section * count + (i ^ distance))
        for section in sections
        for i in range(count)
    ]
    return lax.ppermute(block, ("section", "expert"), route)


def total_of(blocks):
    return functools.reduce(jnp.add, [block.astype(F32) for block in blocks]).astype(BF16)


def body(
    layer_input,
    output_cotangent,
    documents,
    expert_routes,
    attention_gain,
    query_weight,
    key_weight,
    value_weight,
    output_weight,
    router_weight,
    mixture_gain,
    expert_gate,
    expert_up,
    expert_down,
):
    batches, rows, width = layer_input.shape
    groups = lax.axis_size("expert")
    members = lax.axis_size("dp")
    local = expert_gate.shape[1]
    experts_all = local * groups
    me = lax.axis_index("expert")
    first = lax.axis_index("section") == 0

    def choose(upper, lower):
        return jax.tree.map(lambda a, b: jnp.where(first, a, b), upper, lower)

    places = (me * rows + jnp.arange(rows, dtype=jnp.int32)).astype(F32)
    inverse = THETA ** (-jnp.arange(HALF, dtype=F32) * 2.0 / HD)
    angles = inverse[:, None] * places[None, :]
    cosine = jnp.cos(angles)
    sine = jnp.sin(angles)
    number = me * local + jnp.arange(local, dtype=jnp.int32)
    lanes = jnp.arange(LANES, dtype=jnp.int32)
    mark = (lanes[None, :] == number[:, None]).astype(F32)[:, None, :]
    pick = mark + (lanes[None, :] == number[:, None] + LOW).astype(F32)[:, None, :]

    def bias_of(batch):
        labels = documents[batch]
        own = lax.dynamic_slice_in_dim(labels, me * rows, rows)
        pieces = []
        for distance in range(groups):
            source = me ^ distance
            theirs = lax.dynamic_slice_in_dim(labels, source * rows, rows)
            order = source * rows + jnp.arange(rows, dtype=jnp.int32)
            allowed = (theirs[:, None] == own[None, :]) & (
                order[:, None] <= (me * rows + jnp.arange(rows, dtype=jnp.int32))[None, :]
            )
            pieces.append(jnp.where(allowed, 0.0, -BIG))
        return jnp.concatenate(pieces, axis=0)

    def chosen_of(batch):
        named = (expert_routes[0, batch][:, :, None] == lanes[None, None, :]).any(axis=1)
        return jnp.where(named, 0.0, -BIG)

    biases = [bias_of(batch) for batch in range(batches)]
    chosens = [chosen_of(batch) for batch in range(batches)]

    inner, out, router = gather_weights(
        0,
        query_weight[0],
        key_weight[0],
        value_weight[0],
        output_weight[0],
        pad_lanes(router_weight[0]),
    )
    gain_one = attention_gain
    gain_two = mixture_gain
    gate_all, up_all, down_all = (expert_gate[0], expert_up[0], expert_down[0])
    weights = (inner, out, gate_all, up_all, down_all)

    def active(moment):
        return [s for s in range(2) if 0 <= moment - s < batches]

    stored = []
    produced = []
    inbound = jnp.zeros((rows, width), BF16)
    arrays = {
        "p0": [None, shape((1, members, groups, rows, width + LANES), BF16)],
        "p1": [None, shape((1, members, groups, rows, width + LANES), BF16)],
        "g0": [None, shape((1, members, groups, rows, width), BF16)],
        "g1": [None, shape((1, members, groups, rows, width), BF16)],
    }

    def keep_arrays(made):
        for name, array in made.items():
            arrays[name][0] = array

    plans = {
        ("forward", 0): [(0, ("keep",), "p0", 0, True)],
        ("forward", 1): [
            (0, ("line",), "p0", 0, True),
            (0, ("keep",), "p1", 0, True),
            (1, ("keep",), "p0", 0, True),
        ],
        ("forward", 2): [
            (1, ("line",), "p0", 0, True),
            (0, ("line", "plane"), "p1", 0, False),
            (0, ("plane",), "p0", 0, True),
            (1, ("keep",), "p1", 0, True),
        ],
        ("backward", 0): [
            (1, ("keep", "line"), "g0", 0, True),
            (1, ("line",), "p1", 0, True),
            (1, ("plane",), "p0", 0, True),
        ],
        ("backward", 1): [
            (0, ("keep", "line"), "g0", 0, True),
            (1, ("keep", "line"), "g1", 0, True),
            (1, ("plane",), "g0", 0, True),
        ],
        ("backward", 2): [
            (0, ("keep", "line"), "g1", 0, False),
            (0, ("plane",), "g0", 0, True),
        ],
        ("weights", 0): [
            (0, ("plane",), "g1", 0, False),
            (1, ("plane",), "g1", 0, True),
            (1, ("plane",), "p1", 0, True),
        ],
    }

    for moment in range(batches + 1):
        sections = active(moment)
        early = min(moment, batches - 1)
        late = max(moment - 1, 0)
        if sections == [0]:
            entry, bias, chosen = layer_input[early], biases[early], chosens[early]
        elif sections == [1]:
            entry, bias, chosen = inbound, biases[late], chosens[late]
        else:
            entry, bias, chosen = choose(
                (layer_input[early], biases[early], chosens[early]),
                (inbound, biases[late], chosens[late]),
            )
        results, made = forward_layer(
            sections,
            1 + moment,
            entry,
            gain_one,
            cosine,
            sine,
            bias,
            gain_two,
            router,
            chosen,
            pick,
            weights,
            plans["forward", moment],
            arrays,
        )
        keep_arrays(made)
        normed, queries, kv, attended, lse, middle, payloads, output = results
        produced.append(output)
        if moment < batches:
            inbound = from_behind(output, 1)
        stored.append(
            dict(
                held=(entry, bias, queries, kv, lse, middle, payloads),
                normed=normed,
                attended=attended,
                payloads=payloads,
            )
        )

    def attention_terms(section):
        parts = list(
            attention_weights(
            section,
            [
                (
                    stored[batch + section]["normed"],
                    moments[batch + 1 - section][1],
                    stored[batch + section]["attended"],
                    moments[batch + 1 - section][2],
                    stored[batch + section]["payloads"][0],
                    *moments[batch + 1 - section][3:],
                )
                for batch in range(batches)
            ],
            section == 1,
        ))
        small[section] = parts.pop()
        if section == 1:
            return [parts[0]] + [shift(parts[k], "dp", k, [1]) for k in range(1, members)]
        return [parts[0]] + [swap(parts[d], d, [0]) for d in range(1, groups)]

    prepared = None
    terms = [None, None]
    small = [None, None]

    received = None
    moments = []
    for moment in range(batches + 1):
        sections = [s for s in range(2) if 0 <= moment - (1 - s) < batches]
        if received is None:
            grad = output_cotangent[moment]
        else:
            grad = received if moment == batches else choose(received, output_cotangent[moment])
        sets = [
            (s, stored[moment - 1 if s == 0 else moment + 1]["held"]) for s in sections
        ]
        results, made = backward_layer(
            sections,
            2 + batches + moment,
            grad,
            sets,
            gain_one,
            gain_two,
            router,
            cosine,
            sine,
            pick,
            mark,
            weights,
            plans["backward", moment],
            arrays,
        )
        keep_arrays(made)
        entry_grad, sent, turned, branch, logit_grad, gain_one_part, gain_two_part = results
        moments.append((entry_grad, turned, branch, logit_grad, gain_one_part, gain_two_part))
        if moment == 0:
            both = [arrays[name][0].reshape(-1, width + LANES) for name in ("p0", "p1")]
            if sum(block.shape[0] for block in both) <= PREPARED:
                prepared = prepare(both, pick, gate_all, up_all)
        if moment < batches:
            received = from_behind(sent, -1)
            if moment == 0:
                received, prepared = lax.optimization_barrier((received, prepared))

    moments, stored = lax.optimization_barrier((moments, stored))
    terms[1] = attention_terms(1)

    forward = (pick, gate_all, up_all)
    tight = prepared is None

    def halfway(terms):
        pieces = sum_blocks(terms[0], terms[1], width // members)
        arrived = [pieces[0]]
        for k in range(1, max(members, groups)):
            route = []
            for i in range(members):
                for e in range(groups):
                    if k < members:
                        route.append((i * groups + e, (i + k) % members * groups + e))
                    if k < groups:
                        base = (members + i) * groups
                        route.append((base + e, base + (e ^ k)))
            arrived.append(lax.ppermute(pieces[k], ("section", "dp", "expert"), route))
        return arrived

    first_grads = arrays["g0"][0].reshape(-1, width)
    terms[0] = attention_terms(0) if tight else None
    if tight:
        shards = halfway(terms)
        shards, first_grads = lax.optimization_barrier((shards, first_grads))
    partial, made = first_weights(
        3 + 2 * batches,
        plans["weights", 0],
        arrays,
        arrays["p0"][0].reshape(-1, width + LANES),
        first_grads,
        down_all,
        prepared,
        forward,
    )
    keep_arrays(made)
    if not tight:
        stored, partial = lax.optimization_barrier((stored, partial))
        terms[0] = attention_terms(0)
    tokens = [arrays[name][0].reshape(-1, width + LANES) for name in ("p0", "p1")]
    grads = [arrays[name][0].reshape(-1, width) for name in ("g0", "g1")]
    totals = partial if tight else None
    for expert in range(1, local):
        totals = whole_weights(expert, tokens, grads, down_all, prepared, forward, totals)
    small, terms, totals = lax.optimization_barrier((small, terms, totals))
    small = sum_small(4 + 2 * batches, small[0], small[1])
    if not tight:
        terms, small = lax.optimization_barrier((terms, small))
        shards = halfway(terms)
    if totals is None:
        totals = partial
    totals = last_weights(
        (0, 1),
        tokens[-1],
        grads[-1],
        down_all,
        prepared,
        forward,
        totals if tight else partial,
        totals,
    )
    shards, totals = lax.optimization_barrier((shards, totals))
    shard = total_of(shards)
    shards = [shard] + [swap(shard, d, [0, 1]) for d in range(1, groups)]
    gate_grad, up_grad, down_grad = totals
    query_grad, key_grad, value_grad, out_grad = assemble(
        shards,
        [H * HD, KVH * HD, KVH * HD, width],
    )

    final = [choose(moments[batch + 1], moments[batch]) for batch in range(batches)]
    layer_outputs = jnp.stack(
        [choose(produced[batch], produced[batch + 1]) for batch in range(batches)]
    )
    input_grads = jnp.stack([part[0] for part in final])

    depth = width // members
    router_grad = lax.dynamic_slice_in_dim(
        small[:experts_all], lax.axis_index("dp") * depth, depth, 1
    ).T
    return (
        layer_outputs[None],
        input_grads[None],
        small[SMALL - 2][None],
        query_grad[None],
        key_grad[None],
        value_grad[None],
        out_grad[None],
        router_grad[None],
        small[SMALL - 1][None],
        gate_grad[None],
        up_grad[None],
        down_grad[None],
    )


def solution(mesh):
    placed = (
        P(None, ("dp", "expert"), None),
        P(None, ("dp", "expert"), None),
        P(None, "dp"),
        P("section", None, ("dp", "expert"), None),
        P("section", None),
        P("section", "dp", None),
        P("section", "dp", None),
        P("section", "dp", None),
        P("section", "dp", None),
        P("section", "dp", None),
        P("section", None),
        P("section", "expert", None, None),
        P("section", "expert", None, None),
        P("section", "expert", None, None),
    )
    return jax.shard_map(
        body,
        mesh=mesh,
        in_specs=placed,
        out_specs=(
            P("section", None, ("dp", "expert"), None),
            P("section", None, ("dp", "expert"), None),
            P("section", None),
            P("section", "dp", None),
            P("section", "dp", None),
            P("section", "dp", None),
            P("section", "dp", None),
            P("section", "dp", None),
            P("section", None),
            P("section", "expert", None, None),
            P("section", "expert", None, None),
            P("section", "expert", None, None),
        ),
        check_vma=False,
    )
```

```python
import functools

import jax
import jax.numpy as jnp
from jax import lax
from jax.experimental import pallas as pl
from jax.experimental.pallas import tpu as pltpu
from jax.sharding import PartitionSpec as P

H = 24
KVH = 8
HD = 64
GROUP = H // KVH
HALF = HD // 2

EPS = 1e-06
THETA = 10000.0
BIG = 1e30
LANES = 128
LOW = 64
SCALE = HD ** (-0.5)
VMEM = 60 * 1024 * 1024
PREPARED = 8192
SMALL = 16
LARGE = 63 * 1024 * 1024

F32 = jnp.float32
BF16 = jnp.bfloat16


def params(*semantics):
    return pltpu.CompilerParams(vmem_limit_bytes=VMEM, dimension_semantics=semantics or None)


def cost(flops, nbytes):
    return pl.CostEstimate(flops=int(flops), bytes_accessed=int(nbytes), transcendentals=0)


def dot(left, right, contract):
    return lax.dot_general(left, right, (contract, ((), ())), preferred_element_type=F32)


def shape(dims, dtype):
    return jax.ShapeDtypeStruct(dims, dtype)


def whole():
    return pl.BlockSpec(memory_space=pltpu.VMEM)


def shift(block, axis, distance, sections=None):
    count = lax.axis_size(axis)
    if sections is None:
        return lax.ppermute(block, axis, [(i, (i + distance) % count) for i in range(count)])
    route = [
        (section * count + i, section * count + (i + distance) % count)
        for section in sections
        for i in range(count)
    ]
    return lax.ppermute(block, ("section", axis), route)


def from_behind(block, distance):
    devices = range(lax.axis_size("section"))
    route = [(i - distance, i) for i in devices if i - distance in devices]
    return lax.ppermute(block, "section", route)


def spread(block, sections=None, axis="expert"):
    return [block] + [
        shift(block, axis, distance, sections) for distance in range(1, lax.axis_size(axis))
    ]


def partner(me, distance):
    other = me
    bit = 1
    while bit <= distance:
        if distance & bit:
            other = other + bit - 2 * bit * (me // bit % 2)
        bit *= 2
    return other


def plane_peers(blocks):
    me = lax.axis_index("expert")
    here = (lax.axis_index("section"), lax.axis_index("dp"))
    return [here + (partner(me, d),) for d in range(1, blocks)]


def line_peers(members):
    place = lax.axis_index("dp")
    return [
        (lax.axis_index("section"), lax.rem(place + k, members), lax.axis_index("expert"))
        for k in range(1, members)
    ]


def greet(peers):
    barrier = pltpu.get_barrier_semaphore()
    for peer in peers:
        pl.semaphore_signal(barrier, inc=1, device_id=peer, device_id_type=pl.DeviceIdType.MESH)
    pl.semaphore_wait(barrier, len(peers))


def send(source, target, send_sem, recv_sem, peer):
    return pltpu.make_async_remote_copy(
        src_ref=source,
        dst_ref=target,
        send_sem=send_sem,
        recv_sem=recv_sem,
        device_id=peer,
        device_id_type=pl.DeviceIdType.MESH,
    )


def in_section(section):
    return pl.when(lax.axis_index("section") == section)


def in_sections(sections):
    if len(sections) == 1:
        return in_section(sections[0])
    return lambda run: run()


def relay_sems(blocks, members):
    line = (2, members - 1)
    plane = (members - 1, blocks - 1)
    return [pltpu.SemaphoreType.DMA(dims) for dims in (line, line, plane, plane, (blocks,))]


class Relay:
    def __init__(self, section, stages, near, dest, pair, sems):
        self.section, self.near, self.dest = section, near, dest
        self.keeps, self.lines, self.planes = ("keep" in stages, "line" in stages, "plane" in stages)
        self.members, self.blocks = dest.shape[:2]
        self.me, self.place = lax.axis_index("expert"), lax.axis_index("dp")
        self.reach = self.blocks - 1 if pair else self.blocks
        self.sent = range(2 if pair else 1)
        self.line_send, self.line_recv, self.plane_send, self.plane_recv, self.near_sem = sems

    def line(self, which, k):
        slot = which * (self.blocks - 1)
        target = self.dest.at[self.place, partner(self.me, slot)]
        return send(
            self.near.at[slot] if self.keeps else target,
            target,
            self.line_send.at[which, k - 1],
            self.line_recv.at[which, k - 1],
            line_peers(self.members)[k - 1],
        )

    def plane(self, k, d):
        block = self.dest.at[lax.rem(self.place + self.members - k, self.members), self.me]
        return send(
            block,
            block,
            self.plane_send.at[k - 1, d - 1],
            self.plane_recv.at[k - 1, d - 1],
            plane_peers(self.blocks)[d - 1],
        )

    def start(self, which):
        if self.lines and which in self.sent:
            for k in range(1, self.members):
                self.line(which, k).start()

    def copies(self):
        return [
            pltpu.make_async_copy(
                self.near.at[d],
                self.dest.at[self.place, partner(self.me, d)],
                self.near_sem.at[d],
            )
            for d in range(self.blocks)
        ]

    def keep(self):
        if self.keeps:
            for copy in self.copies():
                copy.start()

    def open(self):
        if not self.keeps:
            self.start(0)
            self.start(1)

    def forward(self):
        if self.planes:
            for k in range(1, self.members):
                if self.lines:
                    self.line(0, k).wait_recv()
                for d in range(1, self.reach):
                    self.plane(k, d).start()

    def finish(self):
        for k in range(1, self.members):
            if self.lines:
                for which in self.sent:
                    if which or not self.planes:
                        self.line(which, k).wait_recv()
                    self.line(which, k).wait_send()
            if self.planes:
                for d in range(1, self.reach):
                    self.plane(k, d).wait()
        if self.keeps:
            for copy in self.copies():
                copy.wait()


def make_relays(tasks, near, names, dests, take):
    return [
        Relay(
            section,
            stages,
            near if "keep" in stages else None,
            dests[names.index(name)].at[batch],
            pair,
            take(5),
        )
        for section, stages, name, batch, pair in tasks
    ]


def run_relays(relays, step, sections=None, outside=False):
    for relay in relays:
        if sections is None or (relay.section in sections) != outside:
            in_section(relay.section)(lambda relay=relay: step(relay))


def relay_arrays(tasks, arrays):
    names = sorted({task[2] for task in tasks}, key=lambda name: arrays[name][0] is None)
    held = [arrays[name][0] for name in names if arrays[name][0] is not None]
    return names, held, [arrays[name][1] for name in names]


def enter(sections, relays, blocks):
    for section in range(lax.axis_size("section")):
        peers = []
        own = [relay for relay in relays if relay.section == section]
        if section in sections or any(relay.planes for relay in own):
            peers = plane_peers(blocks)
        if any(relay.lines for relay in own):
            peers = peers + line_peers(own[0].members)
        if peers:
            in_section(section)(lambda peers=peers: greet(peers))


def gather_kernel(q_ref, k_ref, v_ref, o_ref, router_ref, inner, out, router, *scratch):
    inner_room, out_room, local_sem, line_sem, plane_sem, router_sem, turn_sem = scratch
    blocks = inner.shape[0]
    depth = q_ref.shape[0]
    members = inner.shape[1] // depth
    me = lax.axis_index("expert")
    place = lax.axis_index("dp")
    section = lax.axis_index("section")
    diagonal = partner(me, blocks - 1)
    gathered = (inner, out)
    rooms = (inner_room, out_room)
    sent = ((0, 0), (1, 0), (1, blocks - 1), (0, blocks - 1))

    def rows(member):
        return pl.ds(pl.multiple_of(member * depth, depth), depth)

    def fill(d):
        e = partner(me, d)
        at = 0
        for source in (q_ref, k_ref, v_ref):
            part = source.shape[1] // blocks
            columns = pl.ds(pl.multiple_of(e * part, LANES), part)
            inner_room[d, :, at : at + part] = source[:, columns]
            at += part
        part = o_ref.shape[1] // blocks
        out_room[d] = o_ref[:, pl.ds(pl.multiple_of(e * part, LANES), part)]

    def line(which, k):
        array, d = sent[which]
        return send(
            rooms[array].at[d],
            gathered[array].at[partner(me, d), rows(place)],
            line_sem.at[0, which, k - 1],
            line_sem.at[1, which, k - 1],
            line_peers(members)[k - 1],
        )

    def plane(which, k, d):
        piece = gathered[which].at[me, rows(lax.rem(place + members - k, members))]
        return send(
            piece,
            piece,
            plane_sem.at[0, which, k - 1, d - 1],
            plane_sem.at[1, which, k - 1, d - 1],
            plane_peers(blocks)[d - 1],
        )

    def narrow(k):
        return send(
            router_ref,
            router.at[rows(place)],
            router_sem.at[0, k - 1],
            router_sem.at[1, k - 1],
            line_peers(members)[k - 1],
        )

    other = (1 - section, place, me)
    fill(0)
    fill(blocks - 1)
    greet(plane_peers(blocks) + line_peers(members) + [other])

    @in_section(1)
    def _():
        pl.semaphore_wait(turn_sem, 1)

    for which in range(3):
        for k in range(1, members):
            line(which, k).start()
    for k in range(1, members):
        narrow(k).start()

    @in_section(1)
    def _():
        for k in range(1, members):
            line(3, k).start()

    for d in range(1, blocks - 1):
        fill(d)
    copies = [pltpu.make_async_copy(router_ref, router.at[rows(place)], local_sem.at[2 * blocks])]
    for d in range(blocks):
        for array in range(2):
            copies.append(
                pltpu.make_async_copy(
                    rooms[array].at[d],
                    gathered[array].at[partner(me, d), rows(place)],
                    local_sem.at[2 * d + array],
                )
            )
    for copy in copies:
        copy.start()
    for which in range(2):
        for k in range(1, members):
            line(which, k).wait_recv()
            for d in range(1, blocks - 1):
                plane(which, k, d).start()
            if which == 0:

                @in_section(0)
                def _(k=k):
                    plane(0, k, blocks - 1).start()

    for k in range(1, members):
        line(2, k).wait_recv()
        narrow(k).wait()

    @in_section(0)
    def _():
        pl.semaphore_signal(
            turn_sem, inc=1, device_id=other, device_id_type=pl.DeviceIdType.MESH
        )

    for k in range(1, members):
        for which in range(3):
            line(which, k).wait_send()
        for which in range(2):
            for d in range(1, blocks - 1):
                plane(which, k, d).wait()

        @in_section(0)
        def _(k=k):
            plane(0, k, blocks - 1).wait()

        @in_section(1)
        def _(k=k):
            line(3, k).wait()

    for copy in copies:
        copy.wait()


def gather_weights(number, q, k, v, o, router):
    blocks = lax.axis_size("expert")
    members = lax.axis_size("dp")
    depth = q.shape[0]
    wide = (q.shape[1] + k.shape[1] + v.shape[1]) // blocks
    anywhere = pl.BlockSpec(memory_space=pl.ANY)
    return pl.pallas_call(
        gather_kernel,
        in_specs=[whole()] * 5,
        out_specs=[anywhere] * 3,
        out_shape=[
            shape((blocks, depth * members, wide), BF16),
            shape((blocks, depth * members, o.shape[1] // blocks), BF16),
            shape((depth * members, LANES), BF16),
        ],
        scratch_shapes=[
            pltpu.VMEM((blocks, depth, wide), BF16),
            pltpu.VMEM((blocks, depth, o.shape[1] // blocks), BF16),
            pltpu.SemaphoreType.DMA((1 + 2 * blocks,)),
            pltpu.SemaphoreType.DMA((2, 4, members - 1)),
            pltpu.SemaphoreType.DMA((2, 2, members - 1, blocks - 1)),
            pltpu.SemaphoreType.DMA((2, members - 1)),
            pltpu.SemaphoreType.REGULAR,
        ],
        compiler_params=pltpu.CompilerParams(
            vmem_limit_bytes=VMEM, collective_id=number, has_side_effects=True
        ),
        name="gather_weights",
    )(q, k, v, o, router)


def group_of(ref, group):
    base = pl.multiple_of(group * GROUP * HD, HD)
    return jnp.concatenate(
        [ref[pl.ds(base + head * HD, HD), :] for head in range(GROUP)], axis=1
    )


def keys_of(ref, which, group):
    base = pl.multiple_of(group * HD, HD)
    return jnp.concatenate(
        [ref[block, which, pl.ds(base, HD), :] for block in range(ref.shape[0])], axis=1
    )


def turn_heads(turned, cosine, sine, target, at, count, sign):
    for head in range(0, count, HD):
        leading = turned[head : head + HALF]
        trailing = turned[head + HALF : head + HD]
        target[at + head : at + head + HALF] = (leading * cosine - trailing * sine * sign).astype(
            BF16
        )
        target[at + head + HALF : at + head + HD] = (
            trailing * cosine + leading * sine * sign
        ).astype(BF16)


def forward_kernel(sections, tasks, names, held, groups_of_blocks, *refs):
    refs = list(refs)

    def take(count):
        taken = refs[:count]
        del refs[:count]
        return taken

    inputs = take(14)
    take(held)
    outputs = take(8)
    dests = take(len(names))
    scratch = take(23)
    relays = make_relays(tasks, scratch[11], names, dests, take)
    (
    entry_ref,
    gain_one_ref,
    cos_ref,
    sin_ref,
    bias_ref,
    gain_two_ref,
    router_ref,
    chosen_ref,
    pick_ref,
    inner_hbm,
    out_hbm,
    gate_hbm,
    up_hbm,
    down_hbm,
    ) = inputs
    (
    normed_out,
    q_out,
    kv_out,
    att_out,
    lse_out,
    middle_out,
    payload_out,
    output_out,
    ) = outputs
    (
    inner,
    out,
    gates_w,
    ups_w,
    downs_w,
    normed,
    query,
    kv,
    att,
    lse,
    middle,
    payload,
    sent,
    back,
    own,
    result,
    inner_sem,
    out_sem,
    expert_sem,
    kv_sem,
    payload_sem,
    back_sem,
    save_sem,
    ) = scratch
    blocks = kv.shape[0]
    rows, width = entry_ref.shape
    local, _, hidden_width = gates_w.shape
    queries = query.shape[0] // blocks
    keys = kv.shape[2] // blocks
    part = width // blocks

    enter(sections, relays, blocks)
    run_relays(relays, Relay.open)

    @in_sections(sections)
    def _():
        peers = plane_peers(blocks)
        inner_copies = [
            pltpu.make_async_copy(inner_hbm.at[e], inner.at[e], inner_sem.at[e])
            for e in range(blocks)
        ]
        out_copy = pltpu.make_async_copy(out_hbm, out, out_sem)
        expert_copies = []
        for e in range(local):
            band = pl.ds(e * hidden_width, hidden_width)
            expert_copies.append(
                (
                    pltpu.make_async_copy(gate_hbm.at[e], gates_w.at[e], expert_sem.at[e, 0]),
                    pltpu.make_async_copy(up_hbm.at[e], ups_w.at[e], expert_sem.at[e, 1]),
                    pltpu.make_async_copy(down_hbm.at[e], downs_w.at[band], expert_sem.at[e, 2]),
                )
            )
        for copy in inner_copies:
            copy.start()
        out_copy.start()
        for copies in expert_copies:
            for copy in copies:
                copy.start()

        saves = []

        def save(source, target):
            copy = pltpu.make_async_copy(source, target, save_sem.at[len(saves)])
            copy.start()
            saves.append(copy)

        values = entry_ref[...].astype(F32)
        scale = lax.rsqrt(jnp.mean(values * values, axis=-1, keepdims=True) + EPS)
        normed[...] = (values * scale * gain_one_ref[...]).astype(BF16)
        save(normed, normed_out)
        cosine = cos_ref[...]
        sine = sin_ref[...]
        for e in range(blocks):
            inner_copies[e].wait()
            turned = dot(normed[...], inner[e, :, queries:], ((1,), (0,))).T
            turn_heads(turned[:keys], cosine, sine, kv.at[0, 0], e * keys, keys, 1.0)
            kv[0, 1, e * keys : (e + 1) * keys] = turned[keys:].astype(BF16)
        kv_copies = [
            send(kv.at[0], kv.at[d], kv_sem.at[0, d - 1], kv_sem.at[1, d - 1], peers[d - 1])
            for d in range(1, blocks)
        ]
        for copy in kv_copies:
            copy.start()
        for e in range(blocks):
            turned = dot(normed[...], inner[e, :, :queries], ((1,), (0,))).T
            turn_heads(turned, cosine, sine, query, e * queries, queries, 1.0)
        save(query, q_out)
        bias = jnp.concatenate([bias_ref[...]] * GROUP, axis=1)
        for copy in kv_copies:
            copy.wait()
        save(kv, kv_out)
        run_relays(relays, Relay.forward, sections)

        def one(group, carry):
            query_group = group_of(query, group)
            scores = dot(keys_of(kv, 0, group), query_group, ((0,), (0,))) * SCALE + bias
            highest = jnp.max(scores, axis=0, keepdims=True)
            powers = jnp.exp(scores - highest)
            totals = jnp.sum(powers, axis=0, keepdims=True)
            lse[group] = highest + jnp.log(totals)
            probabilities = (powers * (1.0 / totals)).astype(BF16)
            mixed = dot(keys_of(kv, 1, group), probabilities, ((1,), (0,))).astype(BF16)
            for head in range(GROUP):
                base = pl.multiple_of(group * GROUP * HD + head * HD, HD)
                att[pl.ds(base, HD), :] = mixed[:, head * rows : (head + 1) * rows]
            return carry

        lax.fori_loop(0, kv.shape[2] // HD, one, 0)
        save(att, att_out)
        save(lse, lse_out)
        attended = att[...].T
        out_copy.wait()
        for e in range(blocks):
            columns = slice(e * part, (e + 1) * part)
            middle[:, columns] = entry_ref[:, columns].astype(F32) + dot(
                attended, out[e], ((1,), (0,))
            )
        save(middle, middle_out)
        held = middle[...]
        scale = lax.rsqrt(jnp.mean(held * held, axis=-1, keepdims=True) + EPS)
        normed_two = (held * scale * gain_two_ref[...]).astype(BF16)
        payload[0, :, :width] = normed_two
        logits = dot(normed_two, router_ref[...], ((1,), (0,))) + chosen_ref[...]
        highest = jnp.max(logits, axis=-1, keepdims=True)
        powers = jnp.exp(logits - highest)
        shares = powers / jnp.sum(powers, axis=-1, keepdims=True)
        high = shares.astype(BF16).astype(F32)
        payload[0, :, width:] = (high + pltpu.roll(shares - high, LOW, 1)).astype(BF16)
        payload_copies = [
            send(
                payload.at[0],
                payload.at[d],
                payload_sem.at[0, d - 1],
                payload_sem.at[1, d - 1],
                peers[d - 1],
            )
            for d in range(1, blocks)
        ]
        for copy in payload_copies:
            copy.start()
        back_copies = [
            send(sent.at[d - 1], back.at[d - 1], back_sem.at[0, d - 1], back_sem.at[1, d - 1], peers[d - 1])
            for d in range(1, blocks)
        ]
        for at, members in enumerate(groups_of_blocks):
            for d in members:
                if d:
                    payload_copies[d - 1].wait_recv()
            stacked = jnp.concatenate([payload[d] for d in members], axis=0)
            lanes = stacked[:, width:].astype(F32)
            pieces = []
            for e in range(local):
                if at == 0:
                    for copy in expert_copies[e]:
                        copy.wait()
                gate = dot(stacked[:, :width], gates_w[e], ((1,), (0,)))
                up = dot(stacked[:, :width], ups_w[e], ((1,), (0,)))
                share = jnp.sum(lanes * pick_ref[e], axis=-1, keepdims=True)
                pieces.append((gate / (1.0 + jnp.exp(-gate)) * up * share).astype(BF16))
            total = dot(jnp.concatenate(pieces, axis=1), downs_w[...], ((1,), (0,)))
            for place, d in enumerate(members):
                piece = total[place * rows : (place + 1) * rows]
                if d:
                    sent[d - 1] = piece.astype(BF16)
                    back_copies[d - 1].start()
                else:
                    own[...] = middle[...] + piece
        save(payload, payload_out)
        run_relays(relays, Relay.keep, sections)
        total = own[...]
        for d in range(1, blocks):
            back_copies[d - 1].wait_recv()
            total = total + back[d - 1].astype(F32)
        result[...] = total.astype(BF16)
        save(result, output_out)
        for d in range(1, blocks):
            payload_copies[d - 1].wait_send()
            back_copies[d - 1].wait_send()
        for copy in saves:
            copy.wait()

    run_relays(relays, Relay.forward, sections, outside=True)
    run_relays(relays, Relay.finish)


def forward_layer(
    sections,
    number,
    entry,
    gain_one,
    cosine,
    sine,
    bias,
    gain_two,
    router,
    chosen,
    pick,
    weights,
    tasks,
    arrays,
):
    inner, out, gate_all, up_all, down_all = weights
    rows, width = entry.shape
    blocks = inner.shape[0]
    members = lax.axis_size("dp")
    names, before, dests = relay_arrays(tasks, arrays)
    local, _, hidden = gate_all.shape
    keys = KVH * HD
    flops = 2 * rows * width * (H + 2 * KVH) * HD + 4 * rows * rows * blocks * H * HD
    flops += 2 * rows * H * HD * width + 6 * rows * blocks * local * width * hidden
    groups_of_blocks = [[0], list(range(1, blocks - 1)), [blocks - 1]]
    pair = (2, blocks - 1)
    anywhere = pl.BlockSpec(memory_space=pl.ANY)
    results = pl.pallas_call(
        functools.partial(
            forward_kernel, sections, tasks, names, len(before), groups_of_blocks
        ),
        in_specs=[whole()] * 9 + [anywhere] * (5 + len(before)),
        out_specs=[anywhere] * (8 + len(names)),
        out_shape=[
            shape((rows, width), BF16),
            shape((H * HD, rows), BF16),
            shape((blocks, 2, keys, rows), BF16),
            shape((H * HD, rows), BF16),
            shape((KVH, 1, GROUP * rows), F32),
            shape((rows, width), F32),
            shape((blocks, rows, width + LANES), BF16),
            shape((rows, width), BF16),
            *dests,
        ],
        scratch_shapes=[
            pltpu.VMEM(inner.shape, BF16),
            pltpu.VMEM(out.shape, BF16),
            pltpu.VMEM(gate_all.shape, BF16),
            pltpu.VMEM(up_all.shape, BF16),
            pltpu.VMEM((local * hidden, width), BF16),
            pltpu.VMEM((rows, width), BF16),
            pltpu.VMEM((H * HD, rows), BF16),
            pltpu.VMEM((blocks, 2, keys, rows), BF16),
            pltpu.VMEM((H * HD, rows), BF16),
            pltpu.VMEM((KVH, 1, GROUP * rows), F32),
            pltpu.VMEM((rows, width), F32),
            pltpu.VMEM((blocks, rows, width + LANES), BF16),
            pltpu.VMEM((blocks - 1, rows, width), BF16),
            pltpu.VMEM((blocks - 1, rows, width), BF16),
            pltpu.VMEM((rows, width), F32),
            pltpu.VMEM((rows, width), BF16),
            pltpu.SemaphoreType.DMA((blocks,)),
            pltpu.SemaphoreType.DMA(()),
            pltpu.SemaphoreType.DMA((local, 3)),
            pltpu.SemaphoreType.DMA(pair),
            pltpu.SemaphoreType.DMA(pair),
            pltpu.SemaphoreType.DMA(pair),
            pltpu.SemaphoreType.DMA((8,)),
        ]
        + relay_sems(blocks, members) * len(tasks),
        input_output_aliases={14 + i: 8 + i for i in range(len(before))},
        compiler_params=pltpu.CompilerParams(
            vmem_limit_bytes=VMEM, collective_id=number, has_side_effects=True
        ),
        cost_estimate=cost(flops, 3e7),
        name="forward_layer",
    )(
        entry,
        gain_one,
        cosine,
        sine,
        bias,
        gain_two,
        router,
        chosen,
        pick,
        inner,
        out,
        gate_all,
        up_all,
        down_all,
        *before,
    )
    return results[:8], dict(zip(names, results[8:]))


def activation(gate, up, hidden_grad):
    sigmoid = 1.0 / (1.0 + jnp.exp(-gate))
    silu = gate * sigmoid
    slope = sigmoid * (1.0 + gate * (1.0 - sigmoid))
    return silu * up, hidden_grad * up * slope, hidden_grad * silu


def norm_back(values, gain, grad):
    width = values.shape[1]
    scale = lax.rsqrt(jnp.mean(values * values, axis=-1, keepdims=True) + EPS)
    scaled = grad * gain
    inner = jnp.sum(values * scaled, axis=-1, keepdims=True) * (1.0 / width)
    part = scale * scaled - values * (scale * scale * scale * inner)
    return part, jnp.sum(grad * values * scale, axis=0, keepdims=True)


HELD = 7


def backward_kernel(sections, holders, tasks, names, before, groups_of_blocks, *refs):
    refs = list(refs)

    def take(count):
        taken = refs[:count]
        del refs[:count]
        return taken

    g_ref, gain_one_ref, gain_two_ref, router_ref, cos_ref, sin_ref, pick_ref, mark_ref = take(8)
    inner_hbm, out_hbm, gate_hbm, up_hbm, down_hbm = take(5)
    sets = [take(HELD) for _ in holders]
    take(before)
    outputs = take(7)
    dests = take(len(names))
    gates_w, ups_w, downs_w, out, inner = take(5)
    held = take(HELD)
    entry, bias_v, query, kv, lse, middle, payload = held
    grads, gate_v, up_v, own, sent, back = take(6)
    branch, logit, middle_grad, datt = take(4)
    own_kv, sent_kv, back_kv, turned, entry_grad, entry_low, gain_one_v, gain_two_v = take(8)
    expert_sem, out_sem, inner_sem, held_sem, grads_sem, back_sem, kv_sem, save_sem = take(8)
    relays = make_relays(tasks, grads, names, dests, take)
    grad_relays = [relay for relay in relays if relay.keeps]

    blocks, rows, width = grads.shape
    local, _, hidden_width = gates_w.shape
    keys = kv.shape[2]
    part = width // blocks
    queries = H * HD // blocks
    own_keys = keys // blocks

    enter(sections, relays, blocks)
    run_relays(relays, Relay.open)

    @in_sections(sections)
    def _():
        peers = plane_peers(blocks)
        expert_copies = []
        for e in range(local):
            band = pl.ds(e * hidden_width, hidden_width)
            expert_copies.append(
                (
                    pltpu.make_async_copy(gate_hbm.at[e], gates_w.at[e], expert_sem.at[e, 0]),
                    pltpu.make_async_copy(up_hbm.at[e], ups_w.at[e], expert_sem.at[e, 1]),
                    pltpu.make_async_copy(down_hbm.at[e], downs_w.at[band], expert_sem.at[e, 2]),
                )
            )
        out_copy = pltpu.make_async_copy(out_hbm, out, out_sem)
        inner_copy = pltpu.make_async_copy(inner_hbm, inner, inner_sem)
        grads[0] = g_ref[...]
        grads_copies = [
            send(
                grads.at[0],
                grads.at[d],
                grads_sem.at[0, d - 1],
                grads_sem.at[1, d - 1],
                peers[d - 1],
            )
            for d in range(1, blocks)
        ]
        for copy in grads_copies:
            copy.start()

        def fetch(at, index):
            return pltpu.make_async_copy(sets[at][index], held[index], held_sem.at[index])

        order = (HELD - 1,) + tuple(range(HELD - 1))
        for at, section in enumerate(holders):

            @in_section(section)
            def _(at=at):
                fetch(at, HELD - 1).start()

        for copy in expert_copies[0]:
            copy.start()
        for at, section in enumerate(holders):

            @in_section(section)
            def _(at=at):
                for index in order[1:]:
                    fetch(at, index).start()

        for copies in expert_copies[1:]:
            for copy in copies:
                copy.start()
        out_copy.start()
        inner_copy.start()
        run_relays(grad_relays, lambda relay: relay.start(0))

        saves = []

        def save(source, target):
            copy = pltpu.make_async_copy(source, target, save_sem.at[len(saves)])
            copy.start()
            saves.append(copy)

        fetch(0, HELD - 1).wait()
        stacked = payload[...].reshape(blocks * rows, width + LANES)
        for e in range(local):
            for copy in expert_copies[e]:
                copy.wait()
            gate_v[e] = dot(stacked[:, :width], gates_w[e], ((1,), (0,)))
            up_v[e] = dot(stacked[:, :width], ups_w[e], ((1,), (0,)))
        back_copies = [
            send(
                sent.at[d - 1],
                back.at[d - 1],
                back_sem.at[0, d - 1],
                back_sem.at[1, d - 1],
                peers[d - 1],
            )
            for d in range(1, blocks)
        ]
        for members in groups_of_blocks:
            for d in members:
                if d:
                    grads_copies[d - 1].wait_recv()
            if blocks - 1 in members:
                run_relays(grad_relays, lambda relay: relay.start(1))
                run_relays(grad_relays, Relay.keep)

            held_rows = slice(members[0] * rows, (members[-1] + 1) * rows)
            grad = jnp.concatenate([grads[d] for d in members], axis=0)
            lanes = jnp.concatenate([payload[d, :, width:] for d in members], axis=0).astype(F32)
            hidden_grad = dot(grad, downs_w[...], ((1,), (1,)))
            total = jnp.zeros((rows * len(members), width), F32)
            share = jnp.zeros((rows * len(members), LANES), F32)
            for e in range(local):
                columns = slice(e * hidden_width, (e + 1) * hidden_width)
                raw = hidden_grad[:, columns]
                hidden, gate_part, up_part = activation(gate_v[e, held_rows], up_v[e, held_rows], raw)
                hidden = hidden.astype(BF16).astype(F32)
                share = share + jnp.sum(hidden * raw, axis=-1, keepdims=True) * mark_ref[e]
                weight = jnp.sum(lanes * pick_ref[e], axis=-1, keepdims=True)
                total = total + dot((gate_part * weight).astype(BF16), gates_w[e], ((1,), (1,)))
                total = total + dot((up_part * weight).astype(BF16), ups_w[e], ((1,), (1,)))
            high = share.astype(BF16).astype(F32)
            both = high + pltpu.roll(share - high, LOW, 1)
            for place, d in enumerate(members):
                band = slice(place * rows, (place + 1) * rows)
                if d:
                    sent[d - 1, :, :width] = total[band].astype(BF16)
                    sent[d - 1, :, width:] = both[band].astype(BF16)
                    back_copies[d - 1].start()
                else:
                    own[:, :width] = total[band]
                    own[:, width:] = share[band]
        for at, section in enumerate(holders):
            if at == 0:
                for index in order[1:]:
                    fetch(0, index).wait()

        total = own[:, :width]
        share = own[:, width:]
        for d in range(1, blocks):
            back_copies[d - 1].wait_recv()
            total = total + back[d - 1, :, :width].astype(F32)
            share = share + back[d - 1, :, width:].astype(F32)
        run_relays(relays, Relay.forward, sections)
        first = lax.broadcasted_iota(jnp.int32, (1, LANES), 1) < LOW
        shares = payload[0, :, width:].astype(F32)
        shares = jnp.where(first, shares + pltpu.roll(shares, LOW, 1), 0.0)
        share = jnp.where(first, share + pltpu.roll(share, LOW, 1), 0.0)
        weighted = shares * share
        logit_grad = (weighted - shares * jnp.sum(weighted, axis=-1, keepdims=True)).astype(BF16)
        logit[...] = logit_grad
        total = total + dot(logit_grad, router_ref[...], ((1,), (1,)))
        piece, gain_two_v[...] = norm_back(middle[...], gain_two_ref[...], total)
        middle_grad[...] = g_ref[...].astype(F32) + piece
        branch[...] = middle_grad[...].astype(BF16)
        save(logit, outputs[4])
        save(branch, outputs[3])
        save(gain_two_v, outputs[6])
        out_copy.wait()
        total = jnp.zeros(datt.shape, F32)
        for e in range(blocks):
            total = total + dot(out[e], branch[:, e * part : (e + 1) * part], ((1,), (1,)))
        datt[...] = total.astype(BF16)

        bias = jnp.concatenate([bias_v[...]] * GROUP, axis=1)
        cosine = cos_ref[...]
        sine = sin_ref[...]
        per_block = queries // (GROUP * HD)

        def one(group, carry):
            query_group = group_of(query, group)
            key_group = keys_of(kv, 0, group)
            grad_group = group_of(datt, group)
            scores = dot(key_group, query_group, ((0,), (0,))) * SCALE + bias
            probabilities = jnp.exp(scores - lse[group])
            probability_grad = dot(keys_of(kv, 1, group), grad_group, ((0,), (0,)))
            centre = jnp.sum(probabilities * probability_grad, axis=0, keepdims=True)
            score_grad = (probabilities * (probability_grad - centre)).astype(BF16)
            query_part = dot(key_group, score_grad, ((1,), (0,))) * SCALE
            e = lax.div(group, per_block)
            base = lax.rem(group, per_block) * (GROUP * HD)
            for head in range(GROUP):
                start = pl.multiple_of(base + head * HD, HALF)
                leading = query_part[:HALF, head * rows : (head + 1) * rows]
                trailing = query_part[HALF:, head * rows : (head + 1) * rows]
                turned[e, pl.ds(start, HALF), :] = (leading * cosine + trailing * sine).astype(BF16)
                turned[e, pl.ds(start + HALF, HALF), :] = (
                    trailing * cosine - leading * sine
                ).astype(BF16)
            key_part = dot(query_group, score_grad, ((1,), (1,))) * SCALE
            value_part = dot(grad_group, probabilities.astype(BF16), ((1,), (1,)))
            base = pl.multiple_of(group * HD, HD)
            for which, piece in ((0, key_part), (1, value_part)):
                own_kv[which, pl.ds(base, HD), :] = piece[:, :rows]
                for d in range(1, blocks):
                    sent_kv[d - 1, which, pl.ds(base, HD), :] = piece[
                        :, d * rows : (d + 1) * rows
                    ].astype(BF16)
            return carry

        heads = keys // HD
        kv_copies = []
        for half in range(2):
            lax.fori_loop(half * heads // 2, (half + 1) * heads // 2, one, 0)
            band = pl.ds(half * keys // 2, keys // 2)
            for d in range(1, blocks):
                copy = send(
                    sent_kv.at[d - 1, :, band],
                    back_kv.at[d - 1, :, band],
                    kv_sem.at[0, half, d - 1],
                    kv_sem.at[1, half, d - 1],
                    peers[d - 1],
                )
                copy.start()
                kv_copies.append(copy)

        inner_copy.wait()
        total = jnp.zeros((rows, width), F32)
        for e in range(blocks):
            total = total + dot(turned[e, :queries], inner[e, :, :queries], ((0,), (1,)))
        for copy in kv_copies:
            copy.wait_recv()
        pair = own_kv[...]
        for d in range(1, blocks):
            pair = pair + back_kv[d - 1].astype(F32)
        for e in range(blocks):
            band = slice(e * own_keys, (e + 1) * own_keys)
            turn_heads(pair[0, band], cosine, sine, turned.at[e], queries, own_keys, -1.0)
            turned[e, queries + own_keys :] = pair[1, band].astype(BF16)
        save(turned, outputs[2])
        for e in range(blocks):
            total = total + dot(turned[e, queries:], inner[e, :, queries:], ((0,), (1,)))
        piece, gain_one_v[...] = norm_back(entry[...].astype(F32), gain_one_ref[...], total)
        result = middle_grad[...] + piece
        entry_grad[...] = result
        entry_low[...] = result.astype(BF16)
        save(entry_low, outputs[1])
        save(entry_grad, outputs[0])
        save(gain_one_v, outputs[5])
        for d in range(1, blocks):
            grads_copies[d - 1].wait_send()
            back_copies[d - 1].wait_send()
        for copy in kv_copies:
            copy.wait_send()
        for copy in saves:
            copy.wait()

    run_relays(relays, Relay.forward, sections, outside=True)
    run_relays(relays, Relay.finish)


def backward_layer(
    sections,
    number,
    grad,
    sets,
    gain_one,
    gain_two,
    router,
    cosine,
    sine,
    pick,
    mark,
    weights,
    tasks,
    arrays,
):
    names, before, dests = relay_arrays(tasks, arrays)
    inner, out, gate_all, up_all, down_all = weights
    rows, width = grad.shape
    blocks = inner.shape[0]
    members = lax.axis_size("dp")
    local, _, hidden = gate_all.shape
    keys = KVH * HD
    length = rows * blocks
    flops = 4 * rows * width * (H + 2 * KVH) * HD + 10 * rows * length * H * HD
    flops += 2 * rows * H * HD * width + 10 * length * local * width * hidden
    groups_of_blocks = [[0], list(range(1, blocks - 1)), [blocks - 1]]
    pair = (2, blocks - 1)
    anywhere = pl.BlockSpec(memory_space=pl.ANY)
    first_before = 13 + HELD * len(sets)
    held = sets[0][1]
    results = pl.pallas_call(
        functools.partial(
            backward_kernel,
            sections,
            [section for section, _ in sets],
            tasks,
            names,
            len(before),
            groups_of_blocks,
        ),
        in_specs=[whole()] * 8
        + [anywhere] * (5 + HELD * len(sets) + len(before)),
        out_specs=[anywhere] * (7 + len(names)),
        out_shape=[
            shape((rows, width), F32),
            shape((rows, width), BF16),
            shape((blocks, inner.shape[2], rows), BF16),
            shape((rows, width), BF16),
            shape((rows, LANES), BF16),
            shape((1, width), F32),
            shape((1, width), F32),
            *dests,
        ],
        scratch_shapes=[
            pltpu.VMEM(gate_all.shape, BF16),
            pltpu.VMEM(up_all.shape, BF16),
            pltpu.VMEM((local * hidden, width), BF16),
            pltpu.VMEM(out.shape, BF16),
            pltpu.VMEM(inner.shape, BF16),
        ]
        + [pltpu.VMEM(array.shape, array.dtype) for array in held]
        + [
            pltpu.VMEM((blocks, rows, width), BF16),
            pltpu.VMEM((local, length, hidden), F32),
            pltpu.VMEM((local, length, hidden), F32),
            pltpu.VMEM((rows, width + LANES), F32),
            pltpu.VMEM((blocks - 1, rows, width + LANES), BF16),
            pltpu.VMEM((blocks - 1, rows, width + LANES), BF16),
            pltpu.VMEM((rows, width), BF16),
            pltpu.VMEM((rows, LANES), BF16),
            pltpu.VMEM((rows, width), F32),
            pltpu.VMEM((H * HD, rows), BF16),
            pltpu.VMEM((2, keys, rows), F32),
            pltpu.VMEM((blocks - 1, 2, keys, rows), BF16),
            pltpu.VMEM((blocks - 1, 2, keys, rows), BF16),
            pltpu.VMEM((blocks, inner.shape[2], rows), BF16),
            pltpu.VMEM((rows, width), F32),
            pltpu.VMEM((rows, width), BF16),
            pltpu.VMEM((1, width), F32),
            pltpu.VMEM((1, width), F32),
            pltpu.SemaphoreType.DMA((local, 3)),
            pltpu.SemaphoreType.DMA(()),
            pltpu.SemaphoreType.DMA(()),
            pltpu.SemaphoreType.DMA((HELD,)),
            pltpu.SemaphoreType.DMA(pair),
            pltpu.SemaphoreType.DMA(pair),
            pltpu.SemaphoreType.DMA((2, 2, blocks - 1)),
            pltpu.SemaphoreType.DMA((7,)),
        ]
        + relay_sems(blocks, members) * len(tasks),
        input_output_aliases={first_before + i: 7 + i for i in range(len(before))},
        compiler_params=pltpu.CompilerParams(
            vmem_limit_bytes=VMEM, collective_id=number, has_side_effects=True
        ),
        cost_estimate=cost(flops, 4e7),
        name="backward_layer",
    )(
        grad,
        gain_one,
        gain_two,
        router,
        cosine,
        sine,
        pick,
        mark,
        inner,
        out,
        gate_all,
        up_all,
        down_all,
        *[array for _, held_arrays in sets for array in held_arrays],
        *before,
    )
    return results[:7], dict(zip(names, results[7:]))


def prepare_kernel(tile, batches, *refs):
    tokens, (pick, gate_w, up_w, *outputs) = refs[:batches], refs[batches:]
    local, width, hidden_width = gate_w.shape
    count = tokens[0].shape[0] // tile

    def body(x_ref, pick_ref, gate_ref, up_ref, hidden_ref, gate_factor_ref, up_factor_ref):
        entry = x_ref[:, :width]
        weight = jnp.sum(x_ref[:, width:].astype(F32) * pick_ref[0], axis=-1, keepdims=True)
        gate = dot(entry, gate_ref[0], ((1,), (0,)))
        up = dot(entry, up_ref[0], ((1,), (0,)))
        held, gate_part, up_part = activation(gate, up, weight)
        hidden_ref[...] = (held * weight).astype(BF16)
        gate_factor_ref[...] = gate_part.astype(BF16)
        up_factor_ref[...] = up_part.astype(BF16)

    @in_section(0)
    def _():
        weight = pl.BlockSpec((1, width, hidden_width), lambda t, e: (e, 0, 0))
        for batch, x_hbm in enumerate(tokens):
            piece = pl.BlockSpec((tile, hidden_width), lambda t, e: (batch * count + t, e))
            pltpu.emit_pipeline(
                body,
                grid=(count, local),
                in_specs=[
                    pl.BlockSpec((tile, width + LANES), lambda t, e: (t, 0)),
                    pl.BlockSpec((1, 1, LANES), lambda t, e: (e, 0, 0)),
                    weight,
                    weight,
                ],
                out_specs=[piece] * 3,
            )(x_hbm, pick, gate_w, up_w, *outputs)


def prepare(tokens, pick, gate_all, up_all, tile=512):
    local, width, hidden = gate_all.shape
    rows = sum(block.shape[0] for block in tokens)
    anywhere = pl.BlockSpec(memory_space=pl.ANY)
    return pl.pallas_call(
        functools.partial(prepare_kernel, min(tile, tokens[0].shape[0]), len(tokens)),
        in_specs=[anywhere] * (3 + len(tokens)),
        out_specs=[anywhere] * 3,
        out_shape=[shape((rows, local * hidden), BF16)] * 3,
        compiler_params=params(),
        cost_estimate=cost(4 * rows * local * width * hidden, rows * width * 8),
        name="prepare",
    )(*tokens, pick, gate_all, up_all)


def weights_step(ready, x_ref, g_ref, down_ref, held, outs):
    width = g_ref.shape[1]
    entry = x_ref[:, :width]
    grad = g_ref[...]
    hidden_grad = dot(grad, down_ref[0], ((1,), (1,)))
    if ready:
        hidden = held[0][...]
        gate_part = hidden_grad * held[1][...].astype(F32)
        up_part = hidden_grad * held[2][...].astype(F32)
    else:
        pick_ref, gate_ref, up_ref = held[-3:]
        weight = jnp.sum(x_ref[:, width:].astype(F32) * pick_ref[0], axis=-1, keepdims=True)
        gate = dot(entry, gate_ref[0], ((1,), (0,)))
        up = dot(entry, up_ref[0], ((1,), (0,)))
        hidden, gate_part, up_part = activation(gate, up, hidden_grad * weight)
        hidden = (hidden * weight).astype(BF16)
    dgate_ref, dup_ref, ddown_ref = outs
    dgate_ref[0] += dot(entry, gate_part.astype(BF16), ((0,), (0,)))
    dup_ref[0] += dot(entry, up_part.astype(BF16), ((0,), (0,)))
    ddown_ref[0] += dot(hidden, grad, ((0,), (0,)))


def weights_specs(ready, first, tile, expert, shapes):
    width, hidden = shapes
    columns = pl.BlockSpec((1, width, hidden), lambda e, t: (expert(e), 0, 0))
    bands = pl.BlockSpec((1, hidden, width), lambda e, t: (expert(e), 0, 0))
    piece = pl.BlockSpec((tile, hidden), lambda e, t: (first + t, expert(e)))
    specs = [
        pl.BlockSpec((tile, width + LANES), lambda e, t: (t, 0)),
        pl.BlockSpec((tile, width), lambda e, t: (t, 0)),
        bands,
    ]
    if ready:
        specs += [piece] * 3
    specs += [pl.BlockSpec((1, 1, LANES), lambda e, t: (expert(e), 0, 0)), columns, columns]
    return specs, [columns, columns, bands]


def weights_both(ready, x_ref, g_ref, down_ref, held, outs):
    if not ready:
        weights_step(False, x_ref, g_ref, down_ref, held, outs)
        return
    for section in range(2):

        @in_section(section)
        def _(section=section):
            weights_step(section == 0, x_ref, g_ref, down_ref, held, outs)


def first_weights_kernel(ready, tasks, names, *refs):
    refs = list(refs)

    def take(count):
        taken = refs[:count]
        del refs[:count]
        return taken

    x_ref, g_ref, down_ref, *held = take(9 if ready else 6)
    take(len(names))
    outs = take(3)
    dests = take(len(names))
    relays = make_relays(tasks, None, names, dests, take)
    step = pl.program_id(0) * pl.num_programs(1) + pl.program_id(1)

    early = [relay for relay in relays if relay.section == 0]
    late = [relay for relay in relays if relay.section != 0]

    @pl.when(step == 0)
    def _():
        enter([], early, dests[0].shape[2])
        run_relays(early, Relay.forward)

    @pl.when(pl.program_id(1) == 0)
    def _():
        for out in outs:
            out[...] = jnp.zeros_like(out)

    @pl.when(step == pl.num_programs(0) * pl.num_programs(1) - 1)
    def _():
        enter([], late, dests[0].shape[2])
        run_relays(late, Relay.forward)

    weights_both(ready, x_ref, g_ref, down_ref, held, outs)

    @pl.when(step == pl.num_programs(0) * pl.num_programs(1) - 1)
    def _():
        run_relays(relays, Relay.finish)


def first_weights(number, tasks, arrays, experts, tokens, grads, down_all, prepared, forward, tile=512):
    local, hidden, width = down_all.shape
    names, before, dests = relay_arrays(tasks, arrays)
    _, members, blocks, _, _ = dests[0].shape
    rows = grads.shape[0]
    tile = min(tile, rows)
    ready = prepared is not None
    specs, outs = weights_specs(ready, 0, tile, lambda e: e, (width, hidden))
    anywhere = pl.BlockSpec(memory_space=pl.ANY)
    results = pl.pallas_call(
        functools.partial(first_weights_kernel, ready, tasks, names),
        grid=(experts, rows // tile),
        in_specs=specs + [anywhere] * len(names),
        out_specs=outs + [anywhere] * len(names),
        out_shape=[
            shape((local, width, hidden), F32),
            shape((local, width, hidden), F32),
            shape((local, hidden, width), F32),
            *dests,
        ],
        scratch_shapes=relay_sems(blocks, members) * len(tasks),
        input_output_aliases={len(specs) + i: 3 + i for i in range(len(names))},
        compiler_params=pltpu.CompilerParams(
            vmem_limit_bytes=VMEM,
            collective_id=number,
            has_side_effects=True,
            dimension_semantics=("arbitrary", "arbitrary"),
        ),
        cost_estimate=cost(
            8 * rows * width * hidden * experts, rows * (4 * width + 6 * hidden) * experts
        ),
        name="first_weights",
    )(tokens, grads, down_all, *(prepared if ready else ()), *forward, *before)
    return results[:3], dict(zip(names, results[3:]))


def whole_weights_kernel(ready, batches, *refs):
    x_refs, refs = refs[:batches], refs[batches:]
    g_refs, (down_ref, *rest) = refs[:batches], refs[batches:]
    held = rest[: 6 if ready else 3]
    outs = rest[-3:]
    tiles = pl.num_programs(0) // batches

    @pl.when(pl.program_id(0) == 0)
    def _():
        for out in outs:
            out[...] = jnp.zeros_like(out)

    for batch in range(batches):

        @pl.when(pl.program_id(0) // tiles == batch)
        def _(batch=batch):
            weights_both(ready, x_refs[batch], g_refs[batch], down_ref, held, outs)


def whole_weights(expert, tokens, grads, down_all, prepared, forward, chain=None, tile=512):
    local, hidden, width = down_all.shape
    batches = len(tokens)
    rows = grads[0].shape[0]
    tile = min(tile, rows)
    tiles = rows // tile
    ready = prepared is not None
    chained = chain is not None

    def band(batch, lanes):
        return pl.BlockSpec((tile, lanes), lambda t: (jnp.clip(t - batch * tiles, 0, tiles - 1), 0))

    columns = pl.BlockSpec((1, width, hidden), lambda t: (expert, 0, 0))
    bands = pl.BlockSpec((1, hidden, width), lambda t: (expert, 0, 0))
    specs = [band(batch, width + LANES) for batch in range(batches)]
    specs += [band(batch, width) for batch in range(batches)] + [bands]
    if ready:
        specs += [pl.BlockSpec((tile, hidden), lambda t: (t, expert))] * 3
    specs += [pl.BlockSpec((1, 1, LANES), lambda t: (expert, 0, 0)), columns, columns]
    return pl.pallas_call(
        functools.partial(whole_weights_kernel, ready, batches),
        grid=(batches * tiles,),
        in_specs=specs + [pl.BlockSpec(memory_space=pl.ANY)] * (3 if chained else 0),
        out_specs=[columns, columns, bands],
        out_shape=[
            shape((local, width, hidden), F32),
            shape((local, width, hidden), F32),
            shape((local, hidden, width), F32),
        ],
        input_output_aliases={len(specs) + i: i for i in range(3)} if chained else {},
        compiler_params=pltpu.CompilerParams(
            vmem_limit_bytes=LARGE, dimension_semantics=("arbitrary",)
        ),
        cost_estimate=cost(
            8 * rows * batches * width * hidden, rows * batches * (4 * width + 6 * hidden)
        ),
        name="whole_weights",
    )(
        *tokens,
        *grads,
        down_all,
        *(prepared if ready else ()),
        *forward,
        *(chain if chained else ()),
    )


def last_weights_kernel(ready, chained, *refs):
    x_ref, g_ref, down_ref, *rest = refs
    count = 6 if ready else 3
    held, before = rest[:count], rest[count : count + 3]
    outs = rest[count + 6 :] if chained else rest[count + 3 :]

    @pl.when(pl.program_id(1) == 0)
    def _():
        for out, source in zip(outs, before):
            out[...] = source[...]

    weights_both(ready, x_ref, g_ref, down_ref, held, outs)


def last_weights(experts, tokens, grads, down_all, prepared, forward, before, chain=None, tile=512):
    in_place = chain is before
    if in_place:
        chain = None
    local, hidden, width = down_all.shape
    rows = grads.shape[0]
    tile = min(tile, rows)
    chained = chain is not None
    ready = prepared is not None
    first = (prepared[0].shape[0] - rows) // tile if ready else 0
    specs, outs = weights_specs(ready, first, tile, lambda e: experts[0] + e, (width, hidden))
    held = [
        pl.BlockSpec(spec.block_shape, spec.index_map, pipeline_mode=pl.Buffered(1)) for spec in outs
    ]
    count = len(specs)
    anywhere = pl.BlockSpec(memory_space=pl.ANY)
    return pl.pallas_call(
        functools.partial(last_weights_kernel, ready, chained),
        grid=(experts[1] - experts[0], rows // tile),
        in_specs=specs + held + [anywhere] * (3 if chained else 0),
        out_specs=outs,
        out_shape=[
            shape((local, width, hidden), F32),
            shape((local, width, hidden), F32),
            shape((local, hidden, width), F32),
        ],
        input_output_aliases={count + (3 if chained else 0) + i: i for i in range(3)}
        if chained or in_place
        else {},
        compiler_params=pltpu.CompilerParams(
            vmem_limit_bytes=LARGE, dimension_semantics=("arbitrary", "arbitrary")
        ),
        cost_estimate=cost(
            8 * rows * width * hidden * (experts[1] - experts[0]), rows * (4 * width + 6 * hidden)
        ),
        name="last_weights",
    )(
        tokens,
        grads,
        down_all,
        *(prepared if ready else ()),
        *forward,
        *before,
        *(chain if chained else ()),
    )


def attention_weights_kernel(section, batches, blocks, members, by_rows, *refs):
    sets = [refs[8 * m : 8 * m + 8] for m in range(batches)]
    refs = refs[8 * batches :]
    count = members if by_rows else blocks
    outputs = refs[:count]
    small_out = refs[count]
    held = refs[count + 1 : count + 1 + blocks]
    normed, turned, attended, branch, mixed, logit, gains, small, sems, save_sems = refs[
        count + 1 + blocks :
    ]
    place = lax.axis_index("dp")
    depth = held[0].shape[0] // members
    rows = normed.shape[0] // batches
    me = lax.axis_index("expert")
    part = branch.shape[1] // blocks
    columns = turned.shape[1]

    @in_section(section)
    def _():
        copies = []
        for m in range(batches):
            band = pl.ds(m * rows, rows)
            targets = (
                normed.at[band],
                turned.at[:, :, band],
                attended.at[:, band],
                branch.at[band],
                mixed.at[band],
                logit.at[band],
                gains.at[m, 0],
                gains.at[m, 1],
            )
            for i, (source, target) in enumerate(zip(sets[m], targets)):
                copies.append(pltpu.make_async_copy(source, target, sems.at[m, i]))
        for copy in copies:
            copy.start()
        for copy in copies:
            copy.wait()
        router = dot(logit[...], mixed[:, : normed.shape[1]], ((0,), (0,)))
        small[...] = router[: small.shape[0]]
        for i in range(2):
            total = gains[0, i]
            for m in range(1, batches):
                total = total + gains[m, i]
            small[pl.ds(small.shape[0] - 2 + i, 1), :] = total
        saves = [pltpu.make_async_copy(small, small_out, save_sems.at[blocks, 0])]
        saves[0].start()
        for d in [*range(1, blocks), 0]:
            e = partner(me, d)
            at = pl.multiple_of(e * part, LANES)
            held[d][:, :columns] = dot(normed[...], turned[e], ((0,), (1,))).astype(BF16)
            held[d][:, columns:] = dot(
                attended[...], branch[:, pl.ds(at, part)], ((1,), (0,))
            ).astype(BF16)
            if not by_rows:
                saves.append(pltpu.make_async_copy(held[d], outputs[d], save_sems.at[d, 0]))
                saves[-1].start()
                continue
            for k in range(members):
                at = pl.multiple_of(lax.rem(place + k, members) * depth, depth)
                save = pltpu.make_async_copy(
                    held[d].at[pl.ds(at, depth)],
                    outputs[k].at[pl.ds(d * depth, depth)],
                    save_sems.at[d, k],
                )
                save.start()
                saves.append(save)
        for save in saves:
            save.wait()


def attention_weights(section, sets, by_rows):
    members = lax.axis_size("dp")
    batches = len(sets)
    normed, turned, attended, branch, mixed, logit, _, _ = sets[0]
    blocks, columns, rows = turned.shape
    width = branch.shape[1]
    wide = columns + width // blocks
    flat = [array for one in sets for array in one]
    anywhere = pl.BlockSpec(memory_space=pl.ANY)
    return pl.pallas_call(
        functools.partial(
            attention_weights_kernel, section, batches, blocks, members, by_rows
        ),
        in_specs=[anywhere] * len(flat),
        out_specs=[anywhere] * (1 + (members if by_rows else blocks)),
        out_shape=(
            [shape((width * blocks // members, wide), BF16)] * members
            if by_rows
            else [shape((width, wide), BF16)] * blocks
        )
        + [shape((SMALL, width), F32)],
        scratch_shapes=[pltpu.VMEM((width, wide), BF16)] * blocks
        + [
            pltpu.VMEM((batches * rows, width), BF16),
            pltpu.VMEM((blocks, columns, batches * rows), BF16),
            pltpu.VMEM((attended.shape[0], batches * rows), BF16),
            pltpu.VMEM((batches * rows, width), BF16),
            pltpu.VMEM((batches * rows, mixed.shape[1]), BF16),
            pltpu.VMEM((batches * rows, logit.shape[1]), BF16),
            pltpu.VMEM((batches, 2, 1, width), F32),
            pltpu.VMEM((SMALL, width), F32),
            pltpu.SemaphoreType.DMA((batches, 8)),
            pltpu.SemaphoreType.DMA((blocks + 1, members)),
        ],
        compiler_params=params(),
        cost_estimate=cost(2 * batches * rows * width * wide * blocks, 2e7),
        name="attention_weights",
    )(*flat)


def sum_kernel(counts, depth, *refs):
    output = refs[-1]
    wide = output.shape[1]
    tile = depth // 2
    at = 0
    for section, (terms, bands) in enumerate(counts):

        def body(*tiles, terms=terms):
            total = tiles[0][...].astype(F32)
            for piece in tiles[1:terms]:
                total = total + piece[...].astype(F32)
            tiles[terms][...] = total.astype(BF16)

        @in_section(section)
        def _(at=at, terms=terms, bands=bands, section=section, body=body):
            first = 2 * lax.axis_index("dp") if section == 0 else 0
            pltpu.emit_pipeline(
                body,
                grid=(2 * bands,),
                in_specs=[
                    pl.BlockSpec((tile, wide), lambda i: (lax.rem(first + i, 2 * bands), 0))
                ]
                * terms,
                out_specs=[pl.BlockSpec((tile, wide), lambda i: (i, 0))],
            )(*refs[at : at + terms], output)

        at += terms


def sum_blocks(upper, lower, depth):
    wide = upper[0].shape[1]
    rows = max(upper[0].shape[0], lower[0].shape[0])
    counts = [(len(terms), terms[0].shape[0] // depth) for terms in (upper, lower)]
    anywhere = pl.BlockSpec(memory_space=pl.ANY)
    total = pl.pallas_call(
        functools.partial(sum_kernel, counts, depth),
        in_specs=[anywhere] * (len(upper) + len(lower)),
        out_specs=anywhere,
        out_shape=shape((rows, wide), BF16),
        compiler_params=params(),
        cost_estimate=cost(0, rows * wide * 2 * (len(upper) + 1)),
        name="sum_blocks",
    )(*upper, *lower)
    return jnp.split(total, rows // depth, axis=0)


def small_kernel(upper, lower, total, own, sent, plane, line, fetch_sem, plane_sem, line_sem):
    blocks = plane.shape[0] + 1
    members = line.shape[0] + 1
    for section, source in ((0, upper), (1, lower)):

        @in_section(section)
        def _(source=source):
            fetch = pltpu.make_async_copy(source, own, fetch_sem)
            fetch.start()
            fetch.wait()

    greet(plane_peers(blocks) + line_peers(members))
    for peers, room, sems in (
        (plane_peers(blocks), plane, plane_sem),
        (line_peers(members), line, line_sem),
    ):
        sent[...] = own[...].astype(BF16)
        copies = [
            send(sent, room.at[i], sems.at[0, i], sems.at[1, i], peer) for i, peer in enumerate(peers)
        ]
        for copy in copies:
            copy.start()
        for copy in copies:
            copy.wait()
        held = own[...]
        for i in range(len(peers)):
            held = held + room[i].astype(F32)
        own[...] = held
    total[...] = own[...]


def sum_small(number, upper, lower):
    blocks = lax.axis_size("expert")
    members = lax.axis_size("dp")
    return pl.pallas_call(
        small_kernel,
        in_specs=[pl.BlockSpec(memory_space=pl.ANY)] * 2,
        out_specs=whole(),
        out_shape=shape(upper.shape, F32),
        scratch_shapes=[
            pltpu.VMEM(upper.shape, F32),
            pltpu.VMEM(upper.shape, BF16),
            pltpu.VMEM((blocks - 1,) + upper.shape, BF16),
            pltpu.VMEM((members - 1,) + upper.shape, BF16),
            pltpu.SemaphoreType.DMA(()),
            pltpu.SemaphoreType.DMA((2, blocks - 1)),
            pltpu.SemaphoreType.DMA((2, members - 1)),
        ],
        compiler_params=pltpu.CompilerParams(
            vmem_limit_bytes=VMEM, collective_id=number, has_side_effects=True
        ),
        name="sum_small",
    )(upper, lower)


def assemble_kernel(blocks, *refs):
    outputs = refs[blocks:]
    me = lax.axis_index("expert")
    for d in range(blocks):
        e = partner(me, d)
        at = 0
        for out in outputs:
            part = out.shape[1] // blocks
            start = pl.multiple_of(e * part, LANES)
            out[:, pl.ds(start, part)] = refs[d][:, at : at + part].astype(F32)
            at += part


def assemble(shards, widths):
    rows = shards[0].shape[0]
    return pl.pallas_call(
        functools.partial(assemble_kernel, len(shards)),
        in_specs=[whole()] * len(shards),
        out_specs=[whole()] * len(widths),
        out_shape=[shape((rows, columns), F32) for columns in widths],
        compiler_params=params(),
        cost_estimate=cost(0, rows * sum(widths) * 6),
        name="assemble",
    )(*shards)


def pad_lanes(block):
    return jnp.pad(block, ((0, 0), (0, LANES - block.shape[1])))


def swap(block, distance, sections):
    count = lax.axis_size("expert")
    route = [
        (section * count + i, section * count + (i ^ distance))
        for section in sections
        for i in range(count)
    ]
    return lax.ppermute(block, ("section", "expert"), route)


def total_of(blocks):
    return functools.reduce(jnp.add, [block.astype(F32) for block in blocks]).astype(BF16)


def body(
    layer_input,
    output_cotangent,
    documents,
    expert_routes,
    attention_gain,
    query_weight,
    key_weight,
    value_weight,
    output_weight,
    router_weight,
    mixture_gain,
    expert_gate,
    expert_up,
    expert_down,
):
    batches, rows, width = layer_input.shape
    groups = lax.axis_size("expert")
    members = lax.axis_size("dp")
    local = expert_gate.shape[1]
    experts_all = local * groups
    me = lax.axis_index("expert")
    first = lax.axis_index("section") == 0

    def choose(upper, lower):
        return jax.tree.map(lambda a, b: jnp.where(first, a, b), upper, lower)

    places = (me * rows + jnp.arange(rows, dtype=jnp.int32)).astype(F32)
    inverse = THETA ** (-jnp.arange(HALF, dtype=F32) * 2.0 / HD)
    angles = inverse[:, None] * places[None, :]
    cosine = jnp.cos(angles)
    sine = jnp.sin(angles)
    number = me * local + jnp.arange(local, dtype=jnp.int32)
    lanes = jnp.arange(LANES, dtype=jnp.int32)
    mark = (lanes[None, :] == number[:, None]).astype(F32)[:, None, :]
    pick = mark + (lanes[None, :] == number[:, None] + LOW).astype(F32)[:, None, :]

    def bias_of(batch):
        labels = documents[batch]
        own = lax.dynamic_slice_in_dim(labels, me * rows, rows)
        pieces = []
        for distance in range(groups):
            source = me ^ distance
            theirs = lax.dynamic_slice_in_dim(labels, source * rows, rows)
            order = source * rows + jnp.arange(rows, dtype=jnp.int32)
            allowed = (theirs[:, None] == own[None, :]) & (
                order[:, None] <= (me * rows + jnp.arange(rows, dtype=jnp.int32))[None, :]
            )
            pieces.append(jnp.where(allowed, 0.0, -BIG))
        return jnp.concatenate(pieces, axis=0)

    def chosen_of(batch):
        named = (expert_routes[0, batch][:, :, None] == lanes[None, None, :]).any(axis=1)
        return jnp.where(named, 0.0, -BIG)

    biases = [bias_of(batch) for batch in range(batches)]
    chosens = [chosen_of(batch) for batch in range(batches)]

    inner, out, router = gather_weights(
        0,
        query_weight[0],
        key_weight[0],
        value_weight[0],
        output_weight[0],
        pad_lanes(router_weight[0]),
    )
    gain_one = attention_gain
    gain_two = mixture_gain
    gate_all, up_all, down_all = (expert_gate[0], expert_up[0], expert_down[0])
    weights = (inner, out, gate_all, up_all, down_all)

    def active(moment):
        return [s for s in range(2) if 0 <= moment - s < batches]

    stored = []
    produced = []
    inbound = jnp.zeros((rows, width), BF16)
    arrays = {
        "p0": [None, shape((1, members, groups, rows, width + LANES), BF16)],
        "p1": [None, shape((1, members, groups, rows, width + LANES), BF16)],
        "g0": [None, shape((1, members, groups, rows, width), BF16)],
        "g1": [None, shape((1, members, groups, rows, width), BF16)],
    }

    def keep_arrays(made):
        for name, array in made.items():
            arrays[name][0] = array

    plans = {
        ("forward", 0): [(0, ("keep",), "p0", 0, True)],
        ("forward", 1): [
            (0, ("line",), "p0", 0, True),
            (0, ("keep",), "p1", 0, True),
            (1, ("keep",), "p0", 0, True),
        ],
        ("forward", 2): [
            (1, ("line",), "p0", 0, False),
            (0, ("line", "plane"), "p1", 0, True),
            (0, ("plane",), "p0", 0, True),
            (1, ("keep",), "p1", 0, True),
        ],
        ("backward", 0): [
            (1, ("keep", "line"), "g0", 0, True),
            (1, ("line",), "p1", 0, True),
            (1, ("plane",), "p0", 0, False),
        ],
        ("backward", 1): [
            (0, ("keep", "line"), "g0", 0, True),
            (1, ("keep", "line"), "g1", 0, True),
            (1, ("plane",), "g0", 0, True),
        ],
        ("backward", 2): [
            (0, ("keep", "line"), "g1", 0, False),
            (0, ("plane",), "g0", 0, True),
        ],
        ("weights", 0): [
            (0, ("plane",), "g1", 0, False),
            (1, ("plane",), "g1", 0, True),
            (1, ("plane",), "p1", 0, True),
        ],
    }

    for moment in range(batches + 1):
        sections = active(moment)
        early = min(moment, batches - 1)
        late = max(moment - 1, 0)
        if sections == [0]:
            entry, bias, chosen = layer_input[early], biases[early], chosens[early]
        elif sections == [1]:
            entry, bias, chosen = inbound, biases[late], chosens[late]
        else:
            entry, bias, chosen = choose(
                (layer_input[early], biases[early], chosens[early]),
                (inbound, biases[late], chosens[late]),
            )
        results, made = forward_layer(
            sections,
            1 + moment,
            entry,
            gain_one,
            cosine,
            sine,
            bias,
            gain_two,
            router,
            chosen,
            pick,
            weights,
            plans["forward", moment],
            arrays,
        )
        keep_arrays(made)
        normed, queries, kv, attended, lse, middle, payloads, output = results
        produced.append(output)
        if moment < batches:
            inbound = from_behind(output, 1)
        stored.append(
            dict(
                held=(entry, bias, queries, kv, lse, middle, payloads),
                normed=normed,
                attended=attended,
                payloads=payloads,
            )
        )

    def attention_terms(section):
        parts = list(
            attention_weights(
            section,
            [
                (
                    stored[batch + section]["normed"],
                    moments[batch + 1 - section][1],
                    stored[batch + section]["attended"],
                    moments[batch + 1 - section][2],
                    stored[batch + section]["payloads"][0],
                    *moments[batch + 1 - section][3:],
                )
                for batch in range(batches)
            ],
            section == 1,
        ))
        small[section] = parts.pop()
        if section == 1:
            return [parts[0]] + [shift(parts[k], "dp", k, [1]) for k in range(1, members)]
        return [parts[0]] + [swap(parts[d], d, [0]) for d in range(1, groups)]

    prepared = None
    terms = [None, None]
    small = [None, None]

    received = None
    moments = []
    for moment in range(batches + 1):
        sections = [s for s in range(2) if 0 <= moment - (1 - s) < batches]
        if received is None:
            grad = output_cotangent[moment]
        else:
            grad = received if moment == batches else choose(received, output_cotangent[moment])
        sets = [
            (s, stored[moment - 1 if s == 0 else moment + 1]["held"]) for s in sections
        ]
        results, made = backward_layer(
            sections,
            2 + batches + moment,
            grad,
            sets,
            gain_one,
            gain_two,
            router,
            cosine,
            sine,
            pick,
            mark,
            weights,
            plans["backward", moment],
            arrays,
        )
        keep_arrays(made)
        entry_grad, sent, turned, branch, logit_grad, gain_one_part, gain_two_part = results
        moments.append((entry_grad, turned, branch, logit_grad, gain_one_part, gain_two_part))
        if moment == 0:
            both = [arrays[name][0].reshape(-1, width + LANES) for name in ("p0", "p1")]
            if sum(block.shape[0] for block in both) <= PREPARED:
                prepared = prepare(both, pick, gate_all, up_all)
        if moment < batches:
            received = from_behind(sent, -1)
            if moment == 0:
                received, prepared = lax.optimization_barrier((received, prepared))

    moments, stored = lax.optimization_barrier((moments, stored))
    terms[1] = attention_terms(1)

    forward = (pick, gate_all, up_all)
    tight = prepared is None
    some = 1

    def halfway(terms):
        pieces = sum_blocks(terms[0], terms[1], width // members)
        arrived = [pieces[0]]
        for k in range(1, max(members, groups)):
            route = []
            for i in range(members):
                for e in range(groups):
                    if k < members:
                        route.append((i * groups + e, (i + k) % members * groups + e))
                    if k < groups:
                        base = (members + i) * groups
                        route.append((base + e, base + (e ^ k)))
            arrived.append(lax.ppermute(pieces[k], ("section", "dp", "expert"), route))
        return arrived

    first_grads = arrays["g0"][0].reshape(-1, width)
    terms[0] = attention_terms(0) if tight else None
    if tight:
        shards = halfway(terms)
        shards, first_grads = lax.optimization_barrier((shards, first_grads))
    partial, made = first_weights(
        3 + 2 * batches,
        plans["weights", 0],
        arrays,
        some,
        arrays["p0"][0].reshape(-1, width + LANES),
        first_grads,
        down_all,
        prepared,
        forward,
    )
    keep_arrays(made)
    if not tight:
        stored, partial = lax.optimization_barrier((stored, partial))
        terms[0] = attention_terms(0)
    tokens = [arrays[name][0].reshape(-1, width + LANES) for name in ("p0", "p1")]
    grads = [arrays[name][0].reshape(-1, width) for name in ("g0", "g1")]
    totals = partial if tight else None
    for expert in range(some, local):
        totals = whole_weights(expert, tokens, grads, down_all, prepared, forward, totals)
    if not tight:
        terms, totals = lax.optimization_barrier((terms, totals))
        shards = halfway(terms)
    if totals is None:
        totals = partial
    for expert in range(some):
        totals = last_weights(
            (expert, expert + 1),
            tokens[-1],
            grads[-1],
            down_all,
            prepared,
            forward,
            totals if tight else partial,
            totals,
        )
        if expert == max(some - 2, 0):
            shards, totals, small = lax.optimization_barrier((shards, totals, small))
            shard = total_of(shards)
            shard, small = lax.optimization_barrier((shard, small))
            small = sum_small(4 + 2 * batches, small[0], small[1])
            shard, small = lax.optimization_barrier((shard, small))
            shards = [shard] + [swap(shard, d, [0, 1]) for d in range(1, groups)]
    shards, totals = lax.optimization_barrier((shards, totals))
    gate_grad, up_grad, down_grad = totals
    query_grad, key_grad, value_grad, out_grad = assemble(
        shards,
        [H * HD, KVH * HD, KVH * HD, width],
    )

    final = [choose(moments[batch + 1], moments[batch]) for batch in range(batches)]
    layer_outputs = jnp.stack(
        [choose(produced[batch], produced[batch + 1]) for batch in range(batches)]
    )
    input_grads = jnp.stack([part[0] for part in final])

    depth = width // members
    router_grad = lax.dynamic_slice_in_dim(
        small[:experts_all], lax.axis_index("dp") * depth, depth, 1
    ).T
    return (
        layer_outputs[None],
        input_grads[None],
        small[SMALL - 2][None],
        query_grad[None],
        key_grad[None],
        value_grad[None],
        out_grad[None],
        router_grad[None],
        small[SMALL - 1][None],
        gate_grad[None],
        up_grad[None],
        down_grad[None],
    )


def solution(mesh):
    placed = (
        P(None, ("dp", "expert"), None),
        P(None, ("dp", "expert"), None),
        P(None, "dp"),
        P("section", None, ("dp", "expert"), None),
        P("section", None),
        P("section", "dp", None),
        P("section", "dp", None),
        P("section", "dp", None),
        P("section", "dp", None),
        P("section", "dp", None),
        P("section", None),
        P("section", "expert", None, None),
        P("section", "expert", None, None),
        P("section", "expert", None, None),
    )
    return jax.shard_map(
        body,
        mesh=mesh,
        in_specs=placed,
        out_specs=(
            P("section", None, ("dp", "expert"), None),
            P("section", None, ("dp", "expert"), None),
            P("section", None),
            P("section", "dp", None),
            P("section", "dp", None),
            P("section", "dp", None),
            P("section", "dp", None),
            P("section", "dp", None),
            P("section", None),
            P("section", "expert", None, None),
            P("section", "expert", None, None),
            P("section", "expert", None, None),
        ),
        check_vma=False,
    )
```
